32 devices in a mesh: dp: 4 (over x, core), seq: 4 (over z), tensor: 2 (over y).
Axes of the slice: x: 2, y: 2, z: 4, core: 2. Of those that a mesh axis runs over, the one named last changes fastest.
Arguments:
- hidden: bfloat16 [8192, 1536], P(('dp', 'seq')), may hold values from -6 to 6
- cotangent: bfloat16 [8192, 1536], P(('dp', 'seq')), may hold values from -6 to 6
- segments: int32 [8192], P('dp'), may hold values from 0 to 2, as said below
- positions: int32 [8192], P('dp'), may hold values from 0 to 2047, as said below
- first_gain: bfloat16 [1536], replicated, may hold values from 0.5 to 1.5
- query_weight: bfloat16 [1536, 1536], P(('dp', 'seq'), 'tensor'), may hold values from -0.21875 to 0.21875
- query_bias: bfloat16 [1536], P('tensor'), may hold values from -3 to 3
- key_weight: bfloat16 [1536, 256], P(('dp', 'seq'), 'tensor'), may hold values from -0.15625 to 0.15625
- key_bias: bfloat16 [256], P('tensor'), may hold values from -3 to 3
- value_weight: bfloat16 [1536, 256], P(('dp', 'seq'), 'tensor'), may hold values from -0.15625 to 0.15625
- value_bias: bfloat16 [256], P('tensor'), may hold values from -3 to 3
- out_weight: bfloat16 [1536, 1536], P('tensor', ('dp', 'seq')), may hold values from -1.25 to 1.25
- second_gain: bfloat16 [1536], replicated, may hold values from 0.5 to 1.5
- gate_weight: bfloat16 [1536, 8960], P(('dp', 'seq'), 'tensor'), may hold values from -0.15625 to 0.15625
- up_weight: bfloat16 [1536, 8960], P(('dp', 'seq'), 'tensor'), may hold values from -0.15625 to 0.15625
- down_weight: bfloat16 [8960, 1536], P('tensor', ('dp', 'seq')), may hold values from -0.125 to 0.125
Outputs:
- output: bfloat16 [8192, 1536], P(('dp', 'seq'))
- input_gradient: bfloat16 [8192, 1536], P(('dp', 'seq'))
- first_gain_gradient: float32 [1536], replicated
- query_weight_gradient: float32 [1536, 1536], P(('dp', 'seq'), 'tensor')
- query_bias_gradient: float32 [1536], P('tensor')
- key_weight_gradient: float32 [1536, 256], P(('dp', 'seq'), 'tensor')
- key_bias_gradient: float32 [256], P('tensor')
- value_weight_gradient: float32 [1536, 256], P(('dp', 'seq'), 'tensor')
- value_bias_gradient: float32 [256], P('tensor')
- out_weight_gradient: float32 [1536, 1536], P('tensor', ('dp', 'seq'))
- second_gain_gradient: float32 [1536], replicated
- gate_weight_gradient: float32 [1536, 8960], P(('dp', 'seq'), 'tensor')
- up_weight_gradient: float32 [1536, 8960], P(('dp', 'seq'), 'tensor')
- down_weight_gradient: float32 [8960, 1536], P('tensor', ('dp', 'seq'))
The draws below stay inside these ranges and needn't reach their ends.
Inputs may be any that keep to these rules, and one draw needn't show every extreme that they name: `segments`: in each group of 2048 tokens (one index of dp), every aligned block of 512 tokens holds one member: the prompt (segment 0) fills 2 blocks, its blocks in order; each continuation 1 to 2 fills one block. `positions`: prompt tokens hold 0 to 1023 in order; a continuation's tokens hold a start to that start + 511 in order, with the start between 1024 and 1536.
All inputs are finite; a program needn't handle non-finite values.
Results may differ from the reference program's by a relative error of at most 0.018.
Values may be sent and summed in bfloat16 or wider, within the bound.
No kernel may reach another device: no remote copies, remote signals or barrier semaphores. Data moves between devices by JAX's collectives and lax.ppermute only.
A program may use at most 256 MiB of HBM per device.

```python
import math
import jax
import jax.numpy as jnp
from jax import lax

D = 1536
HEADS = 12
KV_HEADS = 2
HEAD_DIM = 128
FF = 8960
TOK_DEV = 512
GROUP_TOKENS = 2048
TOKENS = 8192
PROMPT_LEN = 1024
N_DP = 4
N_SEQ = 4


def group_layout(key):

    def one_group(group_key):
        first_key, second_key, third_key = jax.random.split(group_key, 3)
        picked = jax.random.permutation(first_key, N_SEQ)[:N_SEQ // 2]
        flags = jnp.zeros((N_SEQ,), jnp.int32).at[picked].set(1)
        span_rank = (jnp.cumsum(flags) - 1).astype(jnp.int32)
        follow_rank = jnp.maximum(jnp.cumsum(1 - flags) - 1, 0).astype(jnp.int32)
        order = jax.random.permutation(second_key, N_SEQ // 2).astype(jnp.int32)
        block_segment = jnp.where(flags == 1, 0, order[follow_rank] + 1).astype(jnp.int32)
        gaps = jax.random.randint(third_key, (N_SEQ // 2 + 1,), 0, TOK_DEV + 1).astype(jnp.int32)
        block_gap = gaps[block_segment]
        block_gap = jnp.where((follow_rank == 0) & (flags == 0), TOK_DEV, block_gap).astype(jnp.int32)
        offsets = jnp.arange(TOK_DEV, dtype=jnp.int32)
        block_start = jnp.where(flags == 1, span_rank * TOK_DEV, PROMPT_LEN + block_gap).astype(jnp.int32)
        segment_row = jnp.repeat(block_segment, TOK_DEV)
        place_row = (block_start[:, None] + offsets[None, :]).reshape(-1)
        return (segment_row, place_row)
    segment_all, place_all = jax.vmap(one_group)(jax.random.split(key, N_DP))
    return (segment_all.reshape(-1).astype(jnp.int32), place_all.reshape(-1).astype(jnp.int32))


def draw_segments(key, part):
    layout = group_layout(key)
    return layout[0]


def draw_positions(key, part):
    layout = group_layout(key)
    return layout[1]


def raised(drawn, own_key, source, target, blocks, factor):
    owner, partner = [(jnp.arange(drawn.shape[axis_at]) // (drawn.shape[axis_at] // blocks)).reshape([-1 if axis == axis_at else 1 for axis in range(drawn.ndim)]) for axis_at in (source, target)]
    chosen = jax.random.permutation(own_key, blocks)[partner]
    strong = (owner == chosen) | (owner == (partner + blocks // 2) % blocks)
    return jnp.where(strong, factor * drawn, drawn)


def levels(key, shape, shards, smallest, high):
    def one(axis_at, shards_of):
        heights = jax.random.uniform(jax.random.fold_in(jax.random.fold_in(key, 6), axis_at), (shards_of,), jnp.float32, smallest / len(shards), high / len(shards))
        return jnp.repeat(jnp.exp(heights), shape[axis_at] // shards_of).reshape((-1,) + (1,) * (len(shape) - axis_at - 1))

    factor_of = one(*shards[0])
    for cut in shards[1:]:
        factor_of = factor_of * one(*cut)
    return factor_of


def noise(stream_key, shape, scale, bound, cuts=(), kind=jnp.bfloat16):
    values = scale * jax.random.normal(stream_key, shape, jnp.float32)
    if cuts:
        values = values * levels(stream_key, shape, cuts, -0.22, 0.18)
    return jnp.clip(values, -bound, bound).astype(kind)


def bell_draw_with(stream_key, dims, scale, most, cuts, heavy, kind=jnp.bfloat16):
    array = scale * jax.random.normal(stream_key, dims, jnp.float32)
    if cuts:
        array = array * levels(stream_key, dims, cuts, -0.22, 0.18)
    return jnp.clip(raised(array, jax.random.fold_in(stream_key, 3), *heavy), -most, most).astype(kind)


def setup_inputs(seed: int = 0) -> dict:
    seeds = jax.random.split(jax.random.key(seed), 17)
    return {
        "hidden": bell_draw_with(seeds[0], (TOKENS, D), 1.0, 6.0, ((0, 16),), (0, 1, 16, 2.0)),
        "cotangent": bell_draw_with(seeds[1], (TOKENS, D), 1.0, 6.0, ((0, 16),), (0, 1, 16, 2.0)),
        "segments": draw_segments(jax.random.fold_in(seeds[16], 71), 0),
        "positions": draw_positions(jax.random.fold_in(seeds[16], 71), 0),
        "first_gain": jnp.clip(1.0 + 0.1 * jax.random.normal(seeds[4], (D,), jnp.float32), 0.5, 1.5).astype(jnp.bfloat16),
        "query_weight": noise(seeds[5], (D, HEADS * HEAD_DIM), (D // 2) ** -0.5, 0.21875, ((0, 16), (1, 2))),
        "query_bias": noise(seeds[6], (HEADS * HEAD_DIM,), 0.5, 3.0, ((0, 2),)),
        "key_weight": noise(seeds[7], (D, KV_HEADS * HEAD_DIM), D ** -0.5, 0.15625, ((0, 16), (1, 2))),
        "key_bias": noise(seeds[8], (KV_HEADS * HEAD_DIM,), 0.5, 3.0, ((0, 2),)),
        "value_weight": noise(seeds[9], (D, KV_HEADS * HEAD_DIM), D ** -0.5, 0.15625, ((0, 16), (1, 2))),
        "value_bias": noise(seeds[10], (KV_HEADS * HEAD_DIM,), 0.5, 3.0, ((0, 2),)),
        "out_weight": noise(seeds[11], (HEADS * HEAD_DIM, D), (max(HEADS * HEAD_DIM // 64, 1)) ** -0.5, 1.25, ((0, 2), (1, 16))),
        "second_gain": jnp.clip(1.0 + 0.1 * jax.random.normal(seeds[12], (D,), jnp.float32), 0.5, 1.5).astype(jnp.bfloat16),
        "gate_weight": noise(seeds[13], (D, FF), D ** -0.5, 0.15625, ((0, 16), (1, 2))),
        "up_weight": noise(seeds[14], (D, FF), D ** -0.5, 0.15625, ((0, 16), (1, 2))),
        "down_weight": noise(seeds[15], (FF, D), (FF // 4) ** -0.5, 0.125, ((0, 2), (1, 16))),
    }


EPS = 1e-06
LOG_BASE = math.log(1000000.0)

@jax.custom_vjp
def low(v):
    return lax.optimization_barrier(v.astype(jnp.bfloat16)).astype(jnp.float32)

@jax.custom_vjp
def low_back(v):
    return v

def low_keep(v):
    return (low(v), None)

def low_pass(kept, grad):
    return (grad,)

def back_keep(v):
    return (v, None)

def back_low(kept, grad):
    return (low(grad),)
low.defvjp(low_keep, low_pass)
low_back.defvjp(back_keep, back_low)

def highest(left, right):
    return jnp.dot(left, right, precision=lax.Precision.HIGHEST)

def rms_scale(values, gain):
    return values * lax.rsqrt(lax.optimization_barrier(jnp.mean(values * values, axis=-1, keepdims=True)) + EPS) * gain

def rope_tables(places, width):
    half = width // 2
    freq = jnp.exp(jnp.arange(half, dtype=jnp.float32) * (-2.0 * LOG_BASE / width))
    angle = places.astype(jnp.float32)[:, None] * freq[None, :]
    return (jnp.cos(angle), jnp.sin(angle))

def rotate(values, cosine, sine):
    half = values.shape[-1] // 2
    first = values[..., :half]
    second = values[..., half:]
    cosine = cosine[:, None, :]
    sine = sine[:, None, :]
    return jnp.concatenate([first * cosine - second * sine, second * cosine + first * sine], axis=-1)

def visible(segment_rows, place_rows, segment_keys, place_keys):
    same = (segment_keys[None, :] == 0) | (segment_keys[None, :] == segment_rows[:, None])
    return same & (place_keys[None, :] <= place_rows[:, None])

def reference(hidden, cotangent, segments, positions, first_gain, query_weight, query_bias, key_weight, key_bias, value_weight, value_bias, out_weight, second_gain, gate_weight, up_weight, down_weight):
    cosine, sine = rope_tables(positions, HEAD_DIM)
    blocks = TOKENS // TOK_DEV
    repeat = HEADS // KV_HEADS
    scale = HEAD_DIM ** (-0.5)
    segment_rows = segments.reshape(blocks, TOK_DEV)
    place_rows = positions.reshape(blocks, TOK_DEV)
    segment_groups = segments.reshape(N_DP, GROUP_TOKENS)
    place_groups = positions.reshape(N_DP, GROUP_TOKENS)
    block_index = jnp.arange(blocks, dtype=jnp.int32)

    def forward(inputs, gain_one, weight_query, bias_query, weight_key, bias_key, weight_value, bias_value, weight_out, gain_two, weight_gate, weight_up, weight_down):
        first = low(rms_scale(inputs, gain_one))
        query_linear = low_back(highest(first, weight_query) + bias_query)
        key_linear = low_back(highest(first, weight_key) + bias_key)
        values = low(low_back(highest(first, weight_value) + bias_value))
        queries = low(rotate(query_linear.reshape(TOKENS, HEADS, HEAD_DIM), cosine, sine))
        keys = low(rotate(key_linear.reshape(TOKENS, KV_HEADS, HEAD_DIM), cosine, sine))
        group_keys = keys.reshape(N_DP, GROUP_TOKENS, KV_HEADS, HEAD_DIM)
        group_values = values.reshape(N_DP, GROUP_TOKENS, KV_HEADS, HEAD_DIM)
        query_blocks = queries.reshape(blocks, TOK_DEV, KV_HEADS, repeat, HEAD_DIM)

        def attend(block):
            query_block, segment_block, place_block, index = block
            which = index // N_SEQ
            key_group = lax.dynamic_index_in_dim(group_keys, which, 0, keepdims=False)
            value_group = lax.dynamic_index_in_dim(group_values, which, 0, keepdims=False)
            segment_keys = lax.dynamic_index_in_dim(segment_groups, which, 0, keepdims=False)
            place_keys = lax.dynamic_index_in_dim(place_groups, which, 0, keepdims=False)
            scores = jnp.einsum('tgrd,kgd->grtk', query_block, key_group, precision=lax.Precision.HIGHEST) * scale
            scores = low_back(scores)
            mask = visible(segment_block, place_block, segment_keys, place_keys)
            weights = jax.nn.softmax(jnp.where(mask, scores, -jnp.inf), axis=-1)
            return jnp.einsum('grtk,kgd->tgrd', low(weights), value_group, precision=lax.Precision.HIGHEST)
        attended = lax.map(jax.checkpoint(attend), (query_blocks, segment_rows, place_rows, block_index))
        attended = low(low_back(attended.reshape(TOKENS, HEADS * HEAD_DIM)))
        residual = inputs + low_back(highest(attended, weight_out))
        second = low(rms_scale(residual, gain_two))
        gate = low_back(highest(second, weight_gate))
        upper = low_back(highest(second, weight_up))
        activated = low(jax.nn.silu(gate) * upper)
        return residual + low_back(highest(activated, weight_down))
    primal = (hidden.astype(jnp.float32), first_gain.astype(jnp.float32), query_weight.astype(jnp.float32), query_bias.astype(jnp.float32), key_weight.astype(jnp.float32), key_bias.astype(jnp.float32), value_weight.astype(jnp.float32), value_bias.astype(jnp.float32), out_weight.astype(jnp.float32), second_gain.astype(jnp.float32), gate_weight.astype(jnp.float32), up_weight.astype(jnp.float32), down_weight.astype(jnp.float32))
    result, pullback = jax.vjp(forward, *primal)
    grads = pullback(cotangent.astype(jnp.float32))
    return (result.astype(jnp.bfloat16), grads[0].astype(jnp.bfloat16), grads[1], grads[2], grads[3], grads[4], grads[5], grads[6], grads[7], grads[8], grads[9], grads[10], grads[11], grads[12])
```

```python
import functools
import math

import jax
import jax.numpy as jnp
from jax import lax
from jax.experimental import pallas as pl
from jax.experimental.pallas import tpu as pltpu
from jax.sharding import PartitionSpec as P

HEAD_DIM = 128
EPS = 1e-06
LOG_BASE = math.log(1000000.0)
NEG_FILL = -1e30
LOG2E = 1.0 / math.log(2.0)
MIB = 1024 * 1024
F32 = jnp.float32
BF16 = jnp.bfloat16
FREE = pl.CostEstimate(flops=0, bytes_accessed=0, transcendentals=0)


def product(left, right):
    return jnp.dot(left, right, preferred_element_type=F32)


def left_product(left, right):
    return lax.dot_general(left, right, (((0,), (0,)), ((), ())), preferred_element_type=F32)


def right_product(left, right):
    return lax.dot_general(left, right, (((1,), (1,)), ((), ())), preferred_element_type=F32)


def after(value, *others):
    return lax.optimization_barrier((value,) + others)[0]


def together(*values):
    return lax.optimization_barrier(values)


def dp_swap(value, flip):
    size = lax.axis_size("dp")
    return lax.ppermute(value, "dp", [(i, i ^ flip) for i in range(size)])


def y_swap(value):
    return lax.ppermute(value, "tensor", [(0, 1), (1, 0)])


def z_shift(value, step):
    size = lax.axis_size("seq")
    return lax.ppermute(value, "seq", [(i, (i + step) % size) for i in range(size)])


def assemble_kernel(count, place_ref, *refs):
    pieces, out_ref, sems = refs[:count], refs[count], refs[count + 1]
    copies = [
        pltpu.make_async_copy(piece, out_ref.at[place_ref[i]], sems.at[i])
        for i, piece in enumerate(pieces)
    ]
    for copy in copies:
        copy.start()
    for copy in copies:
        copy.wait()


def assemble(pieces, places):
    count = len(pieces)
    return pl.pallas_call(
        functools.partial(assemble_kernel, count),
        out_shape=jax.ShapeDtypeStruct((count,) + pieces[0].shape, pieces[0].dtype),
        in_specs=[pl.BlockSpec(memory_space=pltpu.SMEM)]
        + [pl.BlockSpec(memory_space=pl.ANY)] * count,
        out_specs=pl.BlockSpec(memory_space=pltpu.VMEM),
        scratch_shapes=[pltpu.SemaphoreType.DMA((count,))],
        compiler_params=pltpu.CompilerParams(vmem_limit_bytes=24 * MIB),
        cost_estimate=FREE,
    )(places, *pieces)


def pair_mask(seg_q, pos_q, seg_k, pos_k):
    return ((seg_k == 0) | (seg_k == seg_q)) & (pos_k <= pos_q)


def attend_kernel(
    rows, factor, flag_ref, q_ref, k_ref, v_ref, sq_ref, pq_ref, sk_ref, pk_ref,
    o_ref, lse_ref, top_ref, sum_ref, acc_ref,
):
    blocks = k_ref.shape[0] // rows
    top_ref[...] = jnp.full_like(top_ref, NEG_FILL)
    sum_ref[...] = jnp.zeros_like(sum_ref)
    acc_ref[...] = jnp.zeros_like(acc_ref)
    q = q_ref[...]

    def block_step(j, masked):
        span = pl.ds(pl.multiple_of(j * rows, rows), rows)
        s = right_product(q, k_ref[span, :]) * factor
        if masked:
            mask = pair_mask(sq_ref[...], pq_ref[...], sk_ref[j], pk_ref[j])
            s = jnp.where(mask, s, NEG_FILL)
        top = top_ref[...]
        new_top = jnp.maximum(top, jnp.max(s, axis=1, keepdims=True))
        e = jnp.exp2(s - new_top)
        if masked:
            e = jnp.where(mask, e, 0.0)
        shrink = jnp.exp2(top - new_top)
        top_ref[...] = new_top
        sum_ref[...] = sum_ref[...] * shrink + jnp.sum(e, axis=1, keepdims=True)
        acc_ref[...] = acc_ref[...] * shrink + product(e.astype(BF16), v_ref[span, :])

    def step(j, carry):
        @pl.when(flag_ref[j] == 2)
        def _():
            block_step(j, False)

        @pl.when(flag_ref[j] == 1)
        def _():
            block_step(j, True)

        return carry

    lax.fori_loop(0, blocks, step, 0)
    total = sum_ref[...]
    o_ref[...] = (acc_ref[...] / total).astype(o_ref.dtype)
    lse_ref[...] = (top_ref[...] + jnp.log2(total))[None]


def attend(q, keys, values, seg_q, pos_q, seg_k, pos_k, flags):
    rows, width = q.shape
    heads = width // HEAD_DIM
    kv_heads = keys.shape[1] // HEAD_DIM
    repeat = heads // kv_heads
    length = keys.shape[0]
    blocks = length // rows
    whole = lambda *shape: pl.BlockSpec(shape, lambda h: (0,) * len(shape))
    return pl.pallas_call(
        functools.partial(attend_kernel, rows, HEAD_DIM ** (-0.5) * LOG2E),
        grid=(heads,),
        in_specs=[
            pl.BlockSpec(memory_space=pltpu.SMEM),
            pl.BlockSpec((rows, HEAD_DIM), lambda h: (0, h)),
            pl.BlockSpec((length, HEAD_DIM), lambda h: (0, h // repeat)),
            pl.BlockSpec((length, HEAD_DIM), lambda h: (0, h // repeat)),
            whole(rows, 1),
            whole(rows, 1),
            whole(blocks, 1, rows),
            whole(blocks, 1, rows),
        ],
        out_specs=[
            pl.BlockSpec((rows, HEAD_DIM), lambda h: (0, h)),
            pl.BlockSpec((1, rows, 1), lambda h: (h, 0, 0)),
        ],
        out_shape=[
            jax.ShapeDtypeStruct((rows, width), BF16),
            jax.ShapeDtypeStruct((heads, rows, 1), F32),
        ],
        scratch_shapes=[
            pltpu.VMEM((rows, 1), F32),
            pltpu.VMEM((rows, 1), F32),
            pltpu.VMEM((rows, HEAD_DIM), F32),
        ],
        compiler_params=pltpu.CompilerParams(vmem_limit_bytes=40 * MIB),
        cost_estimate=FREE,
    )(flags, q, keys, values, seg_q, pos_q, seg_k, pos_k)


def attend_back_kernel(
    rows, factor, scale, repeat, flag_ref, q_ref, k_ref, v_ref, do_ref, lse_ref, cos_ref, sin_ref,
    sq_ref, pq_ref, sk_ref, pk_ref, dq_ref, dk_ref, dv_ref, dk_acc, dv_acc, dq_acc,
    p_keep, dp_keep, delta_ref,
):
    head = pl.program_id(0)
    blocks = k_ref.shape[0] // rows

    @pl.when(lax.rem(head, repeat) == 0)
    def _():
        dk_acc[...] = jnp.zeros_like(dk_acc)
        dv_acc[...] = jnp.zeros_like(dv_acc)

    dq_acc[...] = jnp.zeros_like(dq_acc)
    delta_ref[...] = jnp.zeros_like(delta_ref)
    q = q_ref[...]
    d_o = do_ref[...]
    lse = lse_ref[0]

    def span_of(j):
        return pl.ds(pl.multiple_of(j * rows, rows), rows)

    def first_pass(j, masked):
        p = jnp.exp2(right_product(q, k_ref[span_of(j), :]) * factor - lse)
        if masked:
            mask = pair_mask(sq_ref[...], pq_ref[...], sk_ref[j], pk_ref[j])
            p = jnp.where(mask, p, 0.0)
        dp = right_product(d_o, v_ref[span_of(j), :])
        p_keep[j] = p
        dp_keep[j] = dp
        delta_ref[...] += jnp.sum(p * dp, axis=1, keepdims=True)

    def first_step(j, carry):
        @pl.when(flag_ref[j] == 2)
        def _():
            first_pass(j, False)

        @pl.when(flag_ref[j] == 1)
        def _():
            first_pass(j, True)

        return carry

    lax.fori_loop(0, blocks, first_step, 0)

    def second_step(j, carry):
        @pl.when(flag_ref[j] > 0)
        def _():
            p = p_keep[j]
            ds = (p * (dp_keep[j] - delta_ref[...])).astype(BF16)
            span = span_of(j)
            dv_acc[span, :] += left_product(p.astype(BF16), d_o)
            dk_acc[span, :] += left_product(ds, q)
            dq_acc[...] += product(ds, k_ref[span, :])

        return carry

    lax.fori_loop(0, blocks, second_step, 0)
    (turned,) = rope_lanes(dq_acc[...] * scale, cos_ref[...], -sin_ref[...])
    dq_ref[...] = turned.astype(dq_ref.dtype)

    @pl.when(lax.rem(head, repeat) == repeat - 1)
    def _():
        dk_ref[...] = (dk_acc[...] * scale).astype(dk_ref.dtype)
        dv_ref[...] = dv_acc[...].astype(dv_ref.dtype)


def attend_back(q, keys, values, d_o, lse, cosine, sine, seg_q, pos_q, seg_k, pos_k, flags):
    rows, width = q.shape
    heads = width // HEAD_DIM
    kv_heads = keys.shape[1] // HEAD_DIM
    repeat = heads // kv_heads
    length = keys.shape[0]
    blocks = length // rows
    whole = lambda *shape: pl.BlockSpec(shape, lambda h: (0,) * len(shape))
    per_head = pl.BlockSpec((rows, HEAD_DIM), lambda h: (0, h))
    per_pair = pl.BlockSpec((length, HEAD_DIM), lambda h: (0, h // repeat))
    held = pl.BlockSpec(
        (length, HEAD_DIM), lambda h: (0, h // repeat), pipeline_mode=pl.Buffered(1)
    )
    return pl.pallas_call(
        functools.partial(
            attend_back_kernel, rows, HEAD_DIM ** (-0.5) * LOG2E, HEAD_DIM ** (-0.5), repeat
        ),
        grid=(heads,),
        in_specs=[
            pl.BlockSpec(memory_space=pltpu.SMEM),
            per_head,
            held,
            held,
            per_head,
            pl.BlockSpec((1, rows, 1), lambda h: (h, 0, 0)),
            whole(rows, HEAD_DIM),
            whole(rows, HEAD_DIM),
            whole(rows, 1),
            whole(rows, 1),
            whole(blocks, 1, rows),
            whole(blocks, 1, rows),
        ],
        out_specs=[per_head, per_pair, per_pair],
        out_shape=[
            jax.ShapeDtypeStruct((rows, width), BF16),
            jax.ShapeDtypeStruct(keys.shape, BF16),
            jax.ShapeDtypeStruct(values.shape, BF16),
        ],
        scratch_shapes=[
            pltpu.VMEM((length, HEAD_DIM), F32),
            pltpu.VMEM((length, HEAD_DIM), F32),
            pltpu.VMEM((rows, HEAD_DIM), F32),
            pltpu.VMEM((blocks, rows, rows), F32),
            pltpu.VMEM((blocks, rows, rows), F32),
            pltpu.VMEM((rows, 1), F32),
        ],
        compiler_params=pltpu.CompilerParams(vmem_limit_bytes=58 * MIB),
        cost_estimate=FREE,
    )(flags, q, keys, values, d_o, lse, cosine, sine, seg_q, pos_q, seg_k, pos_k)


def rope_tables(places, width):
    half = width // 2
    freq = jnp.exp(jnp.arange(half, dtype=F32) * (-2.0 * LOG_BASE / width))
    angle = places.astype(F32)[:, None] * freq[None, :]
    return (jnp.cos(angle), jnp.sin(angle))


def rotate(values, cosine, sine):
    half = HEAD_DIM // 2
    parts = []
    for at in range(0, values.shape[1], HEAD_DIM):
        first = values[:, at : at + half]
        second = values[:, at + half : at + HEAD_DIM]
        parts += [first * cosine - second * sine, second * cosine + first * sine]
    return jnp.concatenate(parts, axis=1)


def inverse_rms(values):
    return lax.rsqrt(jnp.mean(values * values, axis=-1, keepdims=True) + EPS)


def norm_backward(upstream, normed, inverse, gain):
    scaled = upstream * gain
    inner = inverse * (scaled - normed * jnp.mean(scaled * normed, axis=-1, keepdims=True))
    return (inner, jnp.sum(upstream * normed, axis=0))


def rope_lanes(values, cosine, sine):
    parts = []
    for at in range(0, values.shape[1], HEAD_DIM):
        head = values[:, at : at + HEAD_DIM]
        parts.append(head * cosine + pltpu.roll(head, HEAD_DIM // 2, 1) * sine)
    return parts


def project_kernel(
    count, q_width, kv_width, place_ref, mine_ref, theirs_ref,
    x_ref, gain_ref, bias_ref, cos_ref, sin_ref, q_ref, kv_ref, h_ref, w_ref, sems,
):
    copies = [
        pltpu.make_async_copy(stack.at[i], w_ref.at[place_ref[at + i]], sems.at[at + i])
        for at, stack in ((0, mine_ref), (count, theirs_ref))
        for i in range(count)
    ]
    for copy in copies:
        copy.start()
    x = x_ref[...].astype(F32)
    normed = x * lax.rsqrt(jnp.mean(x * x, axis=1, keepdims=True) + EPS)
    h = (normed * gain_ref[...]).astype(BF16)
    h_ref[...] = h
    for copy in copies:
        copy.wait()
    depth, columns = x.shape[1], bias_ref.shape[1]
    weights = w_ref[...].reshape(depth, w_ref.shape[2])
    linear = product(h, weights[:, :columns]) + bias_ref[...]
    turned = rope_lanes(linear[:, : q_width + kv_width], cos_ref[...], sin_ref[...])
    heads = q_width // HEAD_DIM
    for i, part in enumerate(turned):
        if i < heads:
            q_ref[:, i * HEAD_DIM : (i + 1) * HEAD_DIM] = part.astype(BF16)
        else:
            at = (i - heads) * HEAD_DIM
            kv_ref[:, at : at + HEAD_DIM] = part.astype(BF16)
    kv_ref[:, kv_width:] = linear[:, q_width + kv_width :].astype(BF16)


def project(mine, theirs, places, inputs, gain, bias, cosine, sine, q_width, kv_width):
    count = mine.shape[0]
    rows, depth = inputs.shape
    columns = bias.shape[0]
    vmem = pl.BlockSpec(memory_space=pltpu.VMEM)
    return pl.pallas_call(
        functools.partial(project_kernel, count, q_width, kv_width),
        out_shape=[
            jax.ShapeDtypeStruct((rows, q_width), BF16),
            jax.ShapeDtypeStruct((rows, 2 * kv_width), BF16),
            jax.ShapeDtypeStruct((rows, depth), BF16),
            jax.ShapeDtypeStruct((2 * count,) + mine.shape[1:], BF16),
        ],
        in_specs=[pl.BlockSpec(memory_space=pltpu.SMEM)]
        + [pl.BlockSpec(memory_space=pl.ANY)] * 2
        + [vmem] * 5,
        out_specs=[vmem] * 4,
        scratch_shapes=[pltpu.SemaphoreType.DMA((2 * count,))],
        compiler_params=pltpu.CompilerParams(vmem_limit_bytes=40 * MIB),
        cost_estimate=FREE,
    )(places, mine, theirs, inputs, gain[None, :], bias[None, :], cosine, sine)


class Cut:
    def __init__(self, total, n_dp):
        tiles = total // n_dp // 128
        first = max(tiles * 3 // 8, 1)
        self.total = total
        self.n_dp = n_dp
        self.main = (first * 128, (tiles - first) * 128)
        self.start = (0, n_dp * self.main[0])
        self.rest_at = n_dp * (self.main[0] + self.main[1])
        self.rest = (total - self.rest_at) // n_dp
        pad = -(-self.rest // 128) * 128
        self.width = (self.main[0], self.main[1] + pad)


def pick(values, index):
    result = values[0]
    for i in range(1, len(values)):
        result = jnp.where(index == i, values[i], result)
    return result


def cut_kernel(cut, place_ref, *refs):
    weights, outs = refs[:3], refs[3:]
    n_dp = cut.n_dp
    for part in range(2):
        main, width = cut.main[part], cut.width[part]
        for k in range(n_dp):
            owner = place_ref[k]
            out = outs[part * n_dp + k]
            for i, w in enumerate(weights):
                at = i * width
                low = pl.multiple_of(cut.start[part] + owner * main, 128)
                out[:, at : at + main] = w[:, pl.ds(low, main)]
                if part == 1 and cut.rest:
                    tail = w[:, cut.rest_at :]
                    rest = pick(
                        [tail[:, b * cut.rest : (b + 1) * cut.rest] for b in range(n_dp)], owner
                    )
                    fill = jnp.zeros((rest.shape[0], width - main - cut.rest), rest.dtype)
                    out[:, at + main : at + width] = jnp.concatenate([rest, fill], axis=1)


def cut_units(cut, weights, owners):
    rows = weights[0].shape[0]
    vmem = pl.BlockSpec(memory_space=pltpu.VMEM)
    outs = pl.pallas_call(
        functools.partial(cut_kernel, cut),
        out_shape=[
            jax.ShapeDtypeStruct((rows, 3 * cut.width[part]), BF16)
            for part in range(2)
            for _ in range(cut.n_dp)
        ],
        in_specs=[pl.BlockSpec(memory_space=pltpu.SMEM)] + [vmem] * 3,
        out_specs=[vmem] * (2 * cut.n_dp),
        compiler_params=pltpu.CompilerParams(vmem_limit_bytes=24 * MIB),
        cost_estimate=FREE,
    )(owners, *weights)
    return outs[: cut.n_dp], outs[cut.n_dp :]


def lay_kernel(cut, place_ref, *refs):
    n_dp = cut.n_dp
    firsts, pairs, downs = (refs[i * n_dp : (i + 1) * n_dp] for i in range(3))
    outs = refs[3 * n_dp :]
    for i, out in enumerate(outs):
        for part in range(2):
            main, width = cut.main[part], cut.width[part]
            for k in range(n_dp):
                if part == 0:
                    piece = firsts[k].at[:, i * width : (i + 1) * width]
                elif i < 2:
                    piece = pairs[k].at[:, i * width : (i + 1) * width]
                else:
                    piece = downs[k]
                owner = place_ref[k]
                low = pl.multiple_of(cut.start[part] + owner * main, 128)
                out[:, pl.ds(low, main)] = piece[:, :main].astype(F32)
        if cut.rest:
            main, width = cut.main[1], cut.width[1]
            tails = []
            for k in range(n_dp):
                piece = pairs[k].at[:, i * width : (i + 1) * width] if i < 2 else downs[k]
                tails.append(piece[:, main:].astype(F32)[:, : cut.rest])
            laid = []
            for b in range(n_dp):
                laid.append(
                    functools.reduce(
                        lambda got, k: jnp.where(place_ref[k] == b, tails[k], got),
                        range(1, n_dp),
                        tails[0],
                    )
                )
            out[:, cut.rest_at :] = jnp.concatenate(laid, axis=1)


def lay_units(cut, pieces, owners):
    rows = pieces[0].shape[0]
    vmem = pl.BlockSpec(memory_space=pltpu.VMEM)
    return pl.pallas_call(
        functools.partial(lay_kernel, cut),
        out_shape=[jax.ShapeDtypeStruct((rows, cut.total), F32)] * 3,
        in_specs=[pl.BlockSpec(memory_space=pltpu.SMEM)] + [vmem] * len(pieces),
        out_specs=[vmem] * 3,
        compiler_params=pltpu.CompilerParams(vmem_limit_bytes=32 * MIB),
        cost_estimate=FREE,
    )(owners, *pieces)


def feed_kernel(count, sums, *refs):
    t_ref, c_ref, w_ref = refs[:3]
    p_ref, back_ref, out_ref = refs[-3:]
    gate_weight, up_weight, down_weight = (
        w_ref.at[:, i * count : (i + 1) * count] for i in range(3)
    )
    tokens = t_ref[...]
    gate = product(tokens, gate_weight[...])
    upper = product(tokens, up_weight[...])
    act_back = product(c_ref[...], down_weight[...])
    sigma = 1.0 / (1.0 + jnp.exp(-gate))
    swish = gate * sigma
    activated = (swish * upper).astype(BF16)
    gate_back = (act_back * upper * sigma * (1.0 + gate * (1.0 - sigma))).astype(BF16)
    upper_back = (act_back * swish).astype(BF16)
    for i, value in enumerate((gate_back, upper_back, activated)):
        p_ref[:, i * count : (i + 1) * count] = value
    back = right_product(gate_back, gate_weight[...]) + right_product(upper_back, up_weight[...])
    out = right_product(activated, down_weight[...])
    if sums:
        back = back + refs[3][...]
        out = out + refs[4][...]
    back_ref[...] = back.astype(back_ref.dtype)
    out_ref[...] = out.astype(out_ref.dtype)


def feed(tokens, cots, weights, side, kept, earlier, dtype):
    rows, width = tokens.shape
    columns = weights.shape[1]
    span = rows // 2
    tall = min(256, span)
    steps = span // tall
    block = lambda w: pl.BlockSpec((tall, w), lambda i: (side * steps + i, 0))
    near = pl.BlockSpec((tall, width), lambda i: (i, 0))
    operands = [tokens, cots, weights]
    in_specs = [
        block(width),
        block(width),
        pl.BlockSpec((width, columns), lambda i: (0, 0), pipeline_mode=pl.Buffered(1)),
    ]
    if earlier is not None:
        operands += list(earlier)
        in_specs += [near, near]
    aliases = {}
    if kept is not None:
        aliases = {len(operands): 0}
        operands.append(kept)
        in_specs.append(pl.BlockSpec(memory_space=pl.ANY))
    return pl.pallas_call(
        functools.partial(feed_kernel, columns // 3, earlier is not None),
        grid=(steps,),
        in_specs=in_specs,
        out_specs=[block(columns), near, near],
        out_shape=[
            jax.ShapeDtypeStruct((rows, columns), BF16),
            jax.ShapeDtypeStruct((span, width), dtype),
            jax.ShapeDtypeStruct((span, width), dtype),
        ],
        input_output_aliases=aliases,
        compiler_params=pltpu.CompilerParams(vmem_limit_bytes=56 * MIB),
        cost_estimate=FREE,
    )(*operands)


def grads_kernel(split, t_ref, c_ref, p_ref, o_ref):
    step = pl.program_id(0)

    @pl.when(step < split)
    def _():
        o_ref[...] = left_product(t_ref[...], p_ref[...]).astype(BF16)

    @pl.when(step >= split)
    def _():
        o_ref[...] = left_product(c_ref[...], p_ref[...]).astype(BF16)


def unit_gradients(tokens, cots, kept, which=(0, 1, 2), cost=FREE):
    rows, width = tokens.shape
    count = kept.shape[1] // 3
    wide = 384 if count % 384 == 0 else 128
    each = count // wide
    split = each * sum(i < 2 for i in which)
    first = which[0] * each
    held = pl.BlockSpec((rows, width), lambda i: (0, 0), pipeline_mode=pl.Buffered(1))
    return pl.pallas_call(
        functools.partial(grads_kernel, split),
        grid=(each * len(which),),
        in_specs=[held, held, pl.BlockSpec((rows, wide), lambda i: (0, first + i))],
        out_specs=pl.BlockSpec((width, wide), lambda i: (0, i)),
        out_shape=jax.ShapeDtypeStruct((width, len(which) * count), BF16),
        compiler_params=pltpu.CompilerParams(vmem_limit_bytes=56 * MIB),
        cost_estimate=cost,
    )(tokens, cots, kept)


def plane_gather(own, *others):
    cut = own.shape[0] // 2
    over_x, over_y, *others = together(dp_swap(own, 2), y_swap(own), *others)
    far_x = y_swap(over_x[:cut])
    far_y = dp_swap(over_y[cut:], 2)
    near = [own, over_y, over_x]
    across = [dp_swap(piece, 1) for piece in near]
    far_x, far_y, *across = together(far_x, far_y, *across)
    far = jnp.concatenate([far_x, far_y], axis=0)
    return near + [far] + across + [dp_swap(far, 1)], others


def plane_scatter(near, over_core, beside):
    t = near.shape[0] // 4
    cut = t // 2

    def summed(low, high):
        return near[low:high] + over_core[low:high].astype(F32)

    corner = summed(3 * t, 4 * t).astype(BF16)
    corner_x, corner_y = beside[0](corner, dp_swap(corner[:cut], 2), y_swap(corner[cut:]))
    to_y = jnp.concatenate(
        [summed(t, t + cut) + corner_x.astype(F32), summed(t + cut, 2 * t)], axis=0
    ).astype(BF16)
    to_x = jnp.concatenate(
        [summed(2 * t, 2 * t + cut), summed(2 * t + cut, 3 * t) + corner_y.astype(F32)], axis=0
    ).astype(BF16)
    over_x, over_y = beside[1](to_x, dp_swap(to_x, 2), y_swap(to_y))
    return summed(0, t) + over_x.astype(F32) + over_y.astype(F32)


def sum_over(values, axes):
    for axis in axes:
        size = lax.axis_size(axis)
        flip = 1
        while flip < size:
            values = values + lax.ppermute(values, axis, [(i, i ^ flip) for i in range(size)])
            flip *= 2
    return values


def on_device(
    hidden, cotangent, segments, positions, first_gain,
    query_weight, query_bias, key_weight, key_bias, value_weight, value_bias,
    out_weight, second_gain, gate_weight, up_weight, down_weight,
):
    n_dp, n_seq = lax.axis_size("dp"), lax.axis_size("seq")
    dp, seq, tensor = (lax.axis_index(a) for a in ("dp", "seq", "tensor"))
    rows, width = hidden.shape
    half = rows // 2
    share = query_weight.shape[0]
    group = segments.shape[0]
    blocks = group // rows
    q_width, kv_width = query_weight.shape[1], key_weight.shape[1]
    kv_end = q_width + kv_width
    dp_owners = jnp.stack([dp ^ k for k in range(n_dp)]).astype(jnp.int32)
    dp_slots = (dp_owners % 2) * (n_dp // 2) + dp_owners // 2
    seq_places = jnp.stack([(seq - s) % n_seq for s in range(n_seq)]).astype(jnp.int32)

    def vector_in(vector):
        parts = vector.reshape(n_dp // 2, 2, n_seq, share)
        return parts.transpose(2, 1, 0, 3).reshape(width).astype(F32)

    def vector_out(vector):
        parts = vector.reshape(n_seq, 2, n_dp // 2, share)
        return parts.transpose(2, 1, 0, 3).reshape(width)

    index = jnp.arange(width, dtype=jnp.int32)
    owner, place = index // (share * n_seq), index // share % n_seq
    slot = owner % 2 * (n_dp // 2) + owner // 2
    inner_of = (place * n_dp + slot) * share + index % share
    shuffle = (inner_of[:, None] == index[None, :]).astype(BF16)

    def relative(values):
        turned = jnp.concatenate([values[half:], values[:half]], axis=0)
        return jnp.where(tensor == 0, values, turned)

    def to_inner(values):
        return product(relative(values), shuffle).astype(BF16)

    def from_inner(values):
        return right_product(values, shuffle).astype(BF16)

    gain_first, gain_second = vector_in(first_gain), vector_in(second_gain)

    def slots_of(flips):
        return jnp.stack(
            [seq_places[s] * n_dp + dp_slots[k] for k in flips for s in range(n_seq)]
        ).astype(jnp.int32)

    cut = Cut(gate_weight.shape[1], n_dp)

    def spread(pieces):
        return [dp_swap(piece, k) if k else piece for k, piece in enumerate(pieces)]

    def stack_units(pieces):
        return assemble(pieces, dp_slots).reshape(n_dp * share, pieces[0].shape[1])

    line = [jnp.concatenate([query_weight, key_weight, value_weight, out_weight.T], axis=1)]
    over_x = []
    for s in range(n_seq):
        over_x.append(dp_swap(line[s], 2))
        if s + 1 == n_seq:
            cot_own = to_inner(cotangent)
            over_x[s], cot_own = together(over_x[s], cot_own)
            break
        moved = z_shift(line[s], 1)
        if s == 0:
            first_parts, second_parts = cut_units(
                cut, (gate_weight, up_weight, down_weight.T), dp_owners
            )
            moved, over_x[s], *parts = together(moved, over_x[s], *first_parts, *second_parts)
            first_parts, second_parts = parts[:n_dp], parts[n_dp:]
        elif s == 1:
            first_parts = spread(first_parts)
            inputs = to_inner(hidden)
            moved, over_x[s], inputs, *first_parts = together(
                moved, over_x[s], inputs, *first_parts
            )
        elif s == 2:
            first_stacked = stack_units(first_parts)
            first_units = lax.all_gather(first_stacked, "seq", axis=0, tiled=True)
            moved, over_x[s], first_stacked = together(moved, over_x[s], first_stacked)
        else:
            moved, over_x[s] = together(moved, over_x[s])
        line.append(moved)
    mine = assemble(line + over_x, jnp.arange(2 * n_seq, dtype=jnp.int32))
    mine, *second_parts = together(mine, *second_parts)
    theirs = dp_swap(mine, 1)
    second_parts = spread(second_parts)
    all_places = slots_of((0, 2, 1, 3))

    own_place = relative(lax.dynamic_slice_in_dim(positions, seq * rows, rows))
    own_segment = relative(lax.dynamic_slice_in_dim(segments, seq * rows, rows))
    cosine, sine = rope_tables(own_place, HEAD_DIM)
    cosine = jnp.concatenate([cosine, cosine], axis=1)
    sine = jnp.concatenate([-sine, sine], axis=1)
    bias = jnp.concatenate([query_bias, key_bias, value_bias]).astype(F32)
    queries, own_kv, first_rounded, attention_weights = project(
        mine, theirs, all_places, inputs, gain_first, bias, cosine, sine, q_width, kv_width
    )
    qkv_end = q_width + 2 * kv_width
    attention_weights = attention_weights.reshape(width, qkv_end + q_width)
    qkv_full, out_full = attention_weights[:, :qkv_end], attention_weights[:, qkv_end:]
    own_kv, cot_own = together(own_kv, cot_own)
    cot_x = dp_swap(cot_own, 2)
    group_kv = [own_kv] + [z_shift(own_kv, s) for s in range(1, n_seq)]
    second_stacked = stack_units(second_parts)
    second_units = lax.all_gather(second_stacked, "seq", axis=0, tiled=True)
    *group_kv, second_stacked = together(*group_kv, second_stacked)
    group_kv = jnp.concatenate(group_kv, axis=0)
    keys, values = group_kv[:, :kv_width], group_kv[:, kv_width:]

    def key_rows(vector):
        taken = jnp.take(vector.reshape(blocks, rows), seq_places, axis=0)
        return relative(taken.T).T

    seg_k, pos_k = key_rows(segments), key_rows(positions)
    seen = pair_mask(
        own_segment[None, :, None], own_place[None, :, None], seg_k[:, None, :], pos_k[:, None, :]
    )
    flags = (jnp.any(seen, axis=(1, 2)).astype(jnp.int32) + jnp.all(seen, axis=(1, 2))).astype(
        jnp.int32
    )
    pairs = (
        own_segment[:, None], own_place[:, None], seg_k[:, None, :], pos_k[:, None, :], flags,
    )
    attended, lse = attend(queries, keys, values, *pairs)
    attended, cot_x = together(attended, cot_x)
    cot_pieces = [cot_own, cot_x, dp_swap(cot_own, 1), dp_swap(cot_x, 1)]

    def reduce_halves(part):
        return part[:half] + y_swap(part[half:].astype(BF16)).astype(F32)

    inputs_half = inputs[:half].astype(F32)
    out_theirs = y_swap(right_product(attended[half:], out_full).astype(BF16))
    out_mine = right_product(attended[:half], out_full)
    out_theirs, out_mine, *cot_pieces = together(out_theirs, out_mine, *cot_pieces)
    cots = assemble(cot_pieces, jnp.arange(4, dtype=jnp.int32)).reshape(-1, width)
    residual = inputs_half + out_mine + out_theirs.astype(F32)
    second_inverse = inverse_rms(residual)
    second_normed = residual * second_inverse
    second_rounded = (second_normed * gain_second).astype(BF16)

    gathered, (cots,) = plane_gather(second_rounded, cots)
    tokens = assemble(gathered, jnp.arange(len(gathered), dtype=jnp.int32)).reshape(-1, width)

    kept, *far = feed(tokens, cots, first_units, 1, None, None, F32)
    kept, *near = feed(tokens, cots, first_units, 0, kept, None, F32)
    first_gradient = unit_gradients(tokens, cots, kept)
    second_weights = after(second_units, first_gradient)
    second_kept, back_far, out_far = feed(tokens, cots, second_weights, 1, None, far, BF16)
    second_kept, back_near, out_near = feed(
        tokens, cots, second_weights, 0, second_kept, near, F32
    )
    second_gradients = []

    def cost_of(count):
        flops = 2 * count * tokens.size * cut.width[1]
        return pl.CostEstimate(flops=flops, bytes_accessed=0, transcendentals=0)

    def gradients_beside(which):
        def run(operand, *moved):
            gradient = unit_gradients(
                tokens, cots, after(second_kept, operand), which, cost_of(len(which))
            )
            *moved, gradient = together(*moved, gradient)
            second_gradients.append(gradient)
            return moved

        return run

    back_core, back_near = together(dp_swap(back_far, 1), back_near)
    second_back = plane_scatter(
        back_near, back_core, (gradients_beside((2,)), gradients_beside((0, 1)))
    )

    def scatter_units(gradient):
        return lax.psum_scatter(gradient, "seq", scatter_dimension=0, tiled=True)

    def exchange_units(mine):
        mine = mine.reshape(n_dp, share, mine.shape[1])
        pieces = []
        for k in range(n_dp):
            piece = lax.dynamic_index_in_dim(mine, dp_slots[k], 0, keepdims=False)
            pieces.append(dp_swap(piece, k) if k else piece)
        return pieces

    first_share = scatter_units(first_gradient)
    second_shares = [scatter_units(g) for g in second_gradients]

    residual_inner, second_gain_term = norm_backward(
        second_back, second_normed, second_inverse, gain_second
    )
    residual_back = cot_own[:half].astype(F32) + residual_inner
    back_half = residual_back.astype(BF16)
    back_other, out_core = together(y_swap(back_half), dp_swap(after(out_far, back_half), 1))
    attention_back = jnp.concatenate([back_half, back_other], axis=0)

    take = lax.dynamic_index_in_dim
    core, x = dp % 2, dp // 2

    def core_halves(gradient):
        parts = gradient.reshape(n_seq, 2, (n_dp // 2) * share, gradient.shape[1])
        return take(parts, core, 1, keepdims=False), take(parts, 1 - core, 1, keepdims=False)

    def x_halves(own, over_core):
        parts = own.astype(F32) + over_core.astype(F32)
        parts = parts.reshape(n_seq, n_dp // 2, share, own.shape[2])
        return take(parts, x, 1, keepdims=False), take(parts, 1 - x, 1, keepdims=False).astype(BF16)

    def place_of(parts, s):
        return take(parts, seq_places[s % n_seq], 0, keepdims=False)

    attended_back = product(attention_back, out_full).astype(BF16)
    out_own, out_sent = core_halves(
        left_product(attention_back, attended).astype(BF16)
    )
    attended_back, first_share, out_sent = together(attended_back, first_share, out_sent)

    over_core = dp_swap(out_sent, 1)
    query_linear_back, key_parts, value_parts = attend_back(
        queries, keys, values, attended_back, lse, cosine, sine, *pairs
    )

    def plain(operand, *moved):
        *moved, operand = together(*moved, operand)
        return moved

    kv_parts = jnp.concatenate([key_parts, value_parts], axis=1)
    kv_parts, over_core, query_linear_back = together(kv_parts, over_core, query_linear_back)

    kv_moved = [z_shift(kv_parts[s * rows : (s + 1) * rows], -s) for s in range(1, n_seq)]
    out_parts, out_sent = x_halves(out_own, over_core)
    out_over_x = dp_swap(out_sent, 2)
    query_own, query_sent = core_halves(
        left_product(first_rounded, query_linear_back).astype(BF16)
    )
    over_core = dp_swap(query_sent, 1)
    *kv_moved, out_over_x, over_core = together(*kv_moved, out_over_x, over_core)
    out_parts = out_parts + out_over_x.astype(F32)
    kv_back = kv_parts[:rows].astype(F32)
    for moved in kv_moved:
        kv_back = kv_back + moved.astype(F32)
    key_linear_back = rotate(
        kv_back[:, :kv_width], cosine[:, : HEAD_DIM // 2], -sine[:, HEAD_DIM // 2 :]
    )
    kv_linear_back = jnp.concatenate([key_linear_back, kv_back[:, kv_width:]], axis=1).astype(BF16)
    linear_back = jnp.concatenate([query_linear_back, kv_linear_back], axis=1)

    query_parts, query_sent = x_halves(query_own, over_core)
    query_over_x = dp_swap(query_sent, 2)
    kv_own, kv_sent = core_halves(left_product(first_rounded, kv_linear_back).astype(BF16))
    over_core = dp_swap(kv_sent, 1)
    first_theirs = y_swap(right_product(linear_back[half:], qkv_full).astype(BF16))
    first_mine = right_product(linear_back[:half], qkv_full)
    query_over_x, over_core, first_theirs, first_mine = together(
        query_over_x, over_core, first_theirs, first_mine
    )
    first_back = first_mine + first_theirs.astype(F32)
    query_parts = query_parts + query_over_x.astype(F32)
    large = jnp.concatenate([query_parts, out_parts], axis=2)

    kv_own, kv_sent = x_halves(kv_own, over_core)
    kv_over_x = dp_swap(kv_sent, 2)
    total = z_shift(place_of(large, 1).astype(BF16), 1)
    first_inverse = inverse_rms(inputs_half)
    input_inner, first_gain_term = norm_backward(
        first_back, inputs_half * first_inverse, first_inverse, gain_first
    )
    input_half = from_inner((residual_back + input_inner).astype(BF16))
    input_other = y_swap(input_half)
    total, kv_over_x, input_other = together(total, kv_over_x, input_other)
    input_gradient = relative(jnp.concatenate([input_half, input_other], axis=0))
    kv_rows = kv_own + kv_over_x.astype(F32)
    kv_total = place_of(kv_rows, 1).astype(BF16)
    first_received = exchange_units(first_share)
    for s in range(1, n_seq):
        total = place_of(large, s + 1) + total.astype(F32)
        kv_total = place_of(kv_rows, s + 1) + z_shift(kv_total, 1).astype(F32)
        if s + 1 < n_seq:
            total, kv_total = together(z_shift(total.astype(BF16), 1), kv_total.astype(BF16))
    large_share, kv_share = total, kv_total
    out_gradient = large_share[:, q_width:].T
    down_out = plane_scatter(out_near, out_core, (plain, plain))
    out_half = from_inner((residual + down_out).astype(BF16))
    output = relative(jnp.concatenate([out_half, y_swap(out_half)], axis=0))
    second_pieces = [exchange_units(share_of) for share_of in second_shares]
    gate_gradient, up_gradient, down_gradient = lay_units(
        cut, first_received + second_pieces[1] + second_pieces[0], dp_owners
    )
    down_gradient = down_gradient.T

    bias_terms = jnp.sum(linear_back.astype(F32), axis=0)
    sums = sum_over(
        jnp.concatenate([first_gain_term, second_gain_term, bias_terms]), ("dp", "seq")
    )
    gain_terms = sum_over(sums[: 2 * width], ("tensor",))
    bias_terms = sums[2 * width :]
    return (
        output,
        input_gradient,
        vector_out(gain_terms[:width]),
        large_share[:, :q_width],
        bias_terms[:q_width],
        kv_share[:, :kv_width],
        bias_terms[q_width:kv_end],
        kv_share[:, kv_width:],
        bias_terms[kv_end:],
        out_gradient,
        vector_out(gain_terms[width:]),
        gate_gradient,
        up_gradient,
        down_gradient,
    )


def solution(mesh):
    tokens = P(("dp", "seq"), None)
    by_row = P(("dp", "seq"), "tensor")
    by_column = P("tensor", ("dp", "seq"))
    heads = P("tensor")
    in_specs = (
        tokens, tokens, P("dp"), P("dp"), P(), by_row, heads, by_row, heads, by_row, heads,
        by_column, P(), by_row, by_row, by_column,
    )
    out_specs = (
        tokens, tokens, P(), by_row, heads, by_row, heads, by_row, heads, by_column, P(),
        by_row, by_row, by_column,
    )
    return jax.shard_map(
        on_device, mesh=mesh, in_specs=in_specs, out_specs=out_specs, check_vma=False
    )
```

```python
import functools
import math

import jax
import jax.numpy as jnp
from jax import lax
from jax.experimental import pallas as pl
from jax.experimental.pallas import tpu as pltpu
from jax.sharding import PartitionSpec as P

HEAD_DIM = 128
EPS = 1e-06
LOG_BASE = math.log(1000000.0)
NEG_FILL = -1e30
LOG2E = 1.0 / math.log(2.0)
MIB = 1024 * 1024
F32 = jnp.float32
BF16 = jnp.bfloat16
FREE = pl.CostEstimate(flops=0, bytes_accessed=0, transcendentals=0)


def product(left, right):
    return jnp.dot(left, right, preferred_element_type=F32)


def left_product(left, right):
    return lax.dot_general(left, right, (((0,), (0,)), ((), ())), preferred_element_type=F32)


def right_product(left, right):
    return lax.dot_general(left, right, (((1,), (1,)), ((), ())), preferred_element_type=F32)


def after(value, *others):
    return lax.optimization_barrier((value,) + others)[0]


def together(*values):
    return lax.optimization_barrier(values)


def dp_swap(value, flip):
    size = lax.axis_size("dp")
    return lax.ppermute(value, "dp", [(i, i ^ flip) for i in range(size)])


def y_swap(value):
    return lax.ppermute(value, "tensor", [(0, 1), (1, 0)])


def z_shift(value, step):
    size = lax.axis_size("seq")
    return lax.ppermute(value, "seq", [(i, (i + step) % size) for i in range(size)])


def assemble_kernel(count, place_ref, *refs):
    pieces, out_ref, sems = refs[:count], refs[count], refs[count + 1]
    copies = [
        pltpu.make_async_copy(piece, out_ref.at[place_ref[i]], sems.at[i])
        for i, piece in enumerate(pieces)
    ]
    for copy in copies:
        copy.start()
    for copy in copies:
        copy.wait()


def assemble(pieces, places):
    count = len(pieces)
    return pl.pallas_call(
        functools.partial(assemble_kernel, count),
        out_shape=jax.ShapeDtypeStruct((count,) + pieces[0].shape, pieces[0].dtype),
        in_specs=[pl.BlockSpec(memory_space=pltpu.SMEM)]
        + [pl.BlockSpec(memory_space=pl.ANY)] * count,
        out_specs=pl.BlockSpec(memory_space=pltpu.VMEM),
        scratch_shapes=[pltpu.SemaphoreType.DMA((count,))],
        compiler_params=pltpu.CompilerParams(vmem_limit_bytes=24 * MIB),
        cost_estimate=FREE,
    )(places, *pieces)


def pair_mask(seg_q, pos_q, seg_k, pos_k):
    return ((seg_k == 0) | (seg_k == seg_q)) & (pos_k <= pos_q)


def attend_kernel(
    rows, factor, flag_ref, q_ref, k_ref, v_ref, sq_ref, pq_ref, sk_ref, pk_ref,
    o_ref, lse_ref, top_ref, sum_ref, acc_ref,
):
    blocks = k_ref.shape[0] // rows
    top_ref[...] = jnp.full_like(top_ref, NEG_FILL)
    sum_ref[...] = jnp.zeros_like(sum_ref)
    acc_ref[...] = jnp.zeros_like(acc_ref)
    q = q_ref[...]

    def block_step(j, masked):
        span = pl.ds(pl.multiple_of(j * rows, rows), rows)
        s = right_product(q, k_ref[span, :]) * factor
        if masked:
            mask = pair_mask(sq_ref[...], pq_ref[...], sk_ref[j], pk_ref[j])
            s = jnp.where(mask, s, NEG_FILL)
        top = top_ref[...]
        new_top = jnp.maximum(top, jnp.max(s, axis=1, keepdims=True))
        e = jnp.exp2(s - new_top)
        if masked:
            e = jnp.where(mask, e, 0.0)
        shrink = jnp.exp2(top - new_top)
        top_ref[...] = new_top
        sum_ref[...] = sum_ref[...] * shrink + jnp.sum(e, axis=1, keepdims=True)
        acc_ref[...] = acc_ref[...] * shrink + product(e.astype(BF16), v_ref[span, :])

    def step(j, carry):
        @pl.when(flag_ref[j] == 2)
        def _():
            block_step(j, False)

        @pl.when(flag_ref[j] == 1)
        def _():
            block_step(j, True)

        return carry

    lax.fori_loop(0, blocks, step, 0)
    total = sum_ref[...]
    o_ref[...] = (acc_ref[...] / total).astype(o_ref.dtype)
    lse_ref[...] = (top_ref[...] + jnp.log2(total))[None]


def attend(q, keys, values, seg_q, pos_q, seg_k, pos_k, flags):
    rows, width = q.shape
    heads = width // HEAD_DIM
    kv_heads = keys.shape[1] // HEAD_DIM
    repeat = heads // kv_heads
    length = keys.shape[0]
    blocks = length // rows
    whole = lambda *shape: pl.BlockSpec(shape, lambda h: (0,) * len(shape))
    return pl.pallas_call(
        functools.partial(attend_kernel, rows, HEAD_DIM ** (-0.5) * LOG2E),
        grid=(heads,),
        in_specs=[
            pl.BlockSpec(memory_space=pltpu.SMEM),
            pl.BlockSpec((rows, HEAD_DIM), lambda h: (0, h)),
            pl.BlockSpec((length, HEAD_DIM), lambda h: (0, h // repeat)),
            pl.BlockSpec((length, HEAD_DIM), lambda h: (0, h // repeat)),
            whole(rows, 1),
            whole(rows, 1),
            whole(blocks, 1, rows),
            whole(blocks, 1, rows),
        ],
        out_specs=[
            pl.BlockSpec((rows, HEAD_DIM), lambda h: (0, h)),
            pl.BlockSpec((1, rows, 1), lambda h: (h, 0, 0)),
        ],
        out_shape=[
            jax.ShapeDtypeStruct((rows, width), BF16),
            jax.ShapeDtypeStruct((heads, rows, 1), F32),
        ],
        scratch_shapes=[
            pltpu.VMEM((rows, 1), F32),
            pltpu.VMEM((rows, 1), F32),
            pltpu.VMEM((rows, HEAD_DIM), F32),
        ],
        compiler_params=pltpu.CompilerParams(vmem_limit_bytes=40 * MIB),
        cost_estimate=FREE,
    )(flags, q, keys, values, seg_q, pos_q, seg_k, pos_k)


def attend_back_kernel(
    rows, factor, scale, repeat, flag_ref, q_ref, k_ref, v_ref, do_ref, lse_ref, cos_ref, sin_ref,
    sq_ref, pq_ref, sk_ref, pk_ref, dq_ref, dkv_ref, dk_acc, dv_acc, dq_acc,
    p_keep, dp_keep, delta_ref,
):
    head = pl.program_id(0)
    blocks = k_ref.shape[0] // rows

    @pl.when(lax.rem(head, repeat) == 0)
    def _():
        dk_acc[...] = jnp.zeros_like(dk_acc)
        dv_acc[...] = jnp.zeros_like(dv_acc)

    dq_acc[...] = jnp.zeros_like(dq_acc)
    delta_ref[...] = jnp.zeros_like(delta_ref)
    q = q_ref[...]
    d_o = do_ref[...]
    lse = lse_ref[0]

    def span_of(j):
        return pl.ds(pl.multiple_of(j * rows, rows), rows)

    def first_pass(j, masked):
        p = jnp.exp2(right_product(q, k_ref[span_of(j), :]) * factor - lse)
        if masked:
            mask = pair_mask(sq_ref[...], pq_ref[...], sk_ref[j], pk_ref[j])
            p = jnp.where(mask, p, 0.0)
        dp = right_product(d_o, v_ref[span_of(j), :])
        p_keep[j] = p
        dp_keep[j] = dp
        delta_ref[...] += jnp.sum(p * dp, axis=1, keepdims=True)

    def first_step(j, carry):
        @pl.when(flag_ref[j] == 2)
        def _():
            first_pass(j, False)

        @pl.when(flag_ref[j] == 1)
        def _():
            first_pass(j, True)

        return carry

    lax.fori_loop(0, blocks, first_step, 0)

    def second_step(j, carry):
        @pl.when(flag_ref[j] > 0)
        def _():
            p = p_keep[j]
            ds = (p * (dp_keep[j] - delta_ref[...])).astype(BF16)
            span = span_of(j)
            dv_acc[span, :] += left_product(p.astype(BF16), d_o)
            dk_acc[span, :] += left_product(ds, q)
            dq_acc[...] += product(ds, k_ref[span, :])

        return carry

    lax.fori_loop(0, blocks, second_step, 0)
    (turned,) = rope_lanes(dq_acc[...] * scale, cos_ref[...], -sin_ref[...])
    dq_ref[...] = turned.astype(dq_ref.dtype)

    @pl.when(lax.rem(head, repeat) == repeat - 1)
    def _():
        dkv_ref[:, :HEAD_DIM] = (dk_acc[...] * scale).astype(dkv_ref.dtype)
        dkv_ref[:, HEAD_DIM:] = dv_acc[...].astype(dkv_ref.dtype)


def attend_back(q, keys, values, d_o, lse, cosine, sine, seg_q, pos_q, seg_k, pos_k, flags):
    rows, width = q.shape
    heads = width // HEAD_DIM
    kv_heads = keys.shape[1] // HEAD_DIM
    repeat = heads // kv_heads
    length = keys.shape[0]
    blocks = length // rows
    whole = lambda *shape: pl.BlockSpec(shape, lambda h: (0,) * len(shape))
    per_head = pl.BlockSpec((rows, HEAD_DIM), lambda h: (0, h))
    held = pl.BlockSpec(
        (length, HEAD_DIM), lambda h: (0, h // repeat), pipeline_mode=pl.Buffered(1)
    )
    return pl.pallas_call(
        functools.partial(
            attend_back_kernel, rows, HEAD_DIM ** (-0.5) * LOG2E, HEAD_DIM ** (-0.5), repeat
        ),
        grid=(heads,),
        in_specs=[
            pl.BlockSpec(memory_space=pltpu.SMEM),
            per_head,
            held,
            held,
            per_head,
            pl.BlockSpec((1, rows, 1), lambda h: (h, 0, 0)),
            whole(rows, HEAD_DIM),
            whole(rows, HEAD_DIM),
            whole(rows, 1),
            whole(rows, 1),
            whole(blocks, 1, rows),
            whole(blocks, 1, rows),
        ],
        out_specs=[per_head, pl.BlockSpec((length, 2 * HEAD_DIM), lambda h: (0, h // repeat))],
        out_shape=[
            jax.ShapeDtypeStruct((rows, width), BF16),
            jax.ShapeDtypeStruct((length, 2 * keys.shape[1]), BF16),
        ],
        scratch_shapes=[
            pltpu.VMEM((length, HEAD_DIM), F32),
            pltpu.VMEM((length, HEAD_DIM), F32),
            pltpu.VMEM((rows, HEAD_DIM), F32),
            pltpu.VMEM((blocks, rows, rows), F32),
            pltpu.VMEM((blocks, rows, rows), F32),
            pltpu.VMEM((rows, 1), F32),
        ],
        compiler_params=pltpu.CompilerParams(vmem_limit_bytes=58 * MIB),
        cost_estimate=FREE,
    )(flags, q, keys, values, d_o, lse, cosine, sine, seg_q, pos_q, seg_k, pos_k)


def rope_tables(places, width):
    half = width // 2
    freq = jnp.exp(jnp.arange(half, dtype=F32) * (-2.0 * LOG_BASE / width))
    angle = places.astype(F32)[:, None] * freq[None, :]
    return (jnp.cos(angle), jnp.sin(angle))


def rotate(values, cosine, sine):
    half = HEAD_DIM // 2
    parts = []
    for at in range(0, values.shape[1], HEAD_DIM):
        first = values[:, at : at + half]
        second = values[:, at + half : at + HEAD_DIM]
        parts += [first * cosine - second * sine, second * cosine + first * sine]
    return jnp.concatenate(parts, axis=1)


def inverse_rms(values):
    return lax.rsqrt(jnp.mean(values * values, axis=-1, keepdims=True) + EPS)


def norm_backward(upstream, normed, inverse, gain):
    scaled = upstream * gain
    inner = inverse * (scaled - normed * jnp.mean(scaled * normed, axis=-1, keepdims=True))
    return (inner, jnp.sum(upstream * normed, axis=0))


def rope_lanes(values, cosine, sine):
    parts = []
    for at in range(0, values.shape[1], HEAD_DIM):
        head = values[:, at : at + HEAD_DIM]
        parts.append(head * cosine + pltpu.roll(head, HEAD_DIM // 2, 1) * sine)
    return parts


def project_kernel(
    count, q_width, kv_width, place_ref, mine_ref, theirs_ref,
    x_ref, gain_ref, bias_ref, cos_ref, sin_ref, q_ref, kv_ref, h_ref, w_ref, sems,
):
    copies = [
        pltpu.make_async_copy(stack.at[i], w_ref.at[place_ref[at + i]], sems.at[at + i])
        for at, stack in ((0, mine_ref), (count, theirs_ref))
        for i in range(count)
    ]
    for copy in copies:
        copy.start()
    x = x_ref[...].astype(F32)
    normed = x * lax.rsqrt(jnp.mean(x * x, axis=1, keepdims=True) + EPS)
    h = (normed * gain_ref[...]).astype(BF16)
    h_ref[...] = h
    for copy in copies:
        copy.wait()
    depth, columns = x.shape[1], bias_ref.shape[1]
    weights = w_ref[...].reshape(depth, w_ref.shape[2])
    linear = product(h, weights[:, :columns]) + bias_ref[...]
    turned = rope_lanes(linear[:, : q_width + kv_width], cos_ref[...], sin_ref[...])
    heads = q_width // HEAD_DIM
    for i, part in enumerate(turned):
        if i < heads:
            q_ref[:, i * HEAD_DIM : (i + 1) * HEAD_DIM] = part.astype(BF16)
        else:
            at = (i - heads) * HEAD_DIM
            kv_ref[:, at : at + HEAD_DIM] = part.astype(BF16)
    kv_ref[:, kv_width:] = linear[:, q_width + kv_width :].astype(BF16)


def project(mine, theirs, places, inputs, gain, bias, cosine, sine, q_width, kv_width):
    count = mine.shape[0]
    rows, depth = inputs.shape
    columns = bias.shape[0]
    vmem = pl.BlockSpec(memory_space=pltpu.VMEM)
    return pl.pallas_call(
        functools.partial(project_kernel, count, q_width, kv_width),
        out_shape=[
            jax.ShapeDtypeStruct((rows, q_width), BF16),
            jax.ShapeDtypeStruct((rows, 2 * kv_width), BF16),
            jax.ShapeDtypeStruct((rows, depth), BF16),
            jax.ShapeDtypeStruct((2 * count,) + mine.shape[1:], BF16),
        ],
        in_specs=[pl.BlockSpec(memory_space=pltpu.SMEM)]
        + [pl.BlockSpec(memory_space=pl.ANY)] * 2
        + [vmem] * 5,
        out_specs=[vmem] * 4,
        scratch_shapes=[pltpu.SemaphoreType.DMA((2 * count,))],
        compiler_params=pltpu.CompilerParams(vmem_limit_bytes=40 * MIB),
        cost_estimate=FREE,
    )(places, mine, theirs, inputs, gain[None, :], bias[None, :], cosine, sine)


class Cut:
    def __init__(self, total, n_dp):
        tiles = total // n_dp // 128
        first = max(tiles * 3 // 8, 1)
        self.total = total
        self.n_dp = n_dp
        self.main = (first * 128, (tiles - first) * 128)
        self.start = (0, n_dp * self.main[0])
        self.rest_at = n_dp * (self.main[0] + self.main[1])
        self.rest = (total - self.rest_at) // n_dp
        pad = -(-self.rest // 128) * 128
        self.width = (self.main[0], self.main[1] + pad)


def pick(values, index):
    result = values[0]
    for i in range(1, len(values)):
        result = jnp.where(index == i, values[i], result)
    return result


def cut_kernel(cut, place_ref, *refs):
    weights, outs = refs[:3], refs[3:]
    n_dp = cut.n_dp
    for part in range(2):
        main, width = cut.main[part], cut.width[part]
        for k in range(n_dp):
            owner = place_ref[k]
            out = outs[part * n_dp + k]
            for i, w in enumerate(weights):
                at = i * width
                low = pl.multiple_of(cut.start[part] + owner * main, 128)
                out[:, at : at + main] = w[:, pl.ds(low, main)]
                if part == 1 and cut.rest:
                    tail = w[:, cut.rest_at :]
                    rest = pick(
                        [tail[:, b * cut.rest : (b + 1) * cut.rest] for b in range(n_dp)], owner
                    )
                    fill = jnp.zeros((rest.shape[0], width - main - cut.rest), rest.dtype)
                    out[:, at + main : at + width] = jnp.concatenate([rest, fill], axis=1)


def cut_units(cut, weights, owners):
    rows = weights[0].shape[0]
    vmem = pl.BlockSpec(memory_space=pltpu.VMEM)
    outs = pl.pallas_call(
        functools.partial(cut_kernel, cut),
        out_shape=[
            jax.ShapeDtypeStruct((rows, 3 * cut.width[part]), BF16)
            for part in range(2)
            for _ in range(cut.n_dp)
        ],
        in_specs=[pl.BlockSpec(memory_space=pltpu.SMEM)] + [vmem] * 3,
        out_specs=[vmem] * (2 * cut.n_dp),
        compiler_params=pltpu.CompilerParams(vmem_limit_bytes=24 * MIB),
        cost_estimate=FREE,
    )(owners, *weights)
    return outs[: cut.n_dp], outs[cut.n_dp :]


def lay_kernel(cut, place_ref, *refs):
    n_dp = cut.n_dp
    firsts, *seconds = (refs[i * n_dp : (i + 1) * n_dp] for i in range(4))
    outs = refs[4 * n_dp :]
    for i, out in enumerate(outs):
        for part in range(2):
            main, width = cut.main[part], cut.width[part]
            for k in range(n_dp):
                piece = seconds[i][k] if part else firsts[k].at[:, i * width : (i + 1) * width]
                owner = place_ref[k]
                low = pl.multiple_of(cut.start[part] + owner * main, 128)
                out[:, pl.ds(low, main)] = piece[:, :main].astype(F32)
        if cut.rest:
            main = cut.main[1]
            tails = [piece[:, main:].astype(F32)[:, : cut.rest] for piece in seconds[i]]
            laid = []
            for b in range(n_dp):
                laid.append(
                    functools.reduce(
                        lambda got, k: jnp.where(place_ref[k] == b, tails[k], got),
                        range(1, n_dp),
                        tails[0],
                    )
                )
            out[:, cut.rest_at :] = jnp.concatenate(laid, axis=1)


def lay_units(cut, pieces, owners):
    rows = pieces[0].shape[0]
    vmem = pl.BlockSpec(memory_space=pltpu.VMEM)
    return pl.pallas_call(
        functools.partial(lay_kernel, cut),
        out_shape=[jax.ShapeDtypeStruct((rows, cut.total), F32)] * 3,
        in_specs=[pl.BlockSpec(memory_space=pltpu.SMEM)] + [vmem] * len(pieces),
        out_specs=[vmem] * 3,
        compiler_params=pltpu.CompilerParams(vmem_limit_bytes=32 * MIB),
        cost_estimate=FREE,
    )(owners, *pieces)


def feed_kernel(count, sums, *refs):
    t_ref, c_ref, w_ref = refs[:3]
    p_ref, back_ref, out_ref = refs[-3:]
    gate_weight, up_weight, down_weight = (
        w_ref.at[:, i * count : (i + 1) * count] for i in range(3)
    )
    tokens = t_ref[...]
    gate = product(tokens, gate_weight[...])
    upper = product(tokens, up_weight[...])
    act_back = product(c_ref[...], down_weight[...])
    sigma = 1.0 / (1.0 + jnp.exp(-gate))
    swish = gate * sigma
    activated = (swish * upper).astype(BF16)
    gate_back = (act_back * upper * sigma * (1.0 + gate * (1.0 - sigma))).astype(BF16)
    upper_back = (act_back * swish).astype(BF16)
    for i, value in enumerate((gate_back, upper_back, activated)):
        p_ref[:, i * count : (i + 1) * count] = value
    back = right_product(gate_back, gate_weight[...]) + right_product(upper_back, up_weight[...])
    out = right_product(activated, down_weight[...])
    if sums:
        back = back + refs[3][...].astype(F32)
        out = out + refs[4][...].astype(F32)
    back_ref[...] = back.astype(back_ref.dtype)
    out_ref[...] = out.astype(out_ref.dtype)


def feed(tokens, cots, weights, side, kept, earlier):
    rows, width = tokens.shape
    columns = weights.shape[1]
    span = rows // 2
    tall = min(256, span)
    steps = span // tall
    block = lambda w: pl.BlockSpec((tall, w), lambda i: (side * steps + i, 0))
    near = pl.BlockSpec((tall, width), lambda i: (i, 0))
    operands = [tokens, cots, weights]
    in_specs = [
        block(width),
        block(width),
        pl.BlockSpec((width, columns), lambda i: (0, 0), pipeline_mode=pl.Buffered(1)),
    ]
    if earlier is not None:
        operands += list(earlier)
        in_specs += [near, near]
    aliases = {}
    if kept is not None:
        aliases = {len(operands): 0}
        operands.append(kept)
        in_specs.append(pl.BlockSpec(memory_space=pl.ANY))
    return pl.pallas_call(
        functools.partial(feed_kernel, columns // 3, earlier is not None),
        grid=(steps,),
        in_specs=in_specs,
        out_specs=[block(columns), near, near],
        out_shape=[
            jax.ShapeDtypeStruct((rows, columns), BF16),
            jax.ShapeDtypeStruct((span, width), BF16),
            jax.ShapeDtypeStruct((span, width), BF16),
        ],
        input_output_aliases=aliases,
        compiler_params=pltpu.CompilerParams(vmem_limit_bytes=56 * MIB),
        cost_estimate=FREE,
    )(*operands)


def grads_kernel(split, t_ref, c_ref, p_ref, o_ref):
    step = pl.program_id(0)

    @pl.when(step < split)
    def _():
        o_ref[...] = left_product(t_ref[...], p_ref[...]).astype(BF16)

    @pl.when(step >= split)
    def _():
        o_ref[...] = left_product(c_ref[...], p_ref[...]).astype(BF16)


def unit_gradients(tokens, cots, kept, which=(0, 1, 2), cost=FREE):
    rows, width = tokens.shape
    count = kept.shape[1] // 3
    wide = 384 if count % 384 == 0 else 128
    each = count // wide
    split = each * sum(i < 2 for i in which)
    first = which[0] * each
    held = pl.BlockSpec((rows, width), lambda i: (0, 0), pipeline_mode=pl.Buffered(1))
    return pl.pallas_call(
        functools.partial(grads_kernel, split),
        grid=(each * len(which),),
        in_specs=[held, held, pl.BlockSpec((rows, wide), lambda i: (0, first + i))],
        out_specs=pl.BlockSpec((width, wide), lambda i: (0, i)),
        out_shape=jax.ShapeDtypeStruct((width, len(which) * count), BF16),
        compiler_params=pltpu.CompilerParams(vmem_limit_bytes=56 * MIB),
        cost_estimate=cost,
    )(tokens, cots, kept)


def d_o_kernel(own_ref, other_ref, w_ref, d_o_ref, rows_ref):
    half = own_ref.shape[0]
    weights = w_ref[...]
    d_o_ref[:half] = product(own_ref[...], weights).astype(BF16)
    d_o_ref[half:] = product(other_ref[...], weights).astype(BF16)
    rows_ref[:half] = own_ref[...]
    rows_ref[half:] = other_ref[...]


def d_o_of(own, other, weights, first, count):
    half, width = own.shape
    wide = math.gcd(first, count)
    whole = lambda *shape: pl.BlockSpec(shape, lambda i: (0, 0))
    return pl.pallas_call(
        d_o_kernel,
        grid=(count // wide,),
        in_specs=[
            whole(half, width),
            whole(half, width),
            pl.BlockSpec((width, wide), lambda i: (0, first // wide + i)),
        ],
        out_specs=[pl.BlockSpec((2 * half, wide), lambda i: (0, i)), whole(2 * half, width)],
        out_shape=[
            jax.ShapeDtypeStruct((2 * half, count), BF16),
            jax.ShapeDtypeStruct((2 * half, width), BF16),
        ],
        compiler_params=pltpu.CompilerParams(vmem_limit_bytes=32 * MIB),
        cost_estimate=FREE,
    )(own, other, weights)


def halves_kernel(n_seq, share, core_ref, left_ref, right_ref, own_ref, sent_ref, keep_ref):
    keep_ref[...] = left_product(left_ref[...], right_ref[...]).astype(BF16)
    tall = own_ref.shape[1]
    for z in range(n_seq):
        for out, core in ((own_ref, core_ref[0]), (sent_ref, 1 - core_ref[0])):
            at = pl.multiple_of((z * 2 + core) * tall, share)
            out[z] = keep_ref[pl.ds(at, tall), :]


def gradient_halves(left, right, core, n_seq, share):
    width, columns = left.shape[1], right.shape[1]
    vmem = pl.BlockSpec(memory_space=pltpu.VMEM)
    half = jax.ShapeDtypeStruct((n_seq, width // (2 * n_seq), columns), BF16)
    return pl.pallas_call(
        functools.partial(halves_kernel, n_seq, share),
        out_shape=[half, half],
        in_specs=[pl.BlockSpec(memory_space=pltpu.SMEM), vmem, vmem],
        out_specs=[vmem, vmem],
        scratch_shapes=[pltpu.VMEM((width, columns), BF16)],
        compiler_params=pltpu.CompilerParams(vmem_limit_bytes=32 * MIB),
        cost_estimate=FREE,
    )(core, left, right)


def plane_gather(own, *others):
    cut = own.shape[0] // 2
    over_x, over_y, *others = together(dp_swap(own, 2), y_swap(own), *others)
    far_x = y_swap(over_x[:cut])
    far_y = dp_swap(over_y[cut:], 2)
    near = [own, over_y, over_x]
    across = [dp_swap(piece, 1) for piece in near]
    far_x, far_y, *across = together(far_x, far_y, *across)
    far = jnp.concatenate([far_x, far_y], axis=0)
    return near + [far] + across + [dp_swap(far, 1)], others


class PlaneScatter:
    def __init__(self, near, over_core):
        self.near, self.over_core = near, over_core
        self.t = near.shape[0] // 4
        self.cut = self.t // 2

    def summed(self, low, high):
        return self.near[low:high].astype(F32) + self.over_core[low:high].astype(F32)

    def corner(self):
        corner = self.summed(3 * self.t, 4 * self.t).astype(BF16)
        return corner[: self.cut], corner[self.cut :]

    def sides(self, corner_x, corner_y):
        t, cut = self.t, self.cut
        to_y = [self.summed(t, t + cut) + corner_x.astype(F32), self.summed(t + cut, 2 * t)]
        to_x = [
            self.summed(2 * t, 2 * t + cut),
            self.summed(2 * t + cut, 3 * t) + corner_y.astype(F32),
        ]
        return tuple(jnp.concatenate(part, axis=0).astype(BF16) for part in (to_x, to_y))

    def home(self, over_x, over_y):
        return self.summed(0, self.t) + over_x.astype(F32) + over_y.astype(F32)


def on_device(
    hidden, cotangent, segments, positions, first_gain,
    query_weight, query_bias, key_weight, key_bias, value_weight, value_bias,
    out_weight, second_gain, gate_weight, up_weight, down_weight,
):
    n_dp, n_seq = lax.axis_size("dp"), lax.axis_size("seq")
    dp, seq, tensor = (lax.axis_index(a) for a in ("dp", "seq", "tensor"))
    rows, width = hidden.shape
    half = rows // 2
    share = query_weight.shape[0]
    group = segments.shape[0]
    blocks = group // rows
    q_width, kv_width = query_weight.shape[1], key_weight.shape[1]
    kv_end = q_width + kv_width
    dp_owners = jnp.stack([dp ^ k for k in range(n_dp)]).astype(jnp.int32)
    dp_slots = (dp_owners % 2) * (n_dp // 2) + dp_owners // 2
    seq_places = jnp.stack([(seq - s) % n_seq for s in range(n_seq)]).astype(jnp.int32)

    def vector_in(vector):
        parts = vector.reshape(n_dp // 2, 2, n_seq, share)
        return parts.transpose(2, 1, 0, 3).reshape(width).astype(F32)

    def vector_out(vector):
        parts = vector.reshape(n_seq, 2, n_dp // 2, share)
        return parts.transpose(2, 1, 0, 3).reshape(width)

    index = jnp.arange(width, dtype=jnp.int32)
    owner, place = index // (share * n_seq), index // share % n_seq
    slot = owner % 2 * (n_dp // 2) + owner // 2
    inner_of = (place * n_dp + slot) * share + index % share
    shuffle = (inner_of[:, None] == index[None, :]).astype(BF16)

    def relative(values):
        turned = jnp.concatenate([values[half:], values[:half]], axis=0)
        return jnp.where(tensor == 0, values, turned)

    def to_inner(values):
        return product(relative(values), shuffle).astype(BF16)

    def from_inner(values):
        return right_product(values, shuffle).astype(BF16)

    gain_first, gain_second = vector_in(first_gain), vector_in(second_gain)

    def slots_of(flips):
        return jnp.stack(
            [seq_places[s] * n_dp + dp_slots[k] for k in flips for s in range(n_seq)]
        ).astype(jnp.int32)

    cut = Cut(gate_weight.shape[1], n_dp)

    def spread(pieces):
        return [dp_swap(piece, k) if k else piece for k, piece in enumerate(pieces)]

    def stack_units(pieces):
        return assemble(pieces, dp_slots).reshape(n_dp * share, pieces[0].shape[1])

    line = [jnp.concatenate([query_weight, key_weight, value_weight, out_weight.T], axis=1)]
    over_x = []
    for s in range(n_seq):
        over_x.append(dp_swap(line[s], 2))
        if s + 1 == n_seq:
            cot_own = to_inner(cotangent)
            over_x[s], cot_own = together(over_x[s], cot_own)
            break
        moved = z_shift(line[s], 1)
        if s == 0:
            first_parts, second_parts = cut_units(
                cut, (gate_weight, up_weight, down_weight.T), dp_owners
            )
            moved, over_x[s], *parts = together(moved, over_x[s], *first_parts, *second_parts)
            first_parts, second_parts = parts[:n_dp], parts[n_dp:]
        elif s == 1:
            first_parts = spread(first_parts)
            inputs = to_inner(hidden)
            moved, over_x[s], inputs, *first_parts = together(
                moved, over_x[s], inputs, *first_parts
            )
        elif s == 2:
            first_stacked = stack_units(first_parts)
            first_units = lax.all_gather(first_stacked, "seq", axis=0, tiled=True)
            moved, over_x[s], first_stacked = together(moved, over_x[s], first_stacked)
        else:
            moved, over_x[s] = together(moved, over_x[s])
        line.append(moved)
    mine = assemble(line + over_x, jnp.arange(2 * n_seq, dtype=jnp.int32))
    theirs = dp_swap(mine, 1)
    all_places = slots_of((0, 2, 1, 3))

    own_place = relative(lax.dynamic_slice_in_dim(positions, seq * rows, rows))
    own_segment = relative(lax.dynamic_slice_in_dim(segments, seq * rows, rows))
    cosine, sine = rope_tables(own_place, HEAD_DIM)
    cosine = jnp.concatenate([cosine, cosine], axis=1)
    sine = jnp.concatenate([-sine, sine], axis=1)
    bias = jnp.concatenate([query_bias, key_bias, value_bias]).astype(F32)
    queries, own_kv, first_rounded, attention_weights = project(
        mine, theirs, all_places, inputs, gain_first, bias, cosine, sine, q_width, kv_width
    )
    qkv_end = q_width + 2 * kv_width
    attention_weights = attention_weights.reshape(width, qkv_end + q_width)
    qkv_full, out_full = attention_weights[:, :qkv_end], attention_weights[:, qkv_end:]
    group_kv = [own_kv] + [z_shift(own_kv, s) for s in range(1, n_seq)]
    second_parts = spread([after(part, own_kv) for part in second_parts])
    *group_kv, cot_own, second_parts = together(*group_kv, cot_own, second_parts)
    second_stacked = stack_units(second_parts)
    second_units = lax.all_gather(second_stacked, "seq", axis=0, tiled=True)
    cot_x = dp_swap(cot_own, 2)
    group_kv = jnp.concatenate(group_kv, axis=0)
    keys, values = group_kv[:, :kv_width], group_kv[:, kv_width:]

    def key_rows(vector):
        taken = jnp.take(vector.reshape(blocks, rows), seq_places, axis=0)
        return relative(taken.T).T

    seg_k, pos_k = key_rows(segments), key_rows(positions)
    seen = pair_mask(
        own_segment[None, :, None], own_place[None, :, None], seg_k[:, None, :], pos_k[:, None, :]
    )
    flags = (jnp.any(seen, axis=(1, 2)).astype(jnp.int32) + jnp.all(seen, axis=(1, 2))).astype(
        jnp.int32
    )
    pairs = (
        own_segment[:, None], own_place[:, None], seg_k[:, None, :], pos_k[:, None, :], flags,
    )
    attended, lse = attend(queries, keys, values, *pairs)
    def reduce_halves(part):
        return part[:half] + y_swap(part[half:].astype(BF16)).astype(F32)

    inputs_half = inputs[:half].astype(F32)
    out_theirs = y_swap(right_product(attended[half:], out_full).astype(BF16))
    out_mine = right_product(attended[:half], out_full)
    out_theirs, out_mine, cot_x = together(out_theirs, out_mine, cot_x)
    cot_pieces = [cot_own, cot_x, dp_swap(cot_own, 1), dp_swap(cot_x, 1)]
    cots = assemble(cot_pieces, jnp.arange(4, dtype=jnp.int32)).reshape(-1, width)
    residual = inputs_half + out_mine + out_theirs.astype(F32)
    second_inverse = inverse_rms(residual)
    second_normed = residual * second_inverse
    second_rounded = (second_normed * gain_second).astype(BF16)

    gathered, (cots,) = plane_gather(second_rounded, cots)
    tokens = assemble(gathered, jnp.arange(len(gathered), dtype=jnp.int32)).reshape(-1, width)

    kept, *far = feed(tokens, cots, first_units, 1, None, None)
    kept, *near = feed(tokens, cots, first_units, 0, kept, None)
    first_gradient = unit_gradients(tokens, cots, kept)
    second_weights = after(second_units, first_gradient)
    second_kept, back_far, out_far = feed(tokens, cots, second_weights, 1, None, far)
    second_kept, back_near, out_near = feed(
        tokens, cots, second_weights, 0, second_kept, near
    )
    first_share = lax.psum_scatter(first_gradient, "seq", scatter_dimension=0, tiled=True)
    flops = 2 * tokens.size * cut.width[1]
    cost = pl.CostEstimate(flops=flops, bytes_accessed=0, transcendentals=0)

    def second_gradient(which, operand):
        return unit_gradients(tokens, cots, after(second_kept, operand), (which,), cost)

    def sum_along_seq(gradient):
        return lax.psum_scatter(gradient, "seq", scatter_dimension=0, tiled=True)

    back = PlaneScatter(*reversed(together(dp_swap(back_far, 1), back_near)))
    corner = back.corner()
    *corners, down_gradient = together(
        dp_swap(corner[0], 2), y_swap(corner[1]), second_gradient(2, corner[0])
    )
    down_share = sum_along_seq(down_gradient)
    sides = back.sides(*corners)
    *over, gate_gradient, first_share = together(
        dp_swap(sides[0], 2), y_swap(sides[1]), second_gradient(0, sides[0]), first_share
    )
    gate_share = sum_along_seq(gate_gradient)
    second_back = back.home(*over)

    residual_inner, second_gain_term = norm_backward(
        second_back, second_normed, second_inverse, gain_second
    )
    residual_back = cot_own[:half].astype(F32) + residual_inner
    back_half = residual_back.astype(BF16)
    back_other, out_core, up_gradient, down_share = together(
        y_swap(back_half), dp_swap(after(out_far, back_half), 1), second_gradient(1, back_half),
        down_share,
    )
    down = PlaneScatter(out_near, out_core)
    attended_back, attention_back = d_o_of(
        back_half, back_other, attention_weights, qkv_end, q_width
    )

    take = lax.dynamic_index_in_dim
    core, x = dp % 2, dp // 2

    def halves_of(left, right):
        return gradient_halves(left, right, core.astype(jnp.int32)[None], n_seq, share)

    def x_halves(own, over_core):
        parts = own.astype(F32) + over_core.astype(F32)
        parts = parts.reshape(n_seq, n_dp // 2, share, own.shape[2])
        return take(parts, x, 1, keepdims=False), take(parts, 1 - x, 1, keepdims=False).astype(BF16)

    def place_of(parts, s):
        return take(parts, seq_places[s % n_seq], 0, keepdims=False)

    def exchange_units(mine):
        mine = mine.reshape(n_dp, share, mine.shape[1])
        pieces = []
        for k in range(n_dp):
            piece = take(mine, dp_slots[k], 0, keepdims=False)
            pieces.append(dp_swap(piece, k) if k else piece)
        return pieces

    first_pieces = exchange_units(after(first_share, back_other))
    out_own, sent = halves_of(attention_back, attended)
    out_over_core = dp_swap(sent, 1)
    query_linear_back, kv_parts = attend_back(
        queries, keys, values, attended_back, lse, cosine, sine, *pairs
    )
    corner = down.corner()
    query_linear_back, kv_parts, out_over_core, gate_share, *arrived = together(
        query_linear_back, kv_parts, out_over_core, gate_share,
        dp_swap(corner[0], 2), y_swap(corner[1]), *first_pieces,
    )
    corners, first_pieces = arrived[:2], arrived[2:]

    kv_moved = [z_shift(kv_parts[s * rows : (s + 1) * rows], -s) for s in range(1, n_seq)]
    out_own, sent = x_halves(out_own, out_over_core)
    out_over_x = dp_swap(sent, 2)
    query_own, query_sent = halves_of(first_rounded, query_linear_back)
    sides = down.sides(*corners)
    out_over_x, query_own, query_sent, up_gradient, *arrived = together(
        out_over_x, query_own, query_sent, up_gradient,
        dp_swap(sides[0], 2), y_swap(sides[1]), *kv_moved,
    )
    over, kv_moved = arrived[:2], arrived[2:]
    out_half = from_inner((residual + down.home(*over)).astype(BF16))
    out_rows = out_own + out_over_x.astype(F32)
    up_share = sum_along_seq(up_gradient)
    kv_back = kv_parts[:rows].astype(F32)
    for moved in kv_moved:
        kv_back = kv_back + moved.astype(F32)
    key_linear_back = rotate(
        kv_back[:, :kv_width], cosine[:, : HEAD_DIM // 2], -sine[:, HEAD_DIM // 2 :]
    )
    kv_linear_back = jnp.concatenate([key_linear_back, kv_back[:, kv_width:]], axis=1).astype(BF16)
    linear_back = jnp.concatenate([query_linear_back, kv_linear_back], axis=1)

    query_over_core = dp_swap(query_sent, 1)
    kv_own, sent = halves_of(first_rounded, kv_linear_back)
    kv_over_core = dp_swap(sent, 1)
    first_theirs = y_swap(right_product(linear_back[half:], qkv_full).astype(BF16))
    first_mine = right_product(linear_back[:half], qkv_full)
    bias_terms = jnp.sum(linear_back.astype(F32), axis=0)
    query_over_core, kv_over_core, out_half = together(query_over_core, kv_over_core, out_half)

    query_own, query_sent = x_halves(query_own, query_over_core)
    query_over_x = dp_swap(query_sent, 2)
    kv_own, sent = x_halves(kv_own, kv_over_core)
    kv_over_x = dp_swap(sent, 2)
    out_other = y_swap(out_half)
    query_over_x, kv_over_x, first_theirs, first_mine, bias_terms = together(
        query_over_x, kv_over_x, first_theirs, first_mine, bias_terms
    )
    large = jnp.concatenate([query_own + query_over_x.astype(F32), out_rows], axis=2)
    kv_rows = kv_own + kv_over_x.astype(F32)

    total = z_shift(place_of(large, 1).astype(BF16), 1)
    kv_total = z_shift(place_of(kv_rows, 1).astype(BF16), 1)
    first_back = first_mine + first_theirs.astype(F32)
    first_inverse = inverse_rms(inputs_half)
    input_inner, first_gain_term = norm_backward(
        first_back, inputs_half * first_inverse, first_inverse, gain_first
    )
    input_half = from_inner((residual_back + input_inner).astype(BF16))
    sums = jnp.concatenate([first_gain_term, second_gain_term, bias_terms])
    total, kv_total, sums, input_half, out_other = together(
        total, kv_total, sums, input_half, out_other
    )
    total = place_of(large, 2) + total.astype(F32)
    kv_total = place_of(kv_rows, 2) + kv_total.astype(F32)

    def shift_add(values, axis):
        size = lax.axis_size(axis)
        moved = [
            lax.ppermute(values, axis, [(i, (i + s) % size) for i in range(size)])
            for s in range(1, size)
        ]
        return functools.reduce(jnp.add, moved, values)

    input_other = y_swap(input_half)
    pieces = [exchange_units(share_of) for share_of in (down_share, gate_share)]
    for s in range(2, n_seq):
        total = z_shift(total.astype(BF16), 1)
        kv_total = z_shift(kv_total.astype(BF16), 1)
        if s == 2:
            sums = shift_add(sums, "dp")
            total, kv_total, sums, up_share, pieces[0] = together(
                total, kv_total, sums, up_share, pieces[0]
            )
        elif s == 3:
            sums = shift_add(sums, "seq")
            total, kv_total, sums, input_other, pieces[1] = together(
                total, kv_total, sums, input_other, pieces[1]
            )
        total = place_of(large, s + 1) + total.astype(F32)
        kv_total = place_of(kv_rows, s + 1) + kv_total.astype(F32)
    down_pieces, gate_pieces = pieces
    up_pieces = exchange_units(up_share)
    gain_terms = shift_add(sums[: 2 * width], "tensor")
    bias_terms = sums[2 * width :]
    input_gradient = relative(jnp.concatenate([input_half, input_other], axis=0))
    output = relative(jnp.concatenate([out_half, out_other], axis=0))
    large_share, kv_share = total, kv_total
    out_gradient = large_share[:, q_width:].T
    gate_gradient, up_gradient, down_gradient = lay_units(
        cut, first_pieces + gate_pieces + up_pieces + down_pieces, dp_owners
    )
    down_gradient = down_gradient.T
    return (
        output,
        input_gradient,
        vector_out(gain_terms[:width]),
        large_share[:, :q_width],
        bias_terms[:q_width],
        kv_share[:, :kv_width],
        bias_terms[q_width:kv_end],
        kv_share[:, kv_width:],
        bias_terms[kv_end:],
        out_gradient,
        vector_out(gain_terms[width:]),
        gate_gradient,
        up_gradient,
        down_gradient,
    )


def solution(mesh):
    tokens = P(("dp", "seq"), None)
    by_row = P(("dp", "seq"), "tensor")
    by_column = P("tensor", ("dp", "seq"))
    heads = P("tensor")
    in_specs = (
        tokens, tokens, P("dp"), P("dp"), P(), by_row, heads, by_row, heads, by_row, heads,
        by_column, P(), by_row, by_row, by_column,
    )
    out_specs = (
        tokens, tokens, P(), by_row, heads, by_row, heads, by_row, heads, by_column, P(),
        by_row, by_row, by_column,
    )
    return jax.shard_map(
        on_device, mesh=mesh, in_specs=in_specs, out_specs=out_specs, check_vma=False
    )
```

```python
import functools
import math

import jax
import jax.numpy as jnp
import numpy as np
from jax import lax
from jax.experimental import pallas as pl
from jax.experimental.pallas import tpu as pltpu
from jax.sharding import PartitionSpec as P

HEAD_DIM = 128
EPS = 1e-06
LOG_BASE = math.log(1000000.0)
NEG_FILL = -1e30
LOG2E = 1.0 / math.log(2.0)
MIB = 1024 * 1024
F32 = jnp.float32
BF16 = jnp.bfloat16
FREE = pl.CostEstimate(flops=0, bytes_accessed=0, transcendentals=0)


def product(left, right):
    return jnp.dot(left, right, preferred_element_type=F32)


def left_product(left, right):
    return lax.dot_general(left, right, (((0,), (0,)), ((), ())), preferred_element_type=F32)


def right_product(left, right):
    return lax.dot_general(left, right, (((1,), (1,)), ((), ())), preferred_element_type=F32)


def after(value, *others):
    return lax.optimization_barrier((value,) + others)[0]


def together(*values):
    return lax.optimization_barrier(values)


def dp_swap(value, flip):
    size = lax.axis_size("dp")
    return lax.ppermute(value, "dp", [(i, i ^ flip) for i in range(size)])


def y_swap(value):
    return lax.ppermute(value, "tensor", [(0, 1), (1, 0)])


def z_shift(value, step):
    size = lax.axis_size("seq")
    return lax.ppermute(value, "seq", [(i, (i + step) % size) for i in range(size)])


def assemble_kernel(count, place_ref, *refs):
    pieces, out_ref, sems = refs[:count], refs[count], refs[count + 1]
    copies = [
        pltpu.make_async_copy(piece, out_ref.at[place_ref[i]], sems.at[i])
        for i, piece in enumerate(pieces)
    ]
    for copy in copies:
        copy.start()
    for copy in copies:
        copy.wait()


def assemble(pieces, places):
    count = len(pieces)
    return pl.pallas_call(
        functools.partial(assemble_kernel, count),
        out_shape=jax.ShapeDtypeStruct((count,) + pieces[0].shape, pieces[0].dtype),
        in_specs=[pl.BlockSpec(memory_space=pltpu.SMEM)]
        + [pl.BlockSpec(memory_space=pl.ANY)] * count,
        out_specs=pl.BlockSpec(memory_space=pltpu.VMEM),
        scratch_shapes=[pltpu.SemaphoreType.DMA((count,))],
        compiler_params=pltpu.CompilerParams(vmem_limit_bytes=24 * MIB),
        cost_estimate=FREE,
    )(places, *pieces)


def pick_kernel(count, place_ref, *refs):
    stacks, outs = refs[:count], refs[count:]
    for i, out in enumerate(outs):
        at = 0
        for stack in stacks:
            wide = stack.shape[2]
            out[:, at : at + wide] = stack[place_ref[i]]
            at += wide


def pick_pieces(stacks, places):
    vmem = pl.BlockSpec(memory_space=pltpu.VMEM)
    slots, rows = stacks[0].shape[:2]
    columns = sum(stack.shape[2] for stack in stacks)
    return pl.pallas_call(
        functools.partial(pick_kernel, len(stacks)),
        out_shape=[jax.ShapeDtypeStruct((rows, columns), stacks[0].dtype)] * slots,
        in_specs=[pl.BlockSpec(memory_space=pltpu.SMEM)] + [vmem] * len(stacks),
        out_specs=[vmem] * slots,
        compiler_params=pltpu.CompilerParams(vmem_limit_bytes=24 * MIB),
        cost_estimate=FREE,
    )(places, *stacks)


SEGMENT_STEP = 1 << 16


def pair_mask(seg_q, pos_q, seg_k, pos_k):
    return ((seg_k == 0) | (seg_k == seg_q)) & (pos_k <= pos_q)


def block_mask(sq_ref, pq_ref, codes):
    segments = codes // SEGMENT_STEP
    return pair_mask(sq_ref[...], pq_ref[...], segments, codes - segments * SEGMENT_STEP)


def attend_kernel(
    rows, factor, flag_ref, q_ref, k_ref, v_ref, sq_ref, pq_ref, code_ref,
    o_ref, lse_ref, top_ref, sum_ref, acc_ref,
):
    blocks = k_ref.shape[0] // rows
    top_ref[...] = jnp.full_like(top_ref, NEG_FILL)
    sum_ref[...] = jnp.zeros_like(sum_ref)
    acc_ref[...] = jnp.zeros_like(acc_ref)
    q = q_ref[...]

    def block_step(j, masked):
        span = pl.ds(pl.multiple_of(j * rows, rows), rows)
        s = right_product(k_ref[span, :], q) * factor
        if masked:
            mask = block_mask(sq_ref, pq_ref, code_ref[j])
            s = jnp.where(mask, s, NEG_FILL)
        top = top_ref[...]
        new_top = jnp.maximum(top, jnp.max(s, axis=0, keepdims=True))
        e = jnp.exp2(s - new_top)
        if masked:
            e = jnp.where(mask, e, 0.0)
        shrink = jnp.exp2(top - new_top)
        top_ref[...] = new_top
        sum_ref[...] = sum_ref[...] * shrink + jnp.sum(e, axis=0, keepdims=True)
        acc_ref[...] = acc_ref[...] * shrink + left_product(v_ref[span, :], e.astype(BF16))

    def step(j, carry):
        @pl.when(flag_ref[j] == 2)
        def _():
            block_step(j, False)

        @pl.when(flag_ref[j] == 1)
        def _():
            block_step(j, True)

        return carry

    lax.fori_loop(0, blocks, step, 0)
    total = sum_ref[...]
    o_ref[...] = (acc_ref[...] / total).T.astype(o_ref.dtype)
    lse_ref[...] = (top_ref[...] + jnp.log2(total))[None]


def attend(q, keys, values, seg_q, pos_q, codes, flags):
    rows, width = q.shape
    heads = width // HEAD_DIM
    kv_heads = keys.shape[1] // HEAD_DIM
    repeat = heads // kv_heads
    length = keys.shape[0]
    blocks = length // rows
    whole = lambda *shape: pl.BlockSpec(shape, lambda h: (0,) * len(shape))
    return pl.pallas_call(
        functools.partial(attend_kernel, rows, HEAD_DIM ** (-0.5) * LOG2E),
        grid=(heads,),
        in_specs=[
            pl.BlockSpec(memory_space=pltpu.SMEM),
            pl.BlockSpec((rows, HEAD_DIM), lambda h: (0, h)),
            pl.BlockSpec((length, HEAD_DIM), lambda h: (0, h // repeat)),
            pl.BlockSpec((length, HEAD_DIM), lambda h: (0, h // repeat)),
            whole(1, rows),
            whole(1, rows),
            whole(blocks, rows, 1),
        ],
        out_specs=[
            pl.BlockSpec((rows, HEAD_DIM), lambda h: (0, h)),
            pl.BlockSpec((1, 1, rows), lambda h: (h, 0, 0)),
        ],
        out_shape=[
            jax.ShapeDtypeStruct((rows, width), BF16),
            jax.ShapeDtypeStruct((heads, 1, rows), F32),
        ],
        scratch_shapes=[
            pltpu.VMEM((1, rows), F32),
            pltpu.VMEM((1, rows), F32),
            pltpu.VMEM((HEAD_DIM, rows), F32),
        ],
        compiler_params=pltpu.CompilerParams(vmem_limit_bytes=40 * MIB),
        cost_estimate=FREE,
    )(flags, q, keys, values, seg_q, pos_q, codes)


def attend_back_kernel(
    rows, factor, scale, repeat, flag_ref, q_ref, k_ref, v_ref, do_ref, lse_ref, cos_ref, sin_ref,
    sq_ref, pq_ref, code_ref, dq_ref, dkv_ref, dk_acc, dv_acc, dq_acc, p_keep, dp_keep, delta_ref,
):
    head = pl.program_id(0)
    blocks = k_ref.shape[0] // rows

    @pl.when(lax.rem(head, repeat) == 0)
    def _():
        dk_acc[...] = jnp.zeros_like(dk_acc)
        dv_acc[...] = jnp.zeros_like(dv_acc)

    dq_acc[...] = jnp.zeros_like(dq_acc)
    delta_ref[...] = jnp.zeros_like(delta_ref)
    q = q_ref[...]
    d_o = do_ref[...]
    lse = lse_ref[0]

    def span_of(j):
        return pl.ds(pl.multiple_of(j * rows, rows), rows)

    def first_pass(j, masked):
        p = jnp.exp2(right_product(k_ref[span_of(j), :], q) * factor - lse)
        if masked:
            p = jnp.where(block_mask(sq_ref, pq_ref, code_ref[j]), p, 0.0)
        dp = right_product(v_ref[span_of(j), :], d_o)
        p_keep[j] = p
        dp_keep[j] = dp
        delta_ref[...] += jnp.sum(p * dp, axis=0, keepdims=True)

    def first_step(j, carry):
        @pl.when(flag_ref[j] == 2)
        def _():
            first_pass(j, False)

        @pl.when(flag_ref[j] == 1)
        def _():
            first_pass(j, True)

        return carry

    lax.fori_loop(0, blocks, first_step, 0)

    def second_step(j, carry):
        @pl.when(flag_ref[j] > 0)
        def _():
            p = p_keep[j]
            ds = (p * (dp_keep[j] - delta_ref[...])).astype(BF16)
            span = span_of(j)
            dv_acc[span, :] += product(p.astype(BF16), d_o)
            dk_acc[span, :] += product(ds, q)
            dq_acc[...] += left_product(k_ref[span, :], ds)

        return carry

    lax.fori_loop(0, blocks, second_step, 0)
    (turned,) = rope_lanes((dq_acc[...] * scale).T, cos_ref[...], -sin_ref[...])
    dq_ref[...] = turned.astype(dq_ref.dtype)

    @pl.when(lax.rem(head, repeat) == repeat - 1)
    def _():
        dkv_ref[:, :HEAD_DIM] = (dk_acc[...] * scale).astype(dkv_ref.dtype)
        dkv_ref[:, HEAD_DIM:] = dv_acc[...].astype(dkv_ref.dtype)


def attend_back(q, keys, values, d_o, lse, cosine, sine, seg_q, pos_q, codes, flags):
    rows, width = q.shape
    heads = width // HEAD_DIM
    kv_heads = keys.shape[1] // HEAD_DIM
    repeat = heads // kv_heads
    length = keys.shape[0]
    blocks = length // rows
    whole = lambda *shape: pl.BlockSpec(shape, lambda h: (0,) * len(shape))
    per_head = pl.BlockSpec((rows, HEAD_DIM), lambda h: (0, h))
    held = pl.BlockSpec(
        (length, HEAD_DIM), lambda h: (0, h // repeat), pipeline_mode=pl.Buffered(1)
    )
    return pl.pallas_call(
        functools.partial(
            attend_back_kernel, rows, HEAD_DIM ** (-0.5) * LOG2E, HEAD_DIM ** (-0.5), repeat
        ),
        grid=(heads,),
        in_specs=[
            pl.BlockSpec(memory_space=pltpu.SMEM),
            per_head,
            held,
            held,
            per_head,
            pl.BlockSpec((1, 1, rows), lambda h: (h, 0, 0)),
            whole(rows, HEAD_DIM),
            whole(rows, HEAD_DIM),
            whole(1, rows),
            whole(1, rows),
            whole(blocks, rows, 1),
        ],
        out_specs=[
            per_head,
            pl.BlockSpec(
                (length, 2 * HEAD_DIM), lambda h: (0, h // repeat), pipeline_mode=pl.Buffered(1)
            ),
        ],
        out_shape=[
            jax.ShapeDtypeStruct((rows, width), BF16),
            jax.ShapeDtypeStruct((length, 2 * keys.shape[1]), BF16),
        ],
        scratch_shapes=[
            pltpu.VMEM((length, HEAD_DIM), F32),
            pltpu.VMEM((length, HEAD_DIM), F32),
            pltpu.VMEM((HEAD_DIM, rows), F32),
            pltpu.VMEM((blocks, rows, rows), F32),
            pltpu.VMEM((blocks, rows, rows), F32),
            pltpu.VMEM((1, rows), F32),
        ],
        compiler_params=pltpu.CompilerParams(vmem_limit_bytes=58 * MIB),
        cost_estimate=FREE,
    )(flags, q, keys, values, d_o, lse, cosine, sine, seg_q, pos_q, codes)


def rope_tables(places, width):
    half = width // 2
    freq = jnp.exp(jnp.arange(half, dtype=F32) * (-2.0 * LOG_BASE / width))
    angle = places.astype(F32)[:, None] * freq[None, :]
    return (jnp.cos(angle), jnp.sin(angle))


def rotate(values, cosine, sine):
    half = HEAD_DIM // 2
    parts = []
    for at in range(0, values.shape[1], HEAD_DIM):
        first = values[:, at : at + half]
        second = values[:, at + half : at + HEAD_DIM]
        parts += [first * cosine - second * sine, second * cosine + first * sine]
    return jnp.concatenate(parts, axis=1)


def inverse_rms(values):
    return lax.rsqrt(jnp.mean(values * values, axis=-1, keepdims=True) + EPS)


def norm_backward(upstream, normed, inverse, gain):
    scaled = upstream * gain
    inner = inverse * (scaled - normed * jnp.mean(scaled * normed, axis=-1, keepdims=True))
    return (inner, jnp.sum(upstream * normed, axis=0))


def rope_lanes(values, cosine, sine):
    parts = []
    for at in range(0, values.shape[1], HEAD_DIM):
        head = values[:, at : at + HEAD_DIM]
        parts.append(head * cosine + pltpu.roll(head, HEAD_DIM // 2, 1) * sine)
    return parts


def project_kernel(
    count, q_width, kv_width, place_ref, mine_ref, theirs_ref,
    x_ref, gain_ref, bias_ref, cos_ref, sin_ref, q_ref, kv_ref, h_ref, w_ref, sems,
):
    copies = [
        pltpu.make_async_copy(stack.at[i], w_ref.at[place_ref[at + i]], sems.at[at + i])
        for at, stack in ((0, mine_ref), (count, theirs_ref))
        for i in range(count)
    ]
    for copy in copies:
        copy.start()
    x = x_ref[...].astype(F32)
    normed = x * lax.rsqrt(jnp.mean(x * x, axis=1, keepdims=True) + EPS)
    h = (normed * gain_ref[...]).astype(BF16)
    h_ref[...] = h
    for copy in copies:
        copy.wait()
    depth, columns = x.shape[1], bias_ref.shape[1]
    weights = w_ref[...].reshape(depth, w_ref.shape[2])
    linear = product(h, weights[:, :columns]) + bias_ref[...]
    turned = rope_lanes(linear[:, : q_width + kv_width], cos_ref[...], sin_ref[...])
    heads = q_width // HEAD_DIM
    for i, part in enumerate(turned):
        if i < heads:
            q_ref[:, i * HEAD_DIM : (i + 1) * HEAD_DIM] = part.astype(BF16)
        else:
            at = (i - heads) * HEAD_DIM
            kv_ref[:, at : at + HEAD_DIM] = part.astype(BF16)
    kv_ref[:, kv_width:] = linear[:, q_width + kv_width :].astype(BF16)


def project(mine, theirs, places, inputs, gain, bias, cosine, sine, q_width, kv_width):
    count = mine.shape[0]
    rows, depth = inputs.shape
    columns = bias.shape[0]
    vmem = pl.BlockSpec(memory_space=pltpu.VMEM)
    return pl.pallas_call(
        functools.partial(project_kernel, count, q_width, kv_width),
        out_shape=[
            jax.ShapeDtypeStruct((rows, q_width), BF16),
            jax.ShapeDtypeStruct((rows, 2 * kv_width), BF16),
            jax.ShapeDtypeStruct((rows, depth), BF16),
            jax.ShapeDtypeStruct((2 * count,) + mine.shape[1:], BF16),
        ],
        in_specs=[pl.BlockSpec(memory_space=pltpu.SMEM)]
        + [pl.BlockSpec(memory_space=pl.ANY)] * 2
        + [vmem] * 5,
        out_specs=[vmem] * 4,
        scratch_shapes=[pltpu.SemaphoreType.DMA((2 * count,))],
        compiler_params=pltpu.CompilerParams(vmem_limit_bytes=40 * MIB),
        cost_estimate=FREE,
    )(places, mine, theirs, inputs, gain[None, :], bias[None, :], cosine, sine)


class Cut:
    def __init__(self, total, n_dp):
        tiles = total // n_dp // 128
        first = max(tiles * 3 // 8, 1)
        self.total = total
        self.n_dp = n_dp
        self.main = (first * 128, (tiles - first) * 128)
        self.start = (0, n_dp * self.main[0])
        self.rest_at = n_dp * (self.main[0] + self.main[1])
        self.rest = (total - self.rest_at) // n_dp
        pad = -(-self.rest // 128) * 128
        self.width = (self.main[0], self.main[1] + pad)


def pick(values, index):
    result = values[0]
    for i in range(1, len(values)):
        result = jnp.where(index == i, values[i], result)
    return result


def cut_kernel(cut, place_ref, *refs):
    weights, outs = refs[:3], refs[3:]
    n_dp = cut.n_dp
    for part in range(2):
        main, width = cut.main[part], cut.width[part]
        for k in range(n_dp):
            owner = place_ref[k]
            out = outs[part * n_dp + k]
            for i, w in enumerate(weights):
                at = i * width
                low = pl.multiple_of(cut.start[part] + owner * main, 128)
                out[:, at : at + main] = w[:, pl.ds(low, main)]
                if part == 1 and cut.rest:
                    tail = w[:, cut.rest_at :]
                    rest = pick(
                        [tail[:, b * cut.rest : (b + 1) * cut.rest] for b in range(n_dp)], owner
                    )
                    fill = jnp.zeros((rest.shape[0], width - main - cut.rest), rest.dtype)
                    out[:, at + main : at + width] = jnp.concatenate([rest, fill], axis=1)


def cut_units(cut, weights, owners):
    rows = weights[0].shape[0]
    vmem = pl.BlockSpec(memory_space=pltpu.VMEM)
    outs = pl.pallas_call(
        functools.partial(cut_kernel, cut),
        out_shape=[
            jax.ShapeDtypeStruct((rows, 3 * cut.width[part]), BF16)
            for part in range(2)
            for _ in range(cut.n_dp)
        ],
        in_specs=[pl.BlockSpec(memory_space=pltpu.SMEM)] + [vmem] * 3,
        out_specs=[vmem] * (2 * cut.n_dp),
        compiler_params=pltpu.CompilerParams(vmem_limit_bytes=24 * MIB),
        cost_estimate=FREE,
    )(owners, *weights)
    return outs[: cut.n_dp], outs[cut.n_dp :]


def lay_kernel(cut, place_ref, *refs):
    n_dp = cut.n_dp
    firsts, ups = refs[:n_dp], refs[n_dp : 2 * n_dp]
    outs = refs[2 * n_dp :]
    down_at = 3 * cut.width[0]
    lasts = ((firsts, down_at + cut.width[1]), (ups, 0), (firsts, down_at))
    for i, out in enumerate(outs):
        last, last_at = lasts[i]
        for part, (pieces, at) in enumerate(((firsts, i * cut.width[0]), lasts[i])):
            main = cut.main[part]
            for k in range(n_dp):
                low = pl.multiple_of(cut.start[part] + place_ref[k] * main, 128)
                out[:, pl.ds(low, main)] = pieces[k][:, at : at + main].astype(F32)
        if cut.rest:
            tails = [
                piece[:, last_at + cut.main[1] : last_at + cut.width[1]].astype(F32)[:, : cut.rest]
                for piece in last
            ]
            laid = []
            for b in range(n_dp):
                laid.append(
                    functools.reduce(
                        lambda got, k: jnp.where(place_ref[k] == b, tails[k], got),
                        range(1, n_dp),
                        tails[0],
                    )
                )
            out[:, cut.rest_at :] = jnp.concatenate(laid, axis=1)


def lay_units(cut, pieces, owners):
    rows = pieces[0].shape[0]
    vmem = pl.BlockSpec(memory_space=pltpu.VMEM)
    return pl.pallas_call(
        functools.partial(lay_kernel, cut),
        out_shape=[jax.ShapeDtypeStruct((rows, cut.total), F32)] * 3,
        in_specs=[pl.BlockSpec(memory_space=pltpu.SMEM)] + [vmem] * len(pieces),
        out_specs=[vmem] * 3,
        compiler_params=pltpu.CompilerParams(vmem_limit_bytes=32 * MIB),
        cost_estimate=FREE,
    )(owners, *pieces)


def feed_kernel(count, sums, *refs):
    t_ref, c_ref, w_ref = refs[:3]
    p_ref, back_ref, out_ref = refs[-3:]
    gate_weight, up_weight, down_weight = (
        w_ref.at[:, i * count : (i + 1) * count] for i in range(3)
    )
    tokens = t_ref[...]
    gate = product(tokens, gate_weight[...])
    upper = product(tokens, up_weight[...])
    act_back = product(c_ref[...], down_weight[...])
    sigma = 1.0 / (1.0 + jnp.exp(-gate))
    swish = gate * sigma
    activated = (swish * upper).astype(BF16)
    gate_back = (act_back * upper * sigma * (1.0 + gate * (1.0 - sigma))).astype(BF16)
    upper_back = (act_back * swish).astype(BF16)
    for i, value in enumerate((gate_back, upper_back, activated)):
        p_ref[:, i * count : (i + 1) * count] = value
    back = right_product(gate_back, gate_weight[...]) + right_product(upper_back, up_weight[...])
    out = right_product(activated, down_weight[...])
    if sums:
        back = back + refs[3][...].astype(F32)
        out = out + refs[4][...].astype(F32)
    back_ref[...] = back.astype(back_ref.dtype)
    out_ref[...] = out.astype(out_ref.dtype)


def feed(tokens, cots, weights, side, kept, earlier):
    rows, width = tokens.shape
    columns = weights.shape[1]
    span = rows // 2
    tall = min(256, span)
    steps = span // tall
    block = lambda w: pl.BlockSpec((tall, w), lambda i: (side * steps + i, 0))
    near = pl.BlockSpec((tall, width), lambda i: (i, 0))
    operands = [tokens, cots, weights]
    in_specs = [
        block(width),
        block(width),
        pl.BlockSpec((width, columns), lambda i: (0, 0), pipeline_mode=pl.Buffered(1)),
    ]
    if earlier is not None:
        operands += list(earlier)
        in_specs += [near, near]
    aliases = {}
    if kept is not None:
        aliases = {len(operands): 0}
        operands.append(kept)
        in_specs.append(pl.BlockSpec(memory_space=pl.ANY))
    return pl.pallas_call(
        functools.partial(feed_kernel, columns // 3, earlier is not None),
        grid=(steps,),
        in_specs=in_specs,
        out_specs=[block(columns), near, near],
        out_shape=[
            jax.ShapeDtypeStruct((rows, columns), BF16),
            jax.ShapeDtypeStruct((span, width), BF16),
            jax.ShapeDtypeStruct((span, width), BF16),
        ],
        input_output_aliases=aliases,
        compiler_params=pltpu.CompilerParams(vmem_limit_bytes=56 * MIB),
        cost_estimate=FREE,
    )(*operands)


def one_grads_kernel(left_ref, p_ref, o_ref):
    o_ref[...] = left_product(left_ref[...], p_ref[...]).astype(BF16)


def grads_kernel(split, t_ref, c_ref, p_ref, o_ref):
    step = pl.program_id(0)

    @pl.when(step < split)
    def _():
        o_ref[...] = left_product(t_ref[...], p_ref[...]).astype(BF16)

    @pl.when(step >= split)
    def _():
        o_ref[...] = left_product(c_ref[...], p_ref[...]).astype(BF16)


def unit_gradients(tokens, cots, kept, which=(0, 1, 2), cost=FREE):
    rows, width = tokens.shape
    count = kept.shape[1] // 3
    wide = 384 if count % 384 == 0 else 128
    each = count // wide
    split = each * sum(i < 2 for i in which)
    first = which[0] * each
    held = pl.BlockSpec((rows, width), lambda i: (0, 0), pipeline_mode=pl.Buffered(1))
    kernel, lefts = functools.partial(grads_kernel, split), (tokens, cots)
    if len(which) == 1:
        kernel, lefts = one_grads_kernel, ((tokens, tokens, cots)[which[0]],)
    return pl.pallas_call(
        kernel,
        grid=(each * len(which),),
        in_specs=[held] * len(lefts) + [pl.BlockSpec((rows, wide), lambda i: (0, first + i))],
        out_specs=pl.BlockSpec((width, wide), lambda i: (0, i)),
        out_shape=jax.ShapeDtypeStruct((width, len(which) * count), BF16),
        compiler_params=pltpu.CompilerParams(vmem_limit_bytes=56 * MIB),
        cost_estimate=cost,
    )(*lefts, kept)


def d_o_kernel(own_ref, other_ref, w_ref, d_o_ref, rows_ref):
    half = own_ref.shape[0]
    weights = w_ref[...]
    d_o_ref[:half] = product(own_ref[...], weights).astype(BF16)
    d_o_ref[half:] = product(other_ref[...], weights).astype(BF16)
    rows_ref[:half] = own_ref[...]
    rows_ref[half:] = other_ref[...]


def d_o_of(own, other, weights, first, count):
    half, width = own.shape
    wide = math.gcd(first, count)
    whole = lambda *shape: pl.BlockSpec(shape, lambda i: (0, 0))
    return pl.pallas_call(
        d_o_kernel,
        grid=(count // wide,),
        in_specs=[
            whole(half, width),
            whole(half, width),
            pl.BlockSpec((width, wide), lambda i: (0, first // wide + i)),
        ],
        out_specs=[pl.BlockSpec((2 * half, wide), lambda i: (0, i)), whole(2 * half, width)],
        out_shape=[
            jax.ShapeDtypeStruct((2 * half, count), BF16),
            jax.ShapeDtypeStruct((2 * half, width), BF16),
        ],
        compiler_params=pltpu.CompilerParams(vmem_limit_bytes=32 * MIB),
        cost_estimate=FREE,
    )(own, other, weights)


def against_kernel(left_ref, right_ref, out_ref):
    out_ref[...] = right_product(left_ref[...], right_ref[...]).astype(out_ref.dtype)


def against(left, right, dtype):
    rows, depth = left.shape
    count = right.shape[0]
    wide = 512 if count % 512 == 0 else count
    return pl.pallas_call(
        against_kernel,
        grid=(count // wide,),
        in_specs=[
            pl.BlockSpec((rows, depth), lambda i: (0, 0)),
            pl.BlockSpec((wide, depth), lambda i: (i, 0)),
        ],
        out_specs=pl.BlockSpec((rows, wide), lambda i: (0, i)),
        out_shape=jax.ShapeDtypeStruct((rows, count), dtype),
        compiler_params=pltpu.CompilerParams(vmem_limit_bytes=32 * MIB),
        cost_estimate=FREE,
    )(left, right)


def halves_kernel(n_seq, share, core_ref, left_ref, right_ref, own_ref, sent_ref, keep_ref):
    keep_ref[...] = left_product(left_ref[...], right_ref[...]).astype(BF16)
    tall = own_ref.shape[1]
    for z in range(n_seq):
        for out, core in ((own_ref, core_ref[0]), (sent_ref, 1 - core_ref[0])):
            at = pl.multiple_of((z * 2 + core) * tall, share)
            out[z] = keep_ref[pl.ds(at, tall), :]


def gradient_halves(left, right, core, n_seq, share):
    width, columns = left.shape[1], right.shape[1]
    vmem = pl.BlockSpec(memory_space=pltpu.VMEM)
    half = jax.ShapeDtypeStruct((n_seq, width // (2 * n_seq), columns), BF16)
    return pl.pallas_call(
        functools.partial(halves_kernel, n_seq, share),
        out_shape=[half, half],
        in_specs=[pl.BlockSpec(memory_space=pltpu.SMEM), vmem, vmem],
        out_specs=[vmem, vmem],
        scratch_shapes=[pltpu.VMEM((width, columns), BF16)],
        compiler_params=pltpu.CompilerParams(vmem_limit_bytes=32 * MIB),
        cost_estimate=FREE,
    )(core, left, right)


def plane_gather(own, *others):
    cut = own.shape[0] // 2
    over_x, over_y, *others = together(dp_swap(own, 2), y_swap(own), *others)
    far_x = y_swap(over_x[:cut])
    far_y = dp_swap(over_y[cut:], 2)
    near = [own, over_y, over_x]
    across = [dp_swap(piece, 1) for piece in near]
    far_x, far_y, *across = together(far_x, far_y, *across)
    far = jnp.concatenate([far_x, far_y], axis=0)
    return near + [far] + across + [dp_swap(far, 1)], others


class PlaneScatter:
    def __init__(self, near, over_core):
        self.near, self.over_core = near, over_core
        self.t = near.shape[0] // 4
        self.cut = self.t // 2

    def summed(self, low, high):
        return self.near[low:high].astype(F32) + self.over_core[low:high].astype(F32)

    def corner(self):
        corner = self.summed(3 * self.t, 4 * self.t).astype(BF16)
        return corner[: self.cut], corner[self.cut :]

    def sides(self, corner_x, corner_y):
        t, cut = self.t, self.cut
        to_y = [self.summed(t, t + cut) + corner_x.astype(F32), self.summed(t + cut, 2 * t)]
        to_x = [
            self.summed(2 * t, 2 * t + cut),
            self.summed(2 * t + cut, 3 * t) + corner_y.astype(F32),
        ]
        return tuple(jnp.concatenate(part, axis=0).astype(BF16) for part in (to_x, to_y))

    def sides_of(self, corner_x):
        t = self.t
        to_y = self.summed(t, 2 * t) + corner_x.astype(F32)
        return self.summed(2 * t, 3 * t).astype(BF16), to_y.astype(BF16)

    def home(self, over_x, over_y):
        return self.summed(0, self.t) + over_x.astype(F32) + over_y.astype(F32)


def on_device(
    hidden, cotangent, segments, positions, first_gain,
    query_weight, query_bias, key_weight, key_bias, value_weight, value_bias,
    out_weight, second_gain, gate_weight, up_weight, down_weight,
):
    n_dp, n_seq = lax.axis_size("dp"), lax.axis_size("seq")
    dp, seq, tensor = (lax.axis_index(a) for a in ("dp", "seq", "tensor"))
    rows, width = hidden.shape
    half = rows // 2
    share = query_weight.shape[0]
    group = segments.shape[0]
    blocks = group // rows
    q_width, kv_width = query_weight.shape[1], key_weight.shape[1]
    kv_end = q_width + kv_width
    def slots_of(owners):
        return (owners % 2) * (n_dp // 2) + owners // 2

    dp_owners = dp ^ jnp.arange(n_dp, dtype=jnp.int32)
    dp_slots = slots_of(dp_owners)
    seq_places = (seq - jnp.arange(n_seq, dtype=jnp.int32) + n_seq) % n_seq
    flips = jnp.repeat(np.array([0, 2, 1, 3], np.int32), n_seq)
    all_places = jnp.tile(seq_places, 4) * n_dp + slots_of(dp ^ flips)
    core, x = (dp % 2).astype(jnp.int32), (dp // 2).astype(jnp.int32)
    dp_owners, dp_slots, seq_places, all_places, core_place, core, x, *scalars = together(
        dp_owners, dp_slots, seq_places, all_places, core[None], core, x,
        *[seq_places[s] for s in range(n_seq)],
    )

    def take(values, index, axis):
        return lax.dynamic_index_in_dim(
            values, index, axis, keepdims=False, allow_negative_indices=False
        )


    def vector_in(vector):
        parts = vector.reshape(n_dp // 2, 2, n_seq, share)
        return parts.transpose(2, 1, 0, 3).reshape(width).astype(F32)

    def vector_out(vector):
        parts = vector.reshape(n_seq, 2, n_dp // 2, share)
        return parts.transpose(2, 1, 0, 3).reshape(width)

    index = jnp.arange(width, dtype=jnp.int32)
    owner, place = index // (share * n_seq), index // share % n_seq
    slot = owner % 2 * (n_dp // 2) + owner // 2
    inner_of = (place * n_dp + slot) * share + index % share
    (shuffle,) = together((inner_of[:, None] == index[None, :]).astype(BF16))

    def relative(values):
        turned = jnp.concatenate([values[half:], values[:half]], axis=0)
        return jnp.where(tensor == 0, values, turned)

    def to_inner(values):
        return product(relative(values), shuffle).astype(BF16)

    def from_inner(values):
        return against(values, shuffle, BF16)

    gain_first, gain_second = vector_in(first_gain), vector_in(second_gain)

    cut = Cut(gate_weight.shape[1], n_dp)

    def spread(pieces):
        return [dp_swap(piece, k) if k else piece for k, piece in enumerate(pieces)]

    def stack_units(pieces):
        return assemble(pieces, dp_slots).reshape(n_dp * share, pieces[0].shape[1])

    own_place = relative(take(positions.reshape(blocks, rows), scalars[0], 0))
    own_segment = relative(take(segments.reshape(blocks, rows), scalars[0], 0))
    def tables(places):
        cosine, sine = rope_tables(places, HEAD_DIM)
        return (
            jnp.concatenate([cosine, cosine], axis=1), jnp.concatenate([-sine, sine], axis=1)
        )


    line = [jnp.concatenate([query_weight, key_weight, value_weight, out_weight.T], axis=1)]
    over_x = []
    for s in range(n_seq):
        over_x.append(dp_swap(line[s], 2))
        if s + 1 == n_seq:
            cot_own = to_inner(after(cotangent, line[s]))
            over_x[s], cot_own = together(over_x[s], cot_own)
            break
        moved = z_shift(line[s], 1)
        if s == 0:
            first_parts, second_parts = cut_units(
                cut, (gate_weight, up_weight, down_weight.T), dp_owners
            )
            moved, over_x[s], *parts = together(moved, over_x[s], *first_parts, *second_parts)
            first_parts, second_parts = parts[:n_dp], parts[n_dp:]
        elif s == 1:
            first_parts = spread(first_parts)
            inputs = to_inner(after(hidden, line[s]))
            cosine, sine = tables(after(own_place, line[s]))
            moved, over_x[s], inputs, cosine, sine, *first_parts = together(
                moved, over_x[s], inputs, cosine, sine, *first_parts
            )
        elif s == 2:
            first_stacked = stack_units(first_parts)
            first_units = lax.all_gather(first_stacked, "seq", axis=0, tiled=True)
            moved, over_x[s], first_stacked = together(moved, over_x[s], first_stacked)
        else:
            moved, over_x[s] = together(moved, over_x[s])
        line.append(moved)
    mine = assemble(line + over_x, jnp.arange(2 * n_seq, dtype=jnp.int32))
    theirs = dp_swap(mine, 1)

    bias = jnp.concatenate([query_bias, key_bias, value_bias]).astype(F32)
    queries, own_kv, first_rounded, attention_weights = project(
        mine, theirs, all_places, inputs, gain_first, bias, cosine, sine, q_width, kv_width
    )
    qkv_end = q_width + 2 * kv_width
    attention_weights = attention_weights.reshape(width, qkv_end + q_width)
    qkv_full, out_full = attention_weights[:, :qkv_end], attention_weights[:, qkv_end:]
    group_kv = [own_kv] + [z_shift(own_kv, s) for s in range(1, n_seq)]
    second_parts = spread([after(part, own_kv) for part in second_parts])
    *group_kv, cot_own, second_parts = together(*group_kv, cot_own, second_parts)
    second_stacked = stack_units(second_parts)
    second_units = lax.all_gather(second_stacked, "seq", axis=0, tiled=True)
    cot_x = dp_swap(cot_own, 2)
    group_kv = jnp.concatenate(group_kv, axis=0)
    keys, values = group_kv[:, :kv_width], group_kv[:, kv_width:]

    def key_rows(vector):
        taken = jnp.take(vector.reshape(blocks, rows), seq_places, axis=0)
        return relative(taken.T).T

    seg_k, pos_k = (key_rows(after(v, own_kv)) for v in (segments, positions))
    seen = pair_mask(
        own_segment[None, :, None], own_place[None, :, None], seg_k[:, None, :], pos_k[:, None, :]
    )
    flags = (jnp.any(seen, axis=(1, 2)).astype(jnp.int32) + jnp.all(seen, axis=(1, 2))).astype(
        jnp.int32
    )
    codes = (seg_k * SEGMENT_STEP + pos_k)[:, :, None]
    pairs = (own_segment[None, :], own_place[None, :], codes, flags)
    attended, lse = attend(queries, keys, values, *pairs)
    def reduce_halves(part):
        return part[:half] + y_swap(part[half:].astype(BF16)).astype(F32)

    inputs_half = inputs[:half].astype(F32)
    out_theirs = y_swap(right_product(attended[half:], out_full).astype(BF16))
    out_mine = right_product(attended[:half], out_full)
    out_theirs, out_mine, cot_x = together(out_theirs, out_mine, cot_x)
    cot_pieces = [cot_own, cot_x, dp_swap(cot_own, 1), dp_swap(cot_x, 1)]
    cots = assemble(cot_pieces, jnp.arange(4, dtype=jnp.int32)).reshape(-1, width)
    residual = inputs_half + out_mine + out_theirs.astype(F32)
    second_inverse = inverse_rms(residual)
    second_normed = residual * second_inverse
    second_rounded = (second_normed * gain_second).astype(BF16)

    gathered, (cots,) = plane_gather(second_rounded, cots)
    tokens = assemble(gathered, jnp.arange(len(gathered), dtype=jnp.int32)).reshape(-1, width)

    kept, *far = feed(tokens, cots, first_units, 1, None, None)
    kept, *near = feed(tokens, cots, first_units, 0, kept, None)
    first_gradient = unit_gradients(tokens, cots, kept)
    second_weights = after(second_units, first_gradient)
    second_kept, back_far, out_far = feed(tokens, cots, second_weights, 1, None, far)
    second_kept, back_near, out_near = feed(
        tokens, cots, second_weights, 0, second_kept, near
    )
    first_share = lax.psum_scatter(first_gradient, "seq", scatter_dimension=0, tiled=True)
    flops = 2 * tokens.size * cut.width[1]
    cost = pl.CostEstimate(flops=flops, bytes_accessed=0, transcendentals=0)

    def second_gradient(which, operand):
        return unit_gradients(tokens, cots, after(second_kept, operand), (which,), cost)

    def sum_along_seq(gradient):
        return lax.psum_scatter(gradient, "seq", scatter_dimension=0, tiled=True)

    back = PlaneScatter(*reversed(together(dp_swap(back_far, 1), back_near)))
    corner = back.corner()
    *corners, down_gradient = together(
        dp_swap(corner[0], 2), y_swap(corner[1]), second_gradient(2, corner[0])
    )
    down_share = sum_along_seq(down_gradient)
    sides = back.sides(*corners)
    *over, gate_gradient, first_share = together(
        dp_swap(sides[0], 2), y_swap(sides[1]), second_gradient(0, sides[0]), first_share
    )
    gate_share = sum_along_seq(gate_gradient)
    second_back = back.home(*over)

    residual_inner, second_gain_term = norm_backward(
        second_back, second_normed, second_inverse, gain_second
    )
    residual_back = cot_own[:half].astype(F32) + residual_inner
    back_half = residual_back.astype(BF16)
    def exchange_units(*shares):
        stacks = [mine.reshape(n_dp, share, mine.shape[1]) for mine in shares]
        pieces = pick_pieces(stacks, dp_slots)
        return [dp_swap(piece, k) if k else piece for k, piece in enumerate(pieces)]

    out_core = dp_swap(after(out_far, back_half), 1)
    corner = PlaneScatter(out_near, out_core).summed(3 * half, 4 * half).astype(BF16)
    back_other, out_core, up_gradient, down_share, corner_x = together(
        y_swap(back_half), out_core, second_gradient(1, back_half), down_share, dp_swap(corner, 2)
    )
    down = PlaneScatter(out_near, out_core)
    attended_back, attention_back = d_o_of(
        back_half, back_other, attention_weights, qkv_end, q_width
    )

    def halves_of(left, right):
        return gradient_halves(left, right, core_place, n_seq, share)

    def x_halves(own, over_core):
        parts = own.astype(F32) + over_core.astype(F32)
        parts = parts.reshape(n_seq, n_dp // 2, share, own.shape[2])
        return take(parts, x, 1), take(parts, 1 - x, 1).astype(BF16)

    def place_of(parts, s):
        return take(parts, scalars[s % n_seq], 0)

    out_own, sent = halves_of(attention_back, attended)
    sides = down.sides_of(corner_x)
    over = dp_swap(sides[0], 2), y_swap(sides[1])
    (out_over_core,) = together(dp_swap(sent, 1))
    out_own, sent = x_halves(out_own, out_over_core)
    out_over_x = dp_swap(sent, 2)
    attended_back, out_sent = together(attended_back, sent)
    query_linear_back, kv_parts = attend_back(
        queries, keys, values, attended_back, lse, cosine, sine, *pairs
    )
    query_linear_back, kv_parts, out_over_x, *over = together(
        query_linear_back, kv_parts, out_over_x, *over
    )

    kv_moved = [z_shift(kv_parts[s * rows : (s + 1) * rows], -s) for s in range(1, n_seq)]
    query_own, query_sent = halves_of(first_rounded, query_linear_back)
    query_own, gate_share, query_over_core, *kv_moved = together(
        query_own, gate_share, dp_swap(query_sent, 1), *kv_moved
    )
    *kv_moved, up_gradient = together(*kv_moved, up_gradient)
    out_rows = out_own + out_over_x.astype(F32)
    up_share = sum_along_seq(up_gradient)
    kv_back = kv_parts[:rows].astype(F32)
    for moved in kv_moved:
        kv_back = kv_back + moved.astype(F32)
    key_linear_back = rotate(
        kv_back[:, :kv_width], cosine[:, : HEAD_DIM // 2], -sine[:, HEAD_DIM // 2 :]
    )
    kv_linear_back = jnp.concatenate([key_linear_back, kv_back[:, kv_width:]], axis=1).astype(BF16)
    linear_back = jnp.concatenate([query_linear_back, kv_linear_back], axis=1)

    query_own, sent = x_halves(query_own, query_over_core)
    query_over_x = dp_swap(sent, 2)
    kv_own, sent = halves_of(first_rounded, kv_linear_back)
    kv_over_core = dp_swap(sent, 1)
    first_theirs = y_swap(against(linear_back[half:], attention_weights, BF16))
    first_mine = against(linear_back[:half], attention_weights, F32)
    query_over_x, kv_over_core = together(query_over_x, kv_over_core)
    large = jnp.concatenate([query_own + query_over_x.astype(F32), out_rows], axis=2)

    kv_own, sent = x_halves(kv_own, kv_over_core)
    kv_over_x = dp_swap(sent, 2)
    total = z_shift(place_of(large, 1).astype(BF16), 1)
    out_half = from_inner((residual + down.home(*over)).astype(BF16))
    total, kv_over_x, first_theirs, first_mine, out_half = together(
        total, kv_over_x, first_theirs, first_mine, out_half
    )
    kv_rows = kv_own + kv_over_x.astype(F32)
    total = place_of(large, 2) + total.astype(F32)

    out_other = y_swap(out_half)
    first_back = first_mine + first_theirs.astype(F32)
    first_inverse = inverse_rms(inputs_half)
    input_inner, first_gain_term = norm_backward(
        first_back, inputs_half * first_inverse, first_inverse, gain_first
    )
    input_half = (residual_back + input_inner).astype(BF16)
    bias_terms = jnp.sum(linear_back.astype(F32), axis=0)
    sums = jnp.concatenate([first_gain_term, second_gain_term, bias_terms])

    def shift_add(values, axis):
        size = lax.axis_size(axis)
        moved = [
            lax.ppermute(values, axis, [(i, (i + s) % size) for i in range(size)])
            for s in range(1, size)
        ]
        return functools.reduce(jnp.add, moved, values)

    input_half = from_inner(input_half)
    input_other = y_swap(input_half)
    pieces = exchange_units(first_share, down_share, gate_share)
    kv_moved = [z_shift(place_of(kv_rows, s).astype(BF16), -s) for s in range(1, n_seq)]
    for s in range(2, n_seq):
        total = z_shift(total.astype(BF16), 1)
        if s == 2:
            total, sums, out_other, up_share, *arrived = together(
                total, sums, out_other, up_share, *kv_moved, *pieces
            )
            kv_moved, pieces = arrived[: n_seq - 1], arrived[n_seq - 1 :]
            sums = shift_add(sums, "dp")
            up_pieces = exchange_units(up_share)
        elif s == 3:
            total, sums, input_other, *up_pieces = together(
                total, sums, input_other, *up_pieces
            )
            sums = shift_add(sums, "seq")
        total = place_of(large, s + 1) + total.astype(F32)
    kv_share = functools.reduce(
        lambda a, b: a + b.astype(F32), kv_moved, place_of(kv_rows, 0)
    )
    gain_terms = shift_add(sums[: 2 * width], "tensor")
    bias_terms = sums[2 * width :]
    input_gradient = relative(jnp.concatenate([input_half, input_other], axis=0))
    output = relative(jnp.concatenate([out_half, out_other], axis=0))
    large_share = total
    out_gradient = large_share[:, q_width:].T
    gate_gradient, up_gradient, down_gradient = lay_units(
        cut, pieces + up_pieces, dp_owners
    )
    down_gradient = down_gradient.T
    return (
        output,
        input_gradient,
        vector_out(gain_terms[:width]),
        large_share[:, :q_width],
        bias_terms[:q_width],
        kv_share[:, :kv_width],
        bias_terms[q_width:kv_end],
        kv_share[:, kv_width:],
        bias_terms[kv_end:],
        out_gradient,
        vector_out(gain_terms[width:]),
        gate_gradient,
        up_gradient,
        down_gradient,
    )


def solution(mesh):
    tokens = P(("dp", "seq"), None)
    by_row = P(("dp", "seq"), "tensor")
    by_column = P("tensor", ("dp", "seq"))
    heads = P("tensor")
    in_specs = (
        tokens, tokens, P("dp"), P("dp"), P(), by_row, heads, by_row, heads, by_row, heads,
        by_column, P(), by_row, by_row, by_column,
    )
    out_specs = (
        tokens, tokens, P(), by_row, heads, by_row, heads, by_row, heads, by_column, P(),
        by_row, by_row, by_column,
    )
    return jax.shard_map(
        on_device, mesh=mesh, in_specs=in_specs, out_specs=out_specs, check_vma=False
    )
```

```python
import functools
import math

import jax
import jax.numpy as jnp
import numpy as np
from jax import lax
from jax.experimental import pallas as pl
from jax.experimental.pallas import tpu as pltpu
from jax.sharding import PartitionSpec as P

HEAD_DIM = 128
EPS = 1e-06
LOG_BASE = math.log(1000000.0)
NEG_FILL = -1e30
LOG2E = 1.0 / math.log(2.0)
MIB = 1024 * 1024
F32 = jnp.float32
BF16 = jnp.bfloat16
FREE = pl.CostEstimate(flops=0, bytes_accessed=0, transcendentals=0)


def product(left, right):
    return jnp.dot(left, right, preferred_element_type=F32)


def left_product(left, right):
    return lax.dot_general(left, right, (((0,), (0,)), ((), ())), preferred_element_type=F32)


def right_product(left, right):
    return lax.dot_general(left, right, (((1,), (1,)), ((), ())), preferred_element_type=F32)


def after(value, *others):
    return lax.optimization_barrier((value,) + others)[0]


def together(*values):
    return lax.optimization_barrier(values)


def dp_swap(value, flip):
    size = lax.axis_size("dp")
    return lax.ppermute(value, "dp", [(i, i ^ flip) for i in range(size)])


def y_swap(value):
    return lax.ppermute(value, "tensor", [(0, 1), (1, 0)])


def z_shift(value, step):
    size = lax.axis_size("seq")
    return lax.ppermute(value, "seq", [(i, (i + step) % size) for i in range(size)])


def assemble_kernel(count, place_ref, *refs):
    pieces, out_ref, sems = refs[:count], refs[count], refs[count + 1]
    copies = [
        pltpu.make_async_copy(piece, out_ref.at[place_ref[i]], sems.at[i])
        for i, piece in enumerate(pieces)
    ]
    for copy in copies:
        copy.start()
    for copy in copies:
        copy.wait()


def assemble(pieces, places):
    count = len(pieces)
    return pl.pallas_call(
        functools.partial(assemble_kernel, count),
        out_shape=jax.ShapeDtypeStruct((count,) + pieces[0].shape, pieces[0].dtype),
        in_specs=[pl.BlockSpec(memory_space=pltpu.SMEM)]
        + [pl.BlockSpec(memory_space=pl.ANY)] * count,
        out_specs=pl.BlockSpec(memory_space=pltpu.VMEM),
        scratch_shapes=[pltpu.SemaphoreType.DMA((count,))],
        compiler_params=pltpu.CompilerParams(vmem_limit_bytes=24 * MIB),
        cost_estimate=FREE,
    )(places, *pieces)


def join_kernel(place_ref, own_ref, other_ref, out_ref):
    half = own_ref.shape[0]
    for ref, place in ((own_ref, place_ref[0]), (other_ref, 1 - place_ref[0])):
        out_ref[pl.ds(pl.multiple_of(place * half, half), half), :] = ref[...]


def join_halves(own, other, place):
    vmem = pl.BlockSpec(memory_space=pltpu.VMEM)
    return pl.pallas_call(
        join_kernel,
        out_shape=jax.ShapeDtypeStruct((2 * own.shape[0], own.shape[1]), own.dtype),
        in_specs=[pl.BlockSpec(memory_space=pltpu.SMEM), vmem, vmem],
        out_specs=vmem,
        compiler_params=pltpu.CompilerParams(vmem_limit_bytes=24 * MIB),
        cost_estimate=FREE,
    )(place, own, other)


def pick_kernel(count, place_ref, *refs):
    stacks, outs = refs[:count], refs[count:]
    for i, out in enumerate(outs):
        at = 0
        for stack in stacks:
            wide = stack.shape[2]
            out[:, at : at + wide] = stack[place_ref[i]]
            at += wide


def pick_pieces(stacks, places):
    vmem = pl.BlockSpec(memory_space=pltpu.VMEM)
    slots, rows = stacks[0].shape[:2]
    columns = sum(stack.shape[2] for stack in stacks)
    return pl.pallas_call(
        functools.partial(pick_kernel, len(stacks)),
        out_shape=[jax.ShapeDtypeStruct((rows, columns), stacks[0].dtype)] * slots,
        in_specs=[pl.BlockSpec(memory_space=pltpu.SMEM)] + [vmem] * len(stacks),
        out_specs=[vmem] * slots,
        compiler_params=pltpu.CompilerParams(vmem_limit_bytes=24 * MIB),
        cost_estimate=FREE,
    )(places, *stacks)


SEGMENT_STEP = 1 << 16


def pair_mask(seg_q, pos_q, seg_k, pos_k):
    return ((seg_k == 0) | (seg_k == seg_q)) & (pos_k <= pos_q)


def block_mask(sq_ref, pq_ref, codes):
    segments = codes // SEGMENT_STEP
    return pair_mask(sq_ref[...], pq_ref[...], segments, codes - segments * SEGMENT_STEP)


def attend_kernel(
    rows, factor, flag_ref, q_ref, k_ref, v_ref, sq_ref, pq_ref, code_ref,
    o_ref, lse_ref, top_ref, sum_ref, acc_ref,
):
    blocks = k_ref.shape[0] // rows
    top_ref[...] = jnp.full_like(top_ref, NEG_FILL)
    sum_ref[...] = jnp.zeros_like(sum_ref)
    acc_ref[...] = jnp.zeros_like(acc_ref)
    q = q_ref[...]

    def block_step(j, masked):
        span = pl.ds(pl.multiple_of(j * rows, rows), rows)
        s = right_product(k_ref[span, :], q) * factor
        if masked:
            mask = block_mask(sq_ref, pq_ref, code_ref[j])
            s = jnp.where(mask, s, NEG_FILL)
        top = top_ref[...]
        new_top = jnp.maximum(top, jnp.max(s, axis=0, keepdims=True))
        e = jnp.exp2(s - new_top)
        if masked:
            e = jnp.where(mask, e, 0.0)
        shrink = jnp.exp2(top - new_top)
        top_ref[...] = new_top
        sum_ref[...] = sum_ref[...] * shrink + jnp.sum(e, axis=0, keepdims=True)
        acc_ref[...] = acc_ref[...] * shrink + left_product(v_ref[span, :], e.astype(BF16))

    def step(j, carry):
        @pl.when(flag_ref[j] == 2)
        def _():
            block_step(j, False)

        @pl.when(flag_ref[j] == 1)
        def _():
            block_step(j, True)

        return carry

    lax.fori_loop(0, blocks, step, 0)
    total = sum_ref[...]
    o_ref[...] = (acc_ref[...] / total).T.astype(o_ref.dtype)
    lse_ref[...] = (top_ref[...] + jnp.log2(total))[None]


def attend(q, keys, values, seg_q, pos_q, codes, flags):
    rows, width = q.shape
    heads = width // HEAD_DIM
    kv_heads = keys.shape[1] // HEAD_DIM
    repeat = heads // kv_heads
    length = keys.shape[0]
    blocks = length // rows
    whole = lambda *shape: pl.BlockSpec(shape, lambda h: (0,) * len(shape))
    return pl.pallas_call(
        functools.partial(attend_kernel, rows, HEAD_DIM ** (-0.5) * LOG2E),
        grid=(heads,),
        in_specs=[
            pl.BlockSpec(memory_space=pltpu.SMEM),
            pl.BlockSpec((rows, HEAD_DIM), lambda h: (0, h)),
            pl.BlockSpec((length, HEAD_DIM), lambda h: (0, h // repeat)),
            pl.BlockSpec((length, HEAD_DIM), lambda h: (0, h // repeat)),
            whole(1, rows),
            whole(1, rows),
            whole(blocks, rows, 1),
        ],
        out_specs=[
            pl.BlockSpec((rows, HEAD_DIM), lambda h: (0, h)),
            pl.BlockSpec((1, 1, rows), lambda h: (h, 0, 0)),
        ],
        out_shape=[
            jax.ShapeDtypeStruct((rows, width), BF16),
            jax.ShapeDtypeStruct((heads, 1, rows), F32),
        ],
        scratch_shapes=[
            pltpu.VMEM((1, rows), F32),
            pltpu.VMEM((1, rows), F32),
            pltpu.VMEM((HEAD_DIM, rows), F32),
        ],
        compiler_params=pltpu.CompilerParams(vmem_limit_bytes=40 * MIB),
        cost_estimate=FREE,
    )(flags, q, keys, values, seg_q, pos_q, codes)


def attend_back_kernel(
    rows, factor, scale, repeat, flag_ref, q_ref, k_ref, v_ref, do_ref, lse_ref, cos_ref, sin_ref,
    sq_ref, pq_ref, code_ref, dq_ref, dkv_ref, dk_acc, dv_acc, dq_acc, p_keep, dp_keep, delta_ref,
):
    head = pl.program_id(0)
    blocks = k_ref.shape[0] // rows

    @pl.when(lax.rem(head, repeat) == 0)
    def _():
        dk_acc[...] = jnp.zeros_like(dk_acc)
        dv_acc[...] = jnp.zeros_like(dv_acc)

    dq_acc[...] = jnp.zeros_like(dq_acc)
    delta_ref[...] = jnp.zeros_like(delta_ref)
    q = q_ref[...]
    d_o = do_ref[...]
    lse = lse_ref[0]

    def span_of(j):
        return pl.ds(pl.multiple_of(j * rows, rows), rows)

    def first_pass(j, masked):
        p = jnp.exp2(right_product(k_ref[span_of(j), :], q) * factor - lse)
        if masked:
            p = jnp.where(block_mask(sq_ref, pq_ref, code_ref[j]), p, 0.0)
        dp = right_product(v_ref[span_of(j), :], d_o)
        p_keep[j] = p
        dp_keep[j] = dp
        delta_ref[...] += jnp.sum(p * dp, axis=0, keepdims=True)

    def first_step(j, carry):
        @pl.when(flag_ref[j] == 2)
        def _():
            first_pass(j, False)

        @pl.when(flag_ref[j] == 1)
        def _():
            first_pass(j, True)

        return carry

    lax.fori_loop(0, blocks, first_step, 0)

    def second_step(j, carry):
        @pl.when(flag_ref[j] > 0)
        def _():
            p = p_keep[j]
            ds = (p * (dp_keep[j] - delta_ref[...])).astype(BF16)
            span = span_of(j)
            dv_acc[span, :] += product(p.astype(BF16), d_o)
            dk_acc[span, :] += product(ds, q)
            dq_acc[...] += left_product(k_ref[span, :], ds)

        return carry

    lax.fori_loop(0, blocks, second_step, 0)
    (turned,) = rope_lanes((dq_acc[...] * scale).T, cos_ref[...], -sin_ref[...])
    dq_ref[...] = turned.astype(dq_ref.dtype)

    @pl.when(lax.rem(head, repeat) == repeat - 1)
    def _():
        dkv_ref[:, :HEAD_DIM] = (dk_acc[...] * scale).astype(dkv_ref.dtype)
        dkv_ref[:, HEAD_DIM:] = dv_acc[...].astype(dkv_ref.dtype)


def attend_back(q, keys, values, d_o, lse, cosine, sine, seg_q, pos_q, codes, flags):
    rows, width = q.shape
    heads = width // HEAD_DIM
    kv_heads = keys.shape[1] // HEAD_DIM
    repeat = heads // kv_heads
    length = keys.shape[0]
    blocks = length // rows
    whole = lambda *shape: pl.BlockSpec(shape, lambda h: (0,) * len(shape))
    per_head = pl.BlockSpec((rows, HEAD_DIM), lambda h: (0, h))
    held = pl.BlockSpec(
        (length, HEAD_DIM), lambda h: (0, h // repeat), pipeline_mode=pl.Buffered(1)
    )
    return pl.pallas_call(
        functools.partial(
            attend_back_kernel, rows, HEAD_DIM ** (-0.5) * LOG2E, HEAD_DIM ** (-0.5), repeat
        ),
        grid=(heads,),
        in_specs=[
            pl.BlockSpec(memory_space=pltpu.SMEM),
            per_head,
            held,
            held,
            per_head,
            pl.BlockSpec((1, 1, rows), lambda h: (h, 0, 0)),
            whole(rows, HEAD_DIM),
            whole(rows, HEAD_DIM),
            whole(1, rows),
            whole(1, rows),
            whole(blocks, rows, 1),
        ],
        out_specs=[
            per_head,
            pl.BlockSpec(
                (length, 2 * HEAD_DIM), lambda h: (0, h // repeat), pipeline_mode=pl.Buffered(1)
            ),
        ],
        out_shape=[
            jax.ShapeDtypeStruct((rows, width), BF16),
            jax.ShapeDtypeStruct((length, 2 * keys.shape[1]), BF16),
        ],
        scratch_shapes=[
            pltpu.VMEM((length, HEAD_DIM), F32),
            pltpu.VMEM((length, HEAD_DIM), F32),
            pltpu.VMEM((HEAD_DIM, rows), F32),
            pltpu.VMEM((blocks, rows, rows), F32),
            pltpu.VMEM((blocks, rows, rows), F32),
            pltpu.VMEM((1, rows), F32),
        ],
        compiler_params=pltpu.CompilerParams(vmem_limit_bytes=58 * MIB),
        cost_estimate=FREE,
    )(flags, q, keys, values, d_o, lse, cosine, sine, seg_q, pos_q, codes)


def rope_tables(places, width):
    half = width // 2
    freq = jnp.exp(jnp.arange(half, dtype=F32) * (-2.0 * LOG_BASE / width))
    angle = places.astype(F32)[:, None] * freq[None, :]
    return (jnp.cos(angle), jnp.sin(angle))


def rotate(values, cosine, sine):
    half = HEAD_DIM // 2
    parts = []
    for at in range(0, values.shape[1], HEAD_DIM):
        first = values[:, at : at + half]
        second = values[:, at + half : at + HEAD_DIM]
        parts += [first * cosine - second * sine, second * cosine + first * sine]
    return jnp.concatenate(parts, axis=1)


def inverse_rms(values):
    return lax.rsqrt(jnp.mean(values * values, axis=-1, keepdims=True) + EPS)


def norm_backward(upstream, normed, inverse, gain):
    scaled = upstream * gain
    inner = inverse * (scaled - normed * jnp.mean(scaled * normed, axis=-1, keepdims=True))
    return (inner, jnp.sum(upstream * normed, axis=0))


def rope_lanes(values, cosine, sine):
    parts = []
    for at in range(0, values.shape[1], HEAD_DIM):
        head = values[:, at : at + HEAD_DIM]
        parts.append(head * cosine + pltpu.roll(head, HEAD_DIM // 2, 1) * sine)
    return parts


def project_kernel(
    count, q_width, kv_width, place_ref, mine_ref, theirs_ref,
    x_ref, gain_ref, bias_ref, cos_ref, sin_ref, q_ref, kv_ref, h_ref, w_ref, sems,
):
    copies = [
        pltpu.make_async_copy(stack.at[i], w_ref.at[place_ref[at + i]], sems.at[at + i])
        for at, stack in ((0, mine_ref), (count, theirs_ref))
        for i in range(count)
    ]
    for copy in copies:
        copy.start()
    x = x_ref[...].astype(F32)
    normed = x * lax.rsqrt(jnp.mean(x * x, axis=1, keepdims=True) + EPS)
    h = (normed * gain_ref[...]).astype(BF16)
    h_ref[...] = h
    for copy in copies:
        copy.wait()
    depth, columns = x.shape[1], bias_ref.shape[1]
    weights = w_ref[...].reshape(depth, w_ref.shape[2])
    linear = product(h, weights[:, :columns]) + bias_ref[...]
    turned = rope_lanes(linear[:, : q_width + kv_width], cos_ref[...], sin_ref[...])
    heads = q_width // HEAD_DIM
    for i, part in enumerate(turned):
        if i < heads:
            q_ref[:, i * HEAD_DIM : (i + 1) * HEAD_DIM] = part.astype(BF16)
        else:
            at = (i - heads) * HEAD_DIM
            kv_ref[:, at : at + HEAD_DIM] = part.astype(BF16)
    kv_ref[:, kv_width:] = linear[:, q_width + kv_width :].astype(BF16)


def project(mine, theirs, places, inputs, gain, bias, cosine, sine, q_width, kv_width):
    count = mine.shape[0]
    rows, depth = inputs.shape
    columns = bias.shape[0]
    vmem = pl.BlockSpec(memory_space=pltpu.VMEM)
    return pl.pallas_call(
        functools.partial(project_kernel, count, q_width, kv_width),
        out_shape=[
            jax.ShapeDtypeStruct((rows, q_width), BF16),
            jax.ShapeDtypeStruct((rows, 2 * kv_width), BF16),
            jax.ShapeDtypeStruct((rows, depth), BF16),
            jax.ShapeDtypeStruct((2 * count,) + mine.shape[1:], BF16),
        ],
        in_specs=[pl.BlockSpec(memory_space=pltpu.SMEM)]
        + [pl.BlockSpec(memory_space=pl.ANY)] * 2
        + [vmem] * 5,
        out_specs=[vmem] * 4,
        scratch_shapes=[pltpu.SemaphoreType.DMA((2 * count,))],
        compiler_params=pltpu.CompilerParams(vmem_limit_bytes=40 * MIB),
        cost_estimate=FREE,
    )(places, mine, theirs, inputs, gain[None, :], bias[None, :], cosine, sine)


class Cut:
    def __init__(self, total, n_dp):
        tiles = total // n_dp // 128
        first = max(tiles * 3 // 8, 1)
        self.total = total
        self.n_dp = n_dp
        self.main = (first * 128, (tiles - first) * 128)
        self.start = (0, n_dp * self.main[0])
        self.rest_at = n_dp * (self.main[0] + self.main[1])
        self.rest = (total - self.rest_at) // n_dp
        pad = -(-self.rest // 128) * 128
        self.width = (self.main[0], self.main[1] + pad)


def pick(values, index):
    result = values[0]
    for i in range(1, len(values)):
        result = jnp.where(index == i, values[i], result)
    return result


def cut_kernel(cut, place_ref, *refs):
    n_dp = cut.n_dp
    sources, outs, (scratch, sems) = refs[:3], refs[3 : 3 + 2 * n_dp], refs[3 + 2 * n_dp :]
    copies = [
        pltpu.make_async_copy(source, scratch.at[i], sems.at[i])
        for i, source in enumerate(sources)
    ]
    for copy in copies:
        copy.start()
    for i, copy in enumerate(copies):
        copy.wait()
        for part in range(2):
            main, width = cut.main[part], cut.width[part]
            for k in range(n_dp):
                owner = place_ref[k]
                out = outs[part * n_dp + k]
                at = i * width
                low = pl.multiple_of(cut.start[part] + owner * main, 128)
                out[:, at : at + main] = scratch[i, :, pl.ds(low, main)]
                if part == 1 and cut.rest:
                    tail = scratch[i, :, cut.rest_at :]
                    rest = pick(
                        [tail[:, b * cut.rest : (b + 1) * cut.rest] for b in range(n_dp)], owner
                    )
                    fill = jnp.zeros((rest.shape[0], width - main - cut.rest), rest.dtype)
                    out[:, at + main : at + width] = jnp.concatenate([rest, fill], axis=1)


def cut_units(cut, weights, owners):
    rows = weights[0].shape[0]
    vmem = pl.BlockSpec(memory_space=pltpu.VMEM)
    outs = pl.pallas_call(
        functools.partial(cut_kernel, cut),
        out_shape=[
            jax.ShapeDtypeStruct((rows, 3 * cut.width[part]), BF16)
            for part in range(2)
            for _ in range(cut.n_dp)
        ],
        in_specs=[pl.BlockSpec(memory_space=pltpu.SMEM)]
        + [pl.BlockSpec(memory_space=pl.ANY)] * 3,
        out_specs=[vmem] * (2 * cut.n_dp),
        scratch_shapes=[
            pltpu.VMEM((3,) + weights[0].shape, BF16),
            pltpu.SemaphoreType.DMA((3,)),
        ],
        compiler_params=pltpu.CompilerParams(vmem_limit_bytes=24 * MIB),
        cost_estimate=FREE,
    )(owners, *weights)
    return outs[: cut.n_dp], outs[cut.n_dp :]


def lay_kernel(cut, place_ref, *refs):
    n_dp = cut.n_dp
    firsts, ups = refs[:n_dp], refs[n_dp : 2 * n_dp]
    outs = refs[2 * n_dp :]
    down_at = 3 * cut.width[0]
    lasts = ((firsts, down_at + cut.width[1]), (ups, 0), (firsts, down_at))
    for i, out in enumerate(outs):
        last, last_at = lasts[i]
        for part, (pieces, at) in enumerate(((firsts, i * cut.width[0]), lasts[i])):
            main = cut.main[part]
            for k in range(n_dp):
                low = pl.multiple_of(cut.start[part] + place_ref[k] * main, 128)
                out[:, pl.ds(low, main)] = pieces[k][:, at : at + main].astype(F32)
        if cut.rest:
            tails = [
                piece[:, last_at + cut.main[1] : last_at + cut.width[1]].astype(F32)[:, : cut.rest]
                for piece in last
            ]
            laid = []
            for b in range(n_dp):
                laid.append(
                    functools.reduce(
                        lambda got, k: jnp.where(place_ref[k] == b, tails[k], got),
                        range(1, n_dp),
                        tails[0],
                    )
                )
            out[:, cut.rest_at :] = jnp.concatenate(laid, axis=1)


def lay_units(cut, pieces, owners):
    rows = pieces[0].shape[0]
    vmem = pl.BlockSpec(memory_space=pltpu.VMEM)
    return pl.pallas_call(
        functools.partial(lay_kernel, cut),
        out_shape=[jax.ShapeDtypeStruct((rows, cut.total), F32)] * 3,
        in_specs=[pl.BlockSpec(memory_space=pltpu.SMEM)] + [vmem] * len(pieces),
        out_specs=[vmem] * 3,
        compiler_params=pltpu.CompilerParams(vmem_limit_bytes=32 * MIB),
        cost_estimate=FREE,
    )(owners, *pieces)


def feed_kernel(count, sums, *refs):
    t_ref, c_ref, w_ref = refs[:3]
    p_ref, back_ref, out_ref = refs[-3:]
    pair_weights = w_ref.at[:, : 2 * count]
    down_weight = w_ref.at[:, 2 * count :]
    pair = product(t_ref[...], pair_weights[...])
    gate, upper = pair[:, :count], pair[:, count:]
    act_back = product(c_ref[...], down_weight[...])
    sigma = 1.0 / (1.0 + jnp.exp(-gate))
    swish = gate * sigma
    activated = (swish * upper).astype(BF16)
    gate_back = (act_back * upper * sigma * (1.0 + gate * (1.0 - sigma))).astype(BF16)
    upper_back = (act_back * swish).astype(BF16)
    for i, value in enumerate((gate_back, upper_back, activated)):
        p_ref[:, i * count : (i + 1) * count] = value
    back = right_product(p_ref[:, : 2 * count], pair_weights[...])
    out = right_product(activated, down_weight[...])
    if sums:
        back = back + refs[3][...].astype(F32)
        out = out + refs[4][...].astype(F32)
    back_ref[...] = back.astype(back_ref.dtype)
    out_ref[...] = out.astype(out_ref.dtype)


def feed(tokens, cots, weights, side, kept, earlier):
    rows, width = tokens.shape
    columns = weights.shape[1]
    span = rows // 2
    tall = min(256, span)
    steps = span // tall
    block = lambda w: pl.BlockSpec((tall, w), lambda i: (side * steps + i, 0))
    near = pl.BlockSpec((tall, width), lambda i: (i, 0))
    operands = [tokens, cots, weights]
    in_specs = [
        block(width),
        block(width),
        pl.BlockSpec((width, columns), lambda i: (0, 0), pipeline_mode=pl.Buffered(1)),
    ]
    if earlier is not None:
        operands += list(earlier)
        in_specs += [near, near]
    aliases = {}
    if kept is not None:
        aliases = {len(operands): 0}
        operands.append(kept)
        in_specs.append(pl.BlockSpec(memory_space=pl.ANY))
    return pl.pallas_call(
        functools.partial(feed_kernel, columns // 3, earlier is not None),
        grid=(steps,),
        in_specs=in_specs,
        out_specs=[block(columns), near, near],
        out_shape=[
            jax.ShapeDtypeStruct((rows, columns), BF16),
            jax.ShapeDtypeStruct((span, width), BF16),
            jax.ShapeDtypeStruct((span, width), BF16),
        ],
        input_output_aliases=aliases,
        compiler_params=pltpu.CompilerParams(vmem_limit_bytes=56 * MIB),
        cost_estimate=FREE,
    )(*operands)


def one_grads_kernel(left_ref, p_ref, o_ref):
    o_ref[...] = left_product(left_ref[...], p_ref[...]).astype(BF16)


def grads_kernel(split, t_ref, c_ref, p_ref, o_ref):
    step = pl.program_id(0)

    @pl.when(step < split)
    def _():
        o_ref[...] = left_product(t_ref[...], p_ref[...]).astype(BF16)

    @pl.when(step >= split)
    def _():
        o_ref[...] = left_product(c_ref[...], p_ref[...]).astype(BF16)


def unit_gradients(tokens, cots, kept, which=(0, 1, 2), cost=FREE):
    rows, width = tokens.shape
    count = kept.shape[1] // 3
    wide = 384 if count % 384 == 0 else 128
    each = count // wide
    split = each * sum(i < 2 for i in which)
    first = which[0] * each
    held = pl.BlockSpec((rows, width), lambda i: (0, 0), pipeline_mode=pl.Buffered(1))
    kernel, lefts = functools.partial(grads_kernel, split), (tokens, cots)
    if len(which) == 1:
        kernel, lefts = one_grads_kernel, ((tokens, tokens, cots)[which[0]],)
    return pl.pallas_call(
        kernel,
        grid=(each * len(which),),
        in_specs=[held] * len(lefts) + [pl.BlockSpec((rows, wide), lambda i: (0, first + i))],
        out_specs=pl.BlockSpec((width, wide), lambda i: (0, i)),
        out_shape=jax.ShapeDtypeStruct((width, len(which) * count), BF16),
        compiler_params=pltpu.CompilerParams(vmem_limit_bytes=56 * MIB),
        cost_estimate=cost,
    )(*lefts, kept)


def d_o_kernel(own_ref, other_ref, w_ref, d_o_ref, rows_ref):
    half = own_ref.shape[0]
    weights = w_ref[...]
    d_o_ref[:half] = product(own_ref[...], weights).astype(BF16)
    d_o_ref[half:] = product(other_ref[...], weights).astype(BF16)
    rows_ref[:half] = own_ref[...]
    rows_ref[half:] = other_ref[...]


def d_o_of(own, other, weights, first, count):
    half, width = own.shape
    wide = math.gcd(first, count)
    whole = lambda *shape: pl.BlockSpec(shape, lambda i: (0, 0))
    return pl.pallas_call(
        d_o_kernel,
        grid=(count // wide,),
        in_specs=[
            whole(half, width),
            whole(half, width),
            pl.BlockSpec((width, wide), lambda i: (0, first // wide + i)),
        ],
        out_specs=[pl.BlockSpec((2 * half, wide), lambda i: (0, i)), whole(2 * half, width)],
        out_shape=[
            jax.ShapeDtypeStruct((2 * half, count), BF16),
            jax.ShapeDtypeStruct((2 * half, width), BF16),
        ],
        compiler_params=pltpu.CompilerParams(vmem_limit_bytes=32 * MIB),
        cost_estimate=FREE,
    )(own, other, weights)


def against_kernel(left_ref, right_ref, out_ref):
    out_ref[...] = right_product(left_ref[...], right_ref[...]).astype(out_ref.dtype)


def against(left, right, dtype):
    rows, depth = left.shape
    count = right.shape[0]
    wide = 512 if count % 512 == 0 else count
    return pl.pallas_call(
        against_kernel,
        grid=(count // wide,),
        in_specs=[
            pl.BlockSpec((rows, depth), lambda i: (0, 0)),
            pl.BlockSpec((wide, depth), lambda i: (i, 0)),
        ],
        out_specs=pl.BlockSpec((rows, wide), lambda i: (0, i)),
        out_shape=jax.ShapeDtypeStruct((rows, count), dtype),
        compiler_params=pltpu.CompilerParams(vmem_limit_bytes=32 * MIB),
        cost_estimate=FREE,
    )(left, right)


def halves_kernel(n_seq, share, core_ref, left_ref, right_ref, own_ref, sent_ref, keep_ref):
    keep_ref[...] = left_product(left_ref[...], right_ref[...]).astype(BF16)
    tall = own_ref.shape[1]
    for z in range(n_seq):
        for out, core in ((own_ref, core_ref[0]), (sent_ref, 1 - core_ref[0])):
            at = pl.multiple_of((z * 2 + core) * tall, share)
            out[z] = keep_ref[pl.ds(at, tall), :]


def gradient_halves(left, right, core, n_seq, share):
    width, columns = left.shape[1], right.shape[1]
    vmem = pl.BlockSpec(memory_space=pltpu.VMEM)
    half = jax.ShapeDtypeStruct((n_seq, width // (2 * n_seq), columns), BF16)
    return pl.pallas_call(
        functools.partial(halves_kernel, n_seq, share),
        out_shape=[half, half],
        in_specs=[pl.BlockSpec(memory_space=pltpu.SMEM), vmem, vmem],
        out_specs=[vmem, vmem],
        scratch_shapes=[pltpu.VMEM((width, columns), BF16)],
        compiler_params=pltpu.CompilerParams(vmem_limit_bytes=32 * MIB),
        cost_estimate=FREE,
    )(core, left, right)


def plane_gather(own, *others):
    cut = own.shape[0] // 2
    over_x, over_y, *others = together(dp_swap(own, 2), y_swap(own), *others)
    far_x = y_swap(over_x[:cut])
    far_y = dp_swap(over_y[cut:], 2)
    near = [own, over_y, over_x]
    across = [dp_swap(piece, 1) for piece in near]
    far_x, far_y, *across = together(far_x, far_y, *across)
    far = jnp.concatenate([far_x, far_y], axis=0)
    return near + [far] + across + [dp_swap(far, 1)], others


class PlaneScatter:
    def __init__(self, near, over_core):
        self.near, self.over_core = near, over_core
        self.t = near.shape[0] // 4
        self.cut = self.t // 2

    def summed(self, low, high):
        return self.near[low:high].astype(F32) + self.over_core[low:high].astype(F32)

    def corner(self):
        corner = self.summed(3 * self.t, 4 * self.t).astype(BF16)
        return corner[: self.cut], corner[self.cut :]

    def sides(self, corner_x, corner_y):
        t, cut = self.t, self.cut
        to_y = [self.summed(t, t + cut) + corner_x.astype(F32), self.summed(t + cut, 2 * t)]
        to_x = [
            self.summed(2 * t, 2 * t + cut),
            self.summed(2 * t + cut, 3 * t) + corner_y.astype(F32),
        ]
        return tuple(jnp.concatenate(part, axis=0).astype(BF16) for part in (to_x, to_y))

    def sides_of(self, corner_x):
        t = self.t
        to_y = self.summed(t, 2 * t) + corner_x.astype(F32)
        return self.summed(2 * t, 3 * t).astype(BF16), to_y.astype(BF16)

    def home(self, over_x, over_y):
        return self.summed(0, self.t) + over_x.astype(F32) + over_y.astype(F32)


def on_device(
    hidden, cotangent, segments, positions, first_gain,
    query_weight, query_bias, key_weight, key_bias, value_weight, value_bias,
    out_weight, second_gain, gate_weight, up_weight, down_weight,
):
    n_dp, n_seq = lax.axis_size("dp"), lax.axis_size("seq")
    dp, seq, tensor = (lax.axis_index(a) for a in ("dp", "seq", "tensor"))
    rows, width = hidden.shape
    half = rows // 2
    share = query_weight.shape[0]
    group = segments.shape[0]
    blocks = group // rows
    q_width, kv_width = query_weight.shape[1], key_weight.shape[1]
    kv_end = q_width + kv_width
    def slots_of(owners):
        return (owners % 2) * (n_dp // 2) + owners // 2

    dp_owners = dp ^ jnp.arange(n_dp, dtype=jnp.int32)
    dp_slots = slots_of(dp_owners)
    seq_places = (seq - jnp.arange(n_seq, dtype=jnp.int32) + n_seq) % n_seq
    flips = jnp.repeat(np.array([0, 2, 1, 3], np.int32), n_seq)
    all_places = jnp.tile(seq_places, 4) * n_dp + slots_of(dp ^ flips)
    core, x = (dp % 2).astype(jnp.int32), (dp // 2).astype(jnp.int32)
    tensor_place = tensor.astype(jnp.int32)[None]
    dp_owners, dp_slots, seq_places, all_places, core_place, tensor_place, core, x, *scalars = together(
        dp_owners, dp_slots, seq_places, all_places, core[None], tensor_place, core, x,
        *[seq_places[s] for s in range(n_seq)],
    )

    def take(values, index, axis):
        return lax.dynamic_index_in_dim(
            values, index, axis, keepdims=False, allow_negative_indices=False
        )


    def vector_in(vector):
        parts = vector.reshape(n_dp // 2, 2, n_seq, share)
        return parts.transpose(2, 1, 0, 3).reshape(width).astype(F32)

    def vector_out(vector):
        parts = vector.reshape(n_seq, 2, n_dp // 2, share)
        return parts.transpose(2, 1, 0, 3).reshape(width)

    index = jnp.arange(width, dtype=jnp.int32)
    owner, place = index // (share * n_seq), index // share % n_seq
    slot = owner % 2 * (n_dp // 2) + owner // 2
    inner_of = (place * n_dp + slot) * share + index % share
    shuffles = []

    def relative(values):
        turned = jnp.concatenate([values[half:], values[:half]], axis=0)
        return jnp.where(tensor == 0, values, turned)

    def to_inner(values):
        return product(relative(values), shuffles[0]).astype(BF16)

    def from_inner(values):
        return against(values, shuffles[0], BF16)

    gain_first, gain_second = vector_in(first_gain), vector_in(second_gain)

    cut = Cut(gate_weight.shape[1], n_dp)

    def spread(pieces):
        return [dp_swap(piece, k) if k else piece for k, piece in enumerate(pieces)]

    def stack_units(pieces):
        return assemble(pieces, dp_slots).reshape(n_dp * share, pieces[0].shape[1])

    own_place = relative(take(positions.reshape(blocks, rows), scalars[0], 0))
    own_segment = relative(take(segments.reshape(blocks, rows), scalars[0], 0))
    def tables(places):
        cosine, sine = rope_tables(places, HEAD_DIM)
        return (
            jnp.concatenate([cosine, cosine], axis=1), jnp.concatenate([-sine, sine], axis=1)
        )


    line = [jnp.concatenate([query_weight, key_weight, value_weight, out_weight.T], axis=1)]
    over_x = []
    for s in range(n_seq):
        over_x.append(dp_swap(line[s], 2))
        if s + 1 == n_seq:
            cot_own = to_inner(after(cotangent, line[s]))
            over_x[s], cot_own = together(over_x[s], cot_own)
            break
        moved = z_shift(line[s], 1)
        if s == 0:
            first_parts, second_parts = cut_units(
                cut, (gate_weight, up_weight, down_weight.T), dp_owners
            )
            moved, over_x[s], *parts = together(moved, over_x[s], *first_parts, *second_parts)
            first_parts, second_parts = parts[:n_dp], parts[n_dp:]
        elif s == 1:
            first_parts = spread(first_parts)
            inner = after(inner_of, line[s])
            shuffles.extend(together((inner[:, None] == index[None, :]).astype(BF16)))
            inputs = to_inner(after(hidden, line[s]))
            cosine, sine = tables(after(own_place, line[s]))
            moved, over_x[s], inputs, cosine, sine, *first_parts = together(
                moved, over_x[s], inputs, cosine, sine, *first_parts
            )
        elif s == 2:
            first_stacked = stack_units(first_parts)
            first_units = lax.all_gather(first_stacked, "seq", axis=0, tiled=True)
            moved, over_x[s], first_stacked = together(moved, over_x[s], first_stacked)
        else:
            moved, over_x[s] = together(moved, over_x[s])
        line.append(moved)
    mine = assemble(line + over_x, jnp.arange(2 * n_seq, dtype=jnp.int32))
    theirs = dp_swap(mine, 1)

    bias = jnp.concatenate([query_bias, key_bias, value_bias]).astype(F32)
    queries, own_kv, first_rounded, attention_weights = project(
        mine, theirs, all_places, inputs, gain_first, bias, cosine, sine, q_width, kv_width
    )
    qkv_end = q_width + 2 * kv_width
    attention_weights = attention_weights.reshape(width, qkv_end + q_width)
    qkv_full, out_full = attention_weights[:, :qkv_end], attention_weights[:, qkv_end:]
    group_kv = [own_kv] + [z_shift(own_kv, s) for s in range(1, n_seq)]
    second_parts = spread([after(part, own_kv) for part in second_parts])
    def key_rows(vector):
        taken = jnp.take(vector.reshape(blocks, rows), seq_places, axis=0)
        return relative(taken.T).T

    seg_k, pos_k = (key_rows(after(v, own_kv)) for v in (segments, positions))
    seen = pair_mask(
        own_segment[None, :, None], own_place[None, :, None], seg_k[:, None, :], pos_k[:, None, :]
    )
    flags = (jnp.any(seen, axis=(1, 2)).astype(jnp.int32) + jnp.all(seen, axis=(1, 2))).astype(
        jnp.int32
    )
    codes = (seg_k * SEGMENT_STEP + pos_k)[:, :, None]
    pairs = (own_segment[None, :], own_place[None, :], codes, flags)
    *group_kv, cot_own, second_parts, pairs = together(*group_kv, cot_own, second_parts, pairs)
    second_stacked = stack_units(second_parts)
    second_units = lax.all_gather(second_stacked, "seq", axis=0, tiled=True)
    cot_x = dp_swap(cot_own, 2)
    group_kv = jnp.concatenate(group_kv, axis=0)
    keys, values = group_kv[:, :kv_width], group_kv[:, kv_width:]

    attended, lse = attend(queries, keys, values, *pairs)
    def reduce_halves(part):
        return part[:half] + y_swap(part[half:].astype(BF16)).astype(F32)

    inputs_half = inputs[:half].astype(F32)
    out_theirs = y_swap(right_product(attended[half:], out_full).astype(BF16))
    out_mine = right_product(attended[:half], out_full)
    out_theirs, out_mine, cot_x = together(out_theirs, out_mine, cot_x)
    cot_pieces = [cot_own, cot_x, dp_swap(cot_own, 1), dp_swap(cot_x, 1)]
    cots = assemble(cot_pieces, jnp.arange(4, dtype=jnp.int32)).reshape(-1, width)
    residual = inputs_half + out_mine + out_theirs.astype(F32)
    second_inverse = inverse_rms(residual)
    second_normed = residual * second_inverse
    second_rounded = (second_normed * gain_second).astype(BF16)

    gathered, (cots,) = plane_gather(second_rounded, cots)
    tokens = assemble(gathered, jnp.arange(len(gathered), dtype=jnp.int32)).reshape(-1, width)

    kept, *far = feed(tokens, cots, first_units, 1, None, None)
    kept, *near = feed(tokens, cots, first_units, 0, kept, None)
    first_gradient = unit_gradients(tokens, cots, kept)
    second_weights = after(second_units, first_gradient)
    second_kept, back_far, out_far = feed(tokens, cots, second_weights, 1, None, far)
    second_kept, back_near, out_near = feed(
        tokens, cots, second_weights, 0, second_kept, near
    )
    first_share = lax.psum_scatter(first_gradient, "seq", scatter_dimension=0, tiled=True)
    flops = 2 * tokens.size * cut.width[1]
    cost = pl.CostEstimate(flops=flops, bytes_accessed=0, transcendentals=0)

    def second_gradient(which, operand):
        return unit_gradients(tokens, cots, after(second_kept, operand), (which,), cost)

    def sum_along_seq(gradient):
        return lax.psum_scatter(gradient, "seq", scatter_dimension=0, tiled=True)

    back = PlaneScatter(*reversed(together(dp_swap(back_far, 1), back_near)))
    corner = back.corner()
    *corners, down_gradient = together(
        dp_swap(corner[0], 2), y_swap(corner[1]), second_gradient(2, corner[0])
    )
    down_share = sum_along_seq(down_gradient)
    sides = back.sides(*corners)
    *over, gate_gradient, first_share = together(
        dp_swap(sides[0], 2), y_swap(sides[1]), second_gradient(0, sides[0]), first_share
    )
    gate_share = sum_along_seq(gate_gradient)
    second_back = back.home(*over)

    residual_inner, second_gain_term = norm_backward(
        second_back, second_normed, second_inverse, gain_second
    )
    residual_back = cot_own[:half].astype(F32) + residual_inner
    back_half = residual_back.astype(BF16)
    def exchange_units(*shares):
        stacks = [mine.reshape(n_dp, share, mine.shape[1]) for mine in shares]
        pieces = pick_pieces(stacks, dp_slots)
        return [dp_swap(piece, k) if k else piece for k, piece in enumerate(pieces)]

    out_core = dp_swap(after(out_far, back_half), 1)
    corner = PlaneScatter(out_near, out_core).summed(3 * half, 4 * half).astype(BF16)
    back_other, out_core, up_gradient, down_share, corner_x = together(
        y_swap(back_half), out_core, second_gradient(1, back_half), down_share, dp_swap(corner, 2)
    )
    down = PlaneScatter(out_near, out_core)
    attended_back, attention_back = d_o_of(
        back_half, back_other, attention_weights, qkv_end, q_width
    )

    def halves_of(left, right):
        return gradient_halves(left, right, core_place, n_seq, share)

    def x_halves(own, over_core):
        parts = own.astype(F32) + over_core.astype(F32)
        parts = parts.reshape(n_seq, n_dp // 2, share, own.shape[2])
        return take(parts, x, 1), take(parts, 1 - x, 1).astype(BF16)

    def place_of(parts, s):
        return take(parts, scalars[s % n_seq], 0)

    out_own, sent = halves_of(attention_back, attended)
    sides = down.sides_of(corner_x)
    over = dp_swap(sides[0], 2), y_swap(sides[1])
    (out_over_core,) = together(dp_swap(sent, 1))
    out_own, sent = x_halves(out_own, out_over_core)
    out_over_x = dp_swap(sent, 2)
    attended_back, out_sent = together(attended_back, sent)
    query_linear_back, kv_parts = attend_back(
        queries, keys, values, attended_back, lse, cosine, sine, *pairs
    )
    query_linear_back, kv_parts, out_over_x, *over = together(
        query_linear_back, kv_parts, out_over_x, *over
    )

    kv_moved = [z_shift(kv_parts[s * rows : (s + 1) * rows], -s) for s in range(1, n_seq)]
    query_own, query_sent = halves_of(first_rounded, query_linear_back)
    query_own, gate_share, query_over_core, *kv_moved = together(
        query_own, gate_share, dp_swap(query_sent, 1), *kv_moved
    )
    *kv_moved, up_gradient = together(*kv_moved, up_gradient)
    out_rows = out_own + out_over_x.astype(F32)
    up_share = sum_along_seq(up_gradient)
    kv_back = kv_parts[:rows].astype(F32)
    for moved in kv_moved:
        kv_back = kv_back + moved.astype(F32)
    key_linear_back = rotate(
        kv_back[:, :kv_width], cosine[:, : HEAD_DIM // 2], -sine[:, HEAD_DIM // 2 :]
    )
    kv_linear_back = jnp.concatenate([key_linear_back, kv_back[:, kv_width:]], axis=1).astype(BF16)
    linear_back = jnp.concatenate([query_linear_back, kv_linear_back], axis=1)

    query_own, sent = x_halves(query_own, query_over_core)
    query_over_x = dp_swap(sent, 2)
    kv_own, sent = halves_of(first_rounded, kv_linear_back)
    kv_over_core = dp_swap(sent, 1)
    first_theirs = y_swap(against(linear_back[half:], attention_weights, BF16))
    first_mine = against(linear_back[:half], attention_weights, F32)
    query_over_x, kv_over_core = together(query_over_x, kv_over_core)
    large = jnp.concatenate([query_own + query_over_x.astype(F32), out_rows], axis=2)

    kv_own, sent = x_halves(kv_own, kv_over_core)
    kv_over_x = dp_swap(sent, 2)
    total = z_shift(place_of(large, 1).astype(BF16), 1)
    out_half = from_inner((residual + down.home(*over)).astype(BF16))
    total, kv_over_x, first_theirs, first_mine, out_half = together(
        total, kv_over_x, first_theirs, first_mine, out_half
    )
    kv_rows = kv_own + kv_over_x.astype(F32)
    total = place_of(large, 2) + total.astype(F32)

    out_other = y_swap(out_half)
    first_back = first_mine + first_theirs.astype(F32)
    first_inverse = inverse_rms(inputs_half)
    input_inner, first_gain_term = norm_backward(
        first_back, inputs_half * first_inverse, first_inverse, gain_first
    )
    input_half = (residual_back + input_inner).astype(BF16)
    bias_terms = jnp.sum(linear_back.astype(F32), axis=0)
    sums = jnp.concatenate([first_gain_term, second_gain_term, bias_terms])

    def shift_add(values, axis):
        size = lax.axis_size(axis)
        moved = [
            lax.ppermute(values, axis, [(i, (i + s) % size) for i in range(size)])
            for s in range(1, size)
        ]
        return functools.reduce(jnp.add, moved, values)

    input_half = from_inner(input_half)
    input_other = y_swap(input_half)
    pieces = exchange_units(first_share, down_share, gate_share)
    kv_moved = [z_shift(place_of(kv_rows, s).astype(BF16), -s) for s in range(1, n_seq)]
    sums = shift_add(sums, "dp")
    for s in range(2, n_seq):
        total = z_shift(total.astype(BF16), 1)
        if s == 2:
            total, sums, out_other, up_share, *arrived = together(
                total, sums, out_other, up_share, *kv_moved, *pieces
            )
            kv_moved, pieces = arrived[: n_seq - 1], arrived[n_seq - 1 :]
            up_pieces = exchange_units(up_share)
            sums = shift_add(sums, "seq")
        elif s == 3:
            total, sums, input_other, *up_pieces = together(
                total, sums, input_other, *up_pieces
            )
        total = place_of(large, s + 1) + total.astype(F32)
    kv_share = functools.reduce(
        lambda a, b: a + b.astype(F32), kv_moved, place_of(kv_rows, 0)
    )
    gain_terms = shift_add(sums[: 2 * width], "tensor")
    bias_terms = sums[2 * width :]
    input_gradient = join_halves(input_half, input_other, tensor_place)
    output = join_halves(out_half, out_other, tensor_place)
    large_share = total
    out_gradient = large_share[:, q_width:].T
    gate_gradient, up_gradient, down_gradient = lay_units(
        cut, pieces + up_pieces, dp_owners
    )
    down_gradient = down_gradient.T
    return (
        output,
        input_gradient,
        vector_out(gain_terms[:width]),
        large_share[:, :q_width],
        bias_terms[:q_width],
        kv_share[:, :kv_width],
        bias_terms[q_width:kv_end],
        kv_share[:, kv_width:],
        bias_terms[kv_end:],
        out_gradient,
        vector_out(gain_terms[width:]),
        gate_gradient,
        up_gradient,
        down_gradient,
    )


def solution(mesh):
    tokens = P(("dp", "seq"), None)
    by_row = P(("dp", "seq"), "tensor")
    by_column = P("tensor", ("dp", "seq"))
    heads = P("tensor")
    in_specs = (
        tokens, tokens, P("dp"), P("dp"), P(), by_row, heads, by_row, heads, by_row, heads,
        by_column, P(), by_row, by_row, by_column,
    )
    out_specs = (
        tokens, tokens, P(), by_row, heads, by_row, heads, by_row, heads, by_column, P(),
        by_row, by_row, by_column,
    )
    return jax.shard_map(
        on_device, mesh=mesh, in_specs=in_specs, out_specs=out_specs, check_vma=False
    )
```

```python
import functools
import math

import jax
import jax.numpy as jnp
import numpy as np
from jax import lax
from jax.experimental import pallas as pl
from jax.experimental.pallas import tpu as pltpu
from jax.sharding import PartitionSpec as P

HEAD_DIM = 128
EPS = 1e-06
LOG_BASE = math.log(1000000.0)
NEG_FILL = -1e30
LOG2E = 1.0 / math.log(2.0)
MIB = 1024 * 1024
F32 = jnp.float32
BF16 = jnp.bfloat16
FREE = pl.CostEstimate(flops=0, bytes_accessed=0, transcendentals=0)


def product(left, right):
    return jnp.dot(left, right, preferred_element_type=F32)


def left_product(left, right):
    return lax.dot_general(left, right, (((0,), (0,)), ((), ())), preferred_element_type=F32)


def right_product(left, right):
    return lax.dot_general(left, right, (((1,), (1,)), ((), ())), preferred_element_type=F32)


def after(value, *others):
    return lax.optimization_barrier((value,) + others)[0]


def together(*values):
    return lax.optimization_barrier(values)


def dp_swap(value, flip):
    size = lax.axis_size("dp")
    return lax.ppermute(value, "dp", [(i, i ^ flip) for i in range(size)])


def y_swap(value):
    return lax.ppermute(value, "tensor", [(0, 1), (1, 0)])


def z_shift(value, step):
    size = lax.axis_size("seq")
    return lax.ppermute(value, "seq", [(i, (i + step) % size) for i in range(size)])


def assemble_kernel(count, place_ref, *refs):
    pieces, out_ref, sems = refs[:count], refs[count], refs[count + 1]
    copies = [
        pltpu.make_async_copy(piece, out_ref.at[place_ref[i]], sems.at[i])
        for i, piece in enumerate(pieces)
    ]
    for copy in copies:
        copy.start()
    for copy in copies:
        copy.wait()


def assemble(pieces, places):
    count = len(pieces)
    return pl.pallas_call(
        functools.partial(assemble_kernel, count),
        out_shape=jax.ShapeDtypeStruct((count,) + pieces[0].shape, pieces[0].dtype),
        in_specs=[pl.BlockSpec(memory_space=pltpu.SMEM)]
        + [pl.BlockSpec(memory_space=pl.ANY)] * count,
        out_specs=pl.BlockSpec(memory_space=pltpu.VMEM),
        scratch_shapes=[pltpu.SemaphoreType.DMA((count,))],
        compiler_params=pltpu.CompilerParams(vmem_limit_bytes=24 * MIB),
        cost_estimate=FREE,
    )(places, *pieces)


def join_kernel(place_ref, own_ref, other_ref, out_ref):
    half = own_ref.shape[0]
    for ref, place in ((own_ref, place_ref[0]), (other_ref, 1 - place_ref[0])):
        out_ref[pl.ds(pl.multiple_of(place * half, half), half), :] = ref[...]


def join_halves(own, other, place):
    vmem = pl.BlockSpec(memory_space=pltpu.VMEM)
    return pl.pallas_call(
        join_kernel,
        out_shape=jax.ShapeDtypeStruct((2 * own.shape[0], own.shape[1]), own.dtype),
        in_specs=[pl.BlockSpec(memory_space=pltpu.SMEM), vmem, vmem],
        out_specs=vmem,
        compiler_params=pltpu.CompilerParams(vmem_limit_bytes=24 * MIB),
        cost_estimate=FREE,
    )(place, own, other)


def pick_kernel(count, place_ref, *refs):
    stacks, outs = refs[:count], refs[count:]
    for i, out in enumerate(outs):
        at = 0
        for stack in stacks:
            wide = stack.shape[2]
            out[:, at : at + wide] = stack[place_ref[i]]
            at += wide


def pick_pieces(stacks, places):
    vmem = pl.BlockSpec(memory_space=pltpu.VMEM)
    slots, rows = stacks[0].shape[:2]
    columns = sum(stack.shape[2] for stack in stacks)
    return pl.pallas_call(
        functools.partial(pick_kernel, len(stacks)),
        out_shape=[jax.ShapeDtypeStruct((rows, columns), stacks[0].dtype)] * slots,
        in_specs=[pl.BlockSpec(memory_space=pltpu.SMEM)] + [vmem] * len(stacks),
        out_specs=[vmem] * slots,
        compiler_params=pltpu.CompilerParams(vmem_limit_bytes=24 * MIB),
        cost_estimate=FREE,
    )(places, *stacks)


SEGMENT_STEP = 1 << 16


def pair_mask(seg_q, pos_q, seg_k, pos_k):
    return ((seg_k == 0) | (seg_k == seg_q)) & (pos_k <= pos_q)


def block_mask(sq_ref, pq_ref, codes):
    segments = codes // SEGMENT_STEP
    return pair_mask(sq_ref[...], pq_ref[...], segments, codes - segments * SEGMENT_STEP)


def attend_kernel(
    rows, factor, flag_ref, q_ref, k_ref, v_ref, sq_ref, pq_ref, code_ref,
    o_ref, lse_ref, top_ref, sum_ref, acc_ref,
):
    blocks = k_ref.shape[0] // rows
    top_ref[...] = jnp.full_like(top_ref, NEG_FILL)
    sum_ref[...] = jnp.zeros_like(sum_ref)
    acc_ref[...] = jnp.zeros_like(acc_ref)
    q = q_ref[...]

    def block_step(j, masked):
        span = pl.ds(pl.multiple_of(j * rows, rows), rows)
        s = right_product(k_ref[span, :], q) * factor
        if masked:
            mask = block_mask(sq_ref, pq_ref, code_ref[j])
            s = jnp.where(mask, s, NEG_FILL)
        top = top_ref[...]
        new_top = jnp.maximum(top, jnp.max(s, axis=0, keepdims=True))
        e = jnp.exp2(s - new_top)
        if masked:
            e = jnp.where(mask, e, 0.0)
        shrink = jnp.exp2(top - new_top)
        top_ref[...] = new_top
        sum_ref[...] = sum_ref[...] * shrink + jnp.sum(e, axis=0, keepdims=True)
        acc_ref[...] = acc_ref[...] * shrink + left_product(v_ref[span, :], e.astype(BF16))

    def step(j, carry):
        @pl.when(flag_ref[j] == 2)
        def _():
            block_step(j, False)

        @pl.when(flag_ref[j] == 1)
        def _():
            block_step(j, True)

        return carry

    lax.fori_loop(0, blocks, step, 0)
    total = sum_ref[...]
    o_ref[...] = (acc_ref[...] / total).T.astype(o_ref.dtype)
    lse_ref[...] = (top_ref[...] + jnp.log2(total))[None]


def attend(q, keys, values, seg_q, pos_q, codes, flags):
    rows, width = q.shape
    heads = width // HEAD_DIM
    kv_heads = keys.shape[1] // HEAD_DIM
    repeat = heads // kv_heads
    length = keys.shape[0]
    blocks = length // rows
    whole = lambda *shape: pl.BlockSpec(shape, lambda h: (0,) * len(shape))
    return pl.pallas_call(
        functools.partial(attend_kernel, rows, HEAD_DIM ** (-0.5) * LOG2E),
        grid=(heads,),
        in_specs=[
            pl.BlockSpec(memory_space=pltpu.SMEM),
            pl.BlockSpec((rows, HEAD_DIM), lambda h: (0, h)),
            pl.BlockSpec((length, HEAD_DIM), lambda h: (0, h // repeat)),
            pl.BlockSpec((length, HEAD_DIM), lambda h: (0, h // repeat)),
            whole(1, rows),
            whole(1, rows),
            whole(blocks, rows, 1),
        ],
        out_specs=[
            pl.BlockSpec((rows, HEAD_DIM), lambda h: (0, h)),
            pl.BlockSpec((1, 1, rows), lambda h: (h, 0, 0)),
        ],
        out_shape=[
            jax.ShapeDtypeStruct((rows, width), BF16),
            jax.ShapeDtypeStruct((heads, 1, rows), F32),
        ],
        scratch_shapes=[
            pltpu.VMEM((1, rows), F32),
            pltpu.VMEM((1, rows), F32),
            pltpu.VMEM((HEAD_DIM, rows), F32),
        ],
        compiler_params=pltpu.CompilerParams(vmem_limit_bytes=40 * MIB),
        cost_estimate=FREE,
    )(flags, q, keys, values, seg_q, pos_q, codes)


def attend_back_kernel(
    rows, factor, scale, repeat, flag_ref, q_ref, k_ref, v_ref, do_ref, lse_ref, cos_ref, sin_ref,
    sq_ref, pq_ref, code_ref, dq_ref, dkv_ref, dk_acc, dv_acc, dq_acc, p_keep, dp_keep, delta_ref,
):
    head = pl.program_id(0)
    blocks = k_ref.shape[0] // rows

    @pl.when(lax.rem(head, repeat) == 0)
    def _():
        dk_acc[...] = jnp.zeros_like(dk_acc)
        dv_acc[...] = jnp.zeros_like(dv_acc)

    dq_acc[...] = jnp.zeros_like(dq_acc)
    delta_ref[...] = jnp.zeros_like(delta_ref)
    q = q_ref[...]
    d_o = do_ref[...]
    lse = lse_ref[0]

    def span_of(j):
        return pl.ds(pl.multiple_of(j * rows, rows), rows)

    def first_pass(j, masked):
        p = jnp.exp2(right_product(k_ref[span_of(j), :], q) * factor - lse)
        if masked:
            p = jnp.where(block_mask(sq_ref, pq_ref, code_ref[j]), p, 0.0)
        dp = right_product(v_ref[span_of(j), :], d_o)
        p_keep[j] = p
        dp_keep[j] = dp
        delta_ref[...] += jnp.sum(p * dp, axis=0, keepdims=True)

    def first_step(j, carry):
        @pl.when(flag_ref[j] == 2)
        def _():
            first_pass(j, False)

        @pl.when(flag_ref[j] == 1)
        def _():
            first_pass(j, True)

        return carry

    lax.fori_loop(0, blocks, first_step, 0)

    def second_step(j, carry):
        @pl.when(flag_ref[j] > 0)
        def _():
            p = p_keep[j]
            ds = (p * (dp_keep[j] - delta_ref[...])).astype(BF16)
            span = span_of(j)
            dv_acc[span, :] += product(p.astype(BF16), d_o)
            dk_acc[span, :] += product(ds, q)
            dq_acc[...] += left_product(k_ref[span, :], ds)

        return carry

    lax.fori_loop(0, blocks, second_step, 0)
    (turned,) = rope_lanes((dq_acc[...] * scale).T, cos_ref[...], -sin_ref[...])
    dq_ref[...] = turned.astype(dq_ref.dtype)

    @pl.when(lax.rem(head, repeat) == repeat - 1)
    def _():
        dkv_ref[:, :HEAD_DIM] = (dk_acc[...] * scale).astype(dkv_ref.dtype)
        dkv_ref[:, HEAD_DIM:] = dv_acc[...].astype(dkv_ref.dtype)


def attend_back(q, keys, values, d_o, lse, cosine, sine, seg_q, pos_q, codes, flags):
    rows, width = q.shape
    heads = width // HEAD_DIM
    kv_heads = keys.shape[1] // HEAD_DIM
    repeat = heads // kv_heads
    length = keys.shape[0]
    blocks = length // rows
    whole = lambda *shape: pl.BlockSpec(shape, lambda h: (0,) * len(shape))
    per_head = pl.BlockSpec((rows, HEAD_DIM), lambda h: (0, h))
    held = pl.BlockSpec(
        (length, HEAD_DIM), lambda h: (0, h // repeat), pipeline_mode=pl.Buffered(1)
    )
    return pl.pallas_call(
        functools.partial(
            attend_back_kernel, rows, HEAD_DIM ** (-0.5) * LOG2E, HEAD_DIM ** (-0.5), repeat
        ),
        grid=(heads,),
        in_specs=[
            pl.BlockSpec(memory_space=pltpu.SMEM),
            per_head,
            held,
            held,
            per_head,
            pl.BlockSpec((1, 1, rows), lambda h: (h, 0, 0)),
            whole(rows, HEAD_DIM),
            whole(rows, HEAD_DIM),
            whole(1, rows),
            whole(1, rows),
            whole(blocks, rows, 1),
        ],
        out_specs=[
            per_head,
            pl.BlockSpec(
                (length, 2 * HEAD_DIM), lambda h: (0, h // repeat), pipeline_mode=pl.Buffered(1)
            ),
        ],
        out_shape=[
            jax.ShapeDtypeStruct((rows, width), BF16),
            jax.ShapeDtypeStruct((length, 2 * keys.shape[1]), BF16),
        ],
        scratch_shapes=[
            pltpu.VMEM((length, HEAD_DIM), F32),
            pltpu.VMEM((length, HEAD_DIM), F32),
            pltpu.VMEM((HEAD_DIM, rows), F32),
            pltpu.VMEM((blocks, rows, rows), F32),
            pltpu.VMEM((blocks, rows, rows), F32),
            pltpu.VMEM((1, rows), F32),
        ],
        compiler_params=pltpu.CompilerParams(vmem_limit_bytes=58 * MIB),
        cost_estimate=FREE,
    )(flags, q, keys, values, d_o, lse, cosine, sine, seg_q, pos_q, codes)


def rope_tables(places, width):
    half = width // 2
    freq = jnp.exp(jnp.arange(half, dtype=F32) * (-2.0 * LOG_BASE / width))
    angle = places.astype(F32)[:, None] * freq[None, :]
    return (jnp.cos(angle), jnp.sin(angle))


def rotate(values, cosine, sine):
    half = HEAD_DIM // 2
    parts = []
    for at in range(0, values.shape[1], HEAD_DIM):
        first = values[:, at : at + half]
        second = values[:, at + half : at + HEAD_DIM]
        parts += [first * cosine - second * sine, second * cosine + first * sine]
    return jnp.concatenate(parts, axis=1)


def inverse_rms(values):
    return lax.rsqrt(jnp.mean(values * values, axis=-1, keepdims=True) + EPS)


def norm_backward(upstream, normed, inverse, gain):
    scaled = upstream * gain
    inner = inverse * (scaled - normed * jnp.mean(scaled * normed, axis=-1, keepdims=True))
    return (inner, jnp.sum(upstream * normed, axis=0))


def rope_lanes(values, cosine, sine):
    parts = []
    for at in range(0, values.shape[1], HEAD_DIM):
        head = values[:, at : at + HEAD_DIM]
        parts.append(head * cosine + pltpu.roll(head, HEAD_DIM // 2, 1) * sine)
    return parts


def project_kernel(
    count, q_width, kv_width, place_ref, mine_ref, theirs_ref,
    x_ref, gain_ref, bias_ref, cos_ref, sin_ref, q_ref, kv_ref, h_ref, w_ref, sems,
):
    copies = [
        pltpu.make_async_copy(stack.at[i], w_ref.at[place_ref[at + i]], sems.at[at + i])
        for at, stack in ((0, mine_ref), (count, theirs_ref))
        for i in range(count)
    ]
    for copy in copies:
        copy.start()
    x = x_ref[...].astype(F32)
    normed = x * lax.rsqrt(jnp.mean(x * x, axis=1, keepdims=True) + EPS)
    h = (normed * gain_ref[...]).astype(BF16)
    h_ref[...] = h
    for copy in copies:
        copy.wait()
    depth, columns = x.shape[1], bias_ref.shape[1]
    weights = w_ref[...].reshape(depth, w_ref.shape[2])
    linear = product(h, weights[:, :columns]) + bias_ref[...]
    turned = rope_lanes(linear[:, : q_width + kv_width], cos_ref[...], sin_ref[...])
    heads = q_width // HEAD_DIM
    for i, part in enumerate(turned):
        if i < heads:
            q_ref[:, i * HEAD_DIM : (i + 1) * HEAD_DIM] = part.astype(BF16)
        else:
            at = (i - heads) * HEAD_DIM
            kv_ref[:, at : at + HEAD_DIM] = part.astype(BF16)
    kv_ref[:, kv_width:] = linear[:, q_width + kv_width :].astype(BF16)


def project(mine, theirs, places, inputs, gain, bias, cosine, sine, q_width, kv_width):
    count = mine.shape[0]
    rows, depth = inputs.shape
    columns = bias.shape[0]
    vmem = pl.BlockSpec(memory_space=pltpu.VMEM)
    return pl.pallas_call(
        functools.partial(project_kernel, count, q_width, kv_width),
        out_shape=[
            jax.ShapeDtypeStruct((rows, q_width), BF16),
            jax.ShapeDtypeStruct((rows, 2 * kv_width), BF16),
            jax.ShapeDtypeStruct((rows, depth), BF16),
            jax.ShapeDtypeStruct((2 * count,) + mine.shape[1:], BF16),
        ],
        in_specs=[pl.BlockSpec(memory_space=pltpu.SMEM)]
        + [pl.BlockSpec(memory_space=pl.ANY)] * 2
        + [vmem] * 5,
        out_specs=[vmem] * 4,
        scratch_shapes=[pltpu.SemaphoreType.DMA((2 * count,))],
        compiler_params=pltpu.CompilerParams(vmem_limit_bytes=40 * MIB),
        cost_estimate=FREE,
    )(places, mine, theirs, inputs, gain[None, :], bias[None, :], cosine, sine)


class Cut:
    def __init__(self, total, n_dp):
        tiles = total // n_dp // 128
        first = max(tiles * 3 // 8, 1)
        self.total = total
        self.n_dp = n_dp
        self.main = (first * 128, (tiles - first) * 128)
        self.start = (0, n_dp * self.main[0])
        self.rest_at = n_dp * (self.main[0] + self.main[1])
        self.rest = (total - self.rest_at) // n_dp
        pad = -(-self.rest // 128) * 128
        self.width = (self.main[0], self.main[1] + pad)


def pick(values, index):
    result = values[0]
    for i in range(1, len(values)):
        result = jnp.where(index == i, values[i], result)
    return result


def cut_kernel(cut, place_ref, *refs):
    n_dp = cut.n_dp
    sources, outs, (scratch, sems) = refs[:3], refs[3 : 3 + 2 * n_dp], refs[3 + 2 * n_dp :]
    copies = [
        pltpu.make_async_copy(source, scratch.at[i], sems.at[i])
        for i, source in enumerate(sources)
    ]
    for copy in copies:
        copy.start()
    for i, copy in enumerate(copies):
        copy.wait()
        for part in range(2):
            main, width = cut.main[part], cut.width[part]
            for k in range(n_dp):
                owner = place_ref[k]
                out = outs[part * n_dp + k]
                at = i * width
                low = pl.multiple_of(cut.start[part] + owner * main, 128)
                out[:, at : at + main] = scratch[i, :, pl.ds(low, main)]
                if part == 1 and cut.rest:
                    tail = scratch[i, :, cut.rest_at :]
                    rest = pick(
                        [tail[:, b * cut.rest : (b + 1) * cut.rest] for b in range(n_dp)], owner
                    )
                    fill = jnp.zeros((rest.shape[0], width - main - cut.rest), rest.dtype)
                    out[:, at + main : at + width] = jnp.concatenate([rest, fill], axis=1)


def cut_units(cut, weights, owners):
    rows = weights[0].shape[0]
    vmem = pl.BlockSpec(memory_space=pltpu.VMEM)
    outs = pl.pallas_call(
        functools.partial(cut_kernel, cut),
        out_shape=[
            jax.ShapeDtypeStruct((rows, 3 * cut.width[part]), BF16)
            for part in range(2)
            for _ in range(cut.n_dp)
        ],
        in_specs=[pl.BlockSpec(memory_space=pltpu.SMEM)]
        + [pl.BlockSpec(memory_space=pl.ANY)] * 3,
        out_specs=[vmem] * (2 * cut.n_dp),
        scratch_shapes=[
            pltpu.VMEM((3,) + weights[0].shape, BF16),
            pltpu.SemaphoreType.DMA((3,)),
        ],
        compiler_params=pltpu.CompilerParams(vmem_limit_bytes=24 * MIB),
        cost_estimate=FREE,
    )(owners, *weights)
    return outs[: cut.n_dp], outs[cut.n_dp :]


def lay_kernel(cut, place_ref, *refs):
    n_dp = cut.n_dp
    firsts, ups = refs[:n_dp], refs[n_dp : 2 * n_dp]
    outs = refs[2 * n_dp :]
    down_at = 3 * cut.width[0]
    lasts = ((firsts, down_at + cut.width[1]), (ups, 0), (firsts, down_at))
    for i, out in enumerate(outs):
        last, last_at = lasts[i]
        for part, (pieces, at) in enumerate(((firsts, i * cut.width[0]), lasts[i])):
            main = cut.main[part]
            for k in range(n_dp):
                low = pl.multiple_of(cut.start[part] + place_ref[k] * main, 128)
                out[:, pl.ds(low, main)] = pieces[k][:, at : at + main].astype(F32)
        if cut.rest:
            tails = [
                piece[:, last_at + cut.main[1] : last_at + cut.width[1]].astype(F32)[:, : cut.rest]
                for piece in last
            ]
            laid = []
            for b in range(n_dp):
                laid.append(
                    functools.reduce(
                        lambda got, k: jnp.where(place_ref[k] == b, tails[k], got),
                        range(1, n_dp),
                        tails[0],
                    )
                )
            out[:, cut.rest_at :] = jnp.concatenate(laid, axis=1)


def lay_units(cut, pieces, owners):
    rows = pieces[0].shape[0]
    vmem = pl.BlockSpec(memory_space=pltpu.VMEM)
    return pl.pallas_call(
        functools.partial(lay_kernel, cut),
        out_shape=[jax.ShapeDtypeStruct((rows, cut.total), F32)] * 3,
        in_specs=[pl.BlockSpec(memory_space=pltpu.SMEM)] + [vmem] * len(pieces),
        out_specs=[vmem] * 3,
        compiler_params=pltpu.CompilerParams(vmem_limit_bytes=32 * MIB),
        cost_estimate=FREE,
    )(owners, *pieces)


def feed_kernel(count, sums, *refs):
    t_ref, c_ref, w_ref = refs[:3]
    p_ref, back_ref, out_ref = refs[-3:]
    pair_weights = w_ref.at[:, : 2 * count]
    down_weight = w_ref.at[:, 2 * count :]
    pair = product(t_ref[...], pair_weights[...])
    gate, upper = pair[:, :count], pair[:, count:]
    act_back = product(c_ref[...], down_weight[...])
    sigma = 1.0 / (1.0 + jnp.exp(-gate))
    swish = gate * sigma
    activated = (swish * upper).astype(BF16)
    gate_back = (act_back * upper * sigma * (1.0 + gate * (1.0 - sigma))).astype(BF16)
    upper_back = (act_back * swish).astype(BF16)
    for i, value in enumerate((gate_back, upper_back, activated)):
        p_ref[:, i * count : (i + 1) * count] = value
    back = right_product(p_ref[:, : 2 * count], pair_weights[...])
    out = right_product(activated, down_weight[...])
    if sums:
        back = back + refs[3][...].astype(F32)
        out = out + refs[4][...].astype(F32)
    back_ref[...] = back.astype(back_ref.dtype)
    out_ref[...] = out.astype(out_ref.dtype)


def feed(tokens, cots, weights, side, kept, earlier):
    rows, width = tokens.shape
    columns = weights.shape[1]
    span = rows // 2
    tall = min(256, span)
    steps = span // tall
    block = lambda w: pl.BlockSpec((tall, w), lambda i: (side * steps + i, 0))
    near = pl.BlockSpec((tall, width), lambda i: (i, 0))
    operands = [tokens, cots, weights]
    in_specs = [
        block(width),
        block(width),
        pl.BlockSpec((width, columns), lambda i: (0, 0), pipeline_mode=pl.Buffered(1)),
    ]
    if earlier is not None:
        operands += list(earlier)
        in_specs += [near, near]
    aliases = {}
    if kept is not None:
        aliases = {len(operands): 0}
        operands.append(kept)
        in_specs.append(pl.BlockSpec(memory_space=pl.ANY))
    return pl.pallas_call(
        functools.partial(feed_kernel, columns // 3, earlier is not None),
        grid=(steps,),
        in_specs=in_specs,
        out_specs=[block(columns), near, near],
        out_shape=[
            jax.ShapeDtypeStruct((rows, columns), BF16),
            jax.ShapeDtypeStruct((span, width), BF16),
            jax.ShapeDtypeStruct((span, width), BF16),
        ],
        input_output_aliases=aliases,
        compiler_params=pltpu.CompilerParams(vmem_limit_bytes=56 * MIB),
        cost_estimate=FREE,
    )(*operands)


def one_grads_kernel(left_ref, p_ref, o_ref):
    o_ref[...] = left_product(left_ref[...], p_ref[...]).astype(BF16)


def grads_kernel(split, t_ref, c_ref, p_ref, o_ref):
    step = pl.program_id(0)

    @pl.when(step < split)
    def _():
        o_ref[...] = left_product(t_ref[...], p_ref[...]).astype(BF16)

    @pl.when(step >= split)
    def _():
        o_ref[...] = left_product(c_ref[...], p_ref[...]).astype(BF16)


def unit_gradients(tokens, cots, kept, which=(0, 1, 2), cost=FREE):
    rows, width = tokens.shape
    count = kept.shape[1] // 3
    wide = 384 if count % 384 == 0 else 128
    each = count // wide
    split = each * sum(i < 2 for i in which)
    first = which[0] * each
    held = pl.BlockSpec((rows, width), lambda i: (0, 0), pipeline_mode=pl.Buffered(1))
    kernel, lefts = functools.partial(grads_kernel, split), (tokens, cots)
    if len(which) == 1:
        kernel, lefts = one_grads_kernel, ((tokens, tokens, cots)[which[0]],)
    return pl.pallas_call(
        kernel,
        grid=(each * len(which),),
        in_specs=[held] * len(lefts) + [pl.BlockSpec((rows, wide), lambda i: (0, first + i))],
        out_specs=pl.BlockSpec((width, wide), lambda i: (0, i)),
        out_shape=jax.ShapeDtypeStruct((width, len(which) * count), BF16),
        compiler_params=pltpu.CompilerParams(vmem_limit_bytes=56 * MIB),
        cost_estimate=cost,
    )(*lefts, kept)


def d_o_kernel(own_ref, other_ref, w_ref, d_o_ref, rows_ref):
    half = own_ref.shape[0]
    weights = w_ref[...]
    d_o_ref[:half] = product(own_ref[...], weights).astype(BF16)
    d_o_ref[half:] = product(other_ref[...], weights).astype(BF16)
    rows_ref[:half] = own_ref[...]
    rows_ref[half:] = other_ref[...]


def d_o_of(own, other, weights, first, count):
    half, width = own.shape
    wide = math.gcd(first, count)
    whole = lambda *shape: pl.BlockSpec(shape, lambda i: (0, 0))
    return pl.pallas_call(
        d_o_kernel,
        grid=(count // wide,),
        in_specs=[
            whole(half, width),
            whole(half, width),
            pl.BlockSpec((width, wide), lambda i: (0, first // wide + i)),
        ],
        out_specs=[pl.BlockSpec((2 * half, wide), lambda i: (0, i)), whole(2 * half, width)],
        out_shape=[
            jax.ShapeDtypeStruct((2 * half, count), BF16),
            jax.ShapeDtypeStruct((2 * half, width), BF16),
        ],
        compiler_params=pltpu.CompilerParams(vmem_limit_bytes=32 * MIB),
        cost_estimate=FREE,
    )(own, other, weights)


def against_kernel(left_ref, right_ref, out_ref):
    out_ref[...] = right_product(left_ref[...], right_ref[...]).astype(out_ref.dtype)


def against(left, right, dtype):
    rows, depth = left.shape
    count = right.shape[0]
    wide = 512 if count % 512 == 0 else count
    return pl.pallas_call(
        against_kernel,
        grid=(count // wide,),
        in_specs=[
            pl.BlockSpec((rows, depth), lambda i: (0, 0)),
            pl.BlockSpec((wide, depth), lambda i: (i, 0)),
        ],
        out_specs=pl.BlockSpec((rows, wide), lambda i: (0, i)),
        out_shape=jax.ShapeDtypeStruct((rows, count), dtype),
        compiler_params=pltpu.CompilerParams(vmem_limit_bytes=32 * MIB),
        cost_estimate=FREE,
    )(left, right)


def halves_kernel(n_seq, share, core_ref, left_ref, right_ref, own_ref, sent_ref, keep_ref):
    keep_ref[...] = left_product(left_ref[...], right_ref[...]).astype(BF16)
    tall = own_ref.shape[1]
    for z in range(n_seq):
        for out, core in ((own_ref, core_ref[0]), (sent_ref, 1 - core_ref[0])):
            at = pl.multiple_of((z * 2 + core) * tall, share)
            out[z] = keep_ref[pl.ds(at, tall), :]


def gradient_halves(left, right, core, n_seq, share):
    width, columns = left.shape[1], right.shape[1]
    vmem = pl.BlockSpec(memory_space=pltpu.VMEM)
    half = jax.ShapeDtypeStruct((n_seq, width // (2 * n_seq), columns), BF16)
    return pl.pallas_call(
        functools.partial(halves_kernel, n_seq, share),
        out_shape=[half, half],
        in_specs=[pl.BlockSpec(memory_space=pltpu.SMEM), vmem, vmem],
        out_specs=[vmem, vmem],
        scratch_shapes=[pltpu.VMEM((width, columns), BF16)],
        compiler_params=pltpu.CompilerParams(vmem_limit_bytes=32 * MIB),
        cost_estimate=FREE,
    )(core, left, right)


def plane_gather(own, *others):
    cut = own.shape[0] // 2
    over_x, over_y, *others = together(dp_swap(own, 2), y_swap(own), *others)
    far_x = y_swap(over_x[:cut])
    far_y = dp_swap(over_y[cut:], 2)
    near = [own, over_y, over_x]
    across = [dp_swap(piece, 1) for piece in near]
    far_x, far_y, *across = together(far_x, far_y, *across)
    far = jnp.concatenate([far_x, far_y], axis=0)
    return near + [far] + across + [dp_swap(far, 1)], others


class PlaneScatter:
    def __init__(self, near, over_core):
        self.near, self.over_core = near, over_core
        self.t = near.shape[0] // 4
        self.cut = self.t // 2

    def summed(self, low, high):
        return self.near[low:high].astype(F32) + self.over_core[low:high].astype(F32)

    def corner(self):
        corner = self.summed(3 * self.t, 4 * self.t).astype(BF16)
        return corner[: self.cut], corner[self.cut :]

    def sides(self, corner_x, corner_y):
        t, cut = self.t, self.cut
        to_y = [self.summed(t, t + cut) + corner_x.astype(F32), self.summed(t + cut, 2 * t)]
        to_x = [
            self.summed(2 * t, 2 * t + cut),
            self.summed(2 * t + cut, 3 * t) + corner_y.astype(F32),
        ]
        return tuple(jnp.concatenate(part, axis=0).astype(BF16) for part in (to_x, to_y))

    def sides_of(self, corner_x):
        t = self.t
        to_y = self.summed(t, 2 * t) + corner_x.astype(F32)
        return self.summed(2 * t, 3 * t).astype(BF16), to_y.astype(BF16)

    def home(self, over_x, over_y):
        return self.summed(0, self.t) + over_x.astype(F32) + over_y.astype(F32)


def on_device(
    hidden, cotangent, segments, positions, first_gain,
    query_weight, query_bias, key_weight, key_bias, value_weight, value_bias,
    out_weight, second_gain, gate_weight, up_weight, down_weight,
):
    n_dp, n_seq = lax.axis_size("dp"), lax.axis_size("seq")
    dp, seq, tensor = (lax.axis_index(a) for a in ("dp", "seq", "tensor"))
    rows, width = hidden.shape
    half = rows // 2
    share = query_weight.shape[0]
    group = segments.shape[0]
    blocks = group // rows
    q_width, kv_width = query_weight.shape[1], key_weight.shape[1]
    kv_end = q_width + kv_width
    def slots_of(owners):
        return (owners % 2) * (n_dp // 2) + owners // 2

    dp_owners = dp ^ jnp.arange(n_dp, dtype=jnp.int32)
    dp_slots = slots_of(dp_owners)
    seq_places = (seq - jnp.arange(n_seq, dtype=jnp.int32) + n_seq) % n_seq
    flips = jnp.repeat(np.array([0, 2, 1, 3], np.int32), n_seq)
    all_places = jnp.tile(seq_places, 4) * n_dp + slots_of(dp ^ flips)
    core, x = (dp % 2).astype(jnp.int32), (dp // 2).astype(jnp.int32)
    tensor_place = tensor.astype(jnp.int32)[None]
    dp_owners, dp_slots, seq_places, all_places, core_place, tensor_place, core, x, *scalars = together(
        dp_owners, dp_slots, seq_places, all_places, core[None], tensor_place, core, x,
        *[seq_places[s] for s in range(n_seq)],
    )

    def take(values, index, axis):
        return lax.dynamic_index_in_dim(
            values, index, axis, keepdims=False, allow_negative_indices=False
        )


    def vector_in(vector):
        parts = vector.reshape(n_dp // 2, 2, n_seq, share)
        return parts.transpose(2, 1, 0, 3).reshape(width).astype(F32)

    def vector_out(vector):
        parts = vector.reshape(n_seq, 2, n_dp // 2, share)
        return parts.transpose(2, 1, 0, 3).reshape(width)

    index = jnp.arange(width, dtype=jnp.int32)
    owner, place = index // (share * n_seq), index // share % n_seq
    slot = owner % 2 * (n_dp // 2) + owner // 2
    inner_of = (place * n_dp + slot) * share + index % share
    shuffles = []

    def relative(values):
        turned = jnp.concatenate([values[half:], values[:half]], axis=0)
        return jnp.where(tensor == 0, values, turned)

    def to_inner(values):
        return product(relative(values), shuffles[0]).astype(BF16)

    def from_inner(values):
        return against(values, shuffles[0], BF16)

    gain_first, gain_second = vector_in(first_gain), vector_in(second_gain)

    cut = Cut(gate_weight.shape[1], n_dp)

    def spread(pieces):
        return [dp_swap(piece, k) if k else piece for k, piece in enumerate(pieces)]

    def stack_units(pieces):
        return assemble(pieces, dp_slots).reshape(n_dp * share, pieces[0].shape[1])

    own_place = relative(take(positions.reshape(blocks, rows), scalars[0], 0))
    own_segment = relative(take(segments.reshape(blocks, rows), scalars[0], 0))
    def tables(places):
        cosine, sine = rope_tables(places, HEAD_DIM)
        return (
            jnp.concatenate([cosine, cosine], axis=1), jnp.concatenate([-sine, sine], axis=1)
        )


    line = [jnp.concatenate([query_weight, key_weight, value_weight, out_weight.T], axis=1)]
    over_x = []
    for s in range(n_seq):
        over_x.append(dp_swap(line[s], 2))
        if s + 1 == n_seq:
            cot_own = to_inner(after(cotangent, line[s]))
            over_x[s], cot_own = together(over_x[s], cot_own)
            break
        moved = z_shift(line[s], 1)
        if s == 0:
            first_parts, second_parts = cut_units(
                cut, (gate_weight, up_weight, down_weight.T), dp_owners
            )
            moved, over_x[s], *parts = together(moved, over_x[s], *first_parts, *second_parts)
            first_parts, second_parts = parts[:n_dp], parts[n_dp:]
        elif s == 1:
            first_parts = spread(first_parts)
            inner = after(inner_of, line[s])
            shuffles.extend(together((inner[:, None] == index[None, :]).astype(BF16)))
            inputs = to_inner(after(hidden, line[s]))
            cosine, sine = tables(after(own_place, line[s]))
            moved, over_x[s], inputs, cosine, sine, *first_parts = together(
                moved, over_x[s], inputs, cosine, sine, *first_parts
            )
        elif s == 2:
            first_stacked = stack_units(first_parts)
            first_units = lax.all_gather(first_stacked, "seq", axis=0, tiled=True)
            moved, over_x[s], first_stacked = together(moved, over_x[s], first_stacked)
        else:
            moved, over_x[s] = together(moved, over_x[s])
        line.append(moved)
    mine = assemble(line + over_x, jnp.arange(2 * n_seq, dtype=jnp.int32))
    theirs = dp_swap(mine, 1)

    bias = jnp.concatenate([query_bias, key_bias, value_bias]).astype(F32)
    queries, own_kv, first_rounded, attention_weights = project(
        mine, theirs, all_places, inputs, gain_first, bias, cosine, sine, q_width, kv_width
    )
    qkv_end = q_width + 2 * kv_width
    attention_weights = attention_weights.reshape(width, qkv_end + q_width)
    qkv_full, out_full = attention_weights[:, :qkv_end], attention_weights[:, qkv_end:]
    group_kv = [own_kv] + [z_shift(own_kv, s) for s in range(1, n_seq)]
    second_parts = spread([after(part, own_kv) for part in second_parts])
    def key_rows(vector):
        taken = jnp.take(vector.reshape(blocks, rows), seq_places, axis=0)
        return relative(taken.T).T

    seg_k, pos_k = (key_rows(after(v, own_kv)) for v in (segments, positions))
    seen = pair_mask(
        own_segment[None, :, None], own_place[None, :, None], seg_k[:, None, :], pos_k[:, None, :]
    )
    flags = (jnp.any(seen, axis=(1, 2)).astype(jnp.int32) + jnp.all(seen, axis=(1, 2))).astype(
        jnp.int32
    )
    codes = (seg_k * SEGMENT_STEP + pos_k)[:, :, None]
    pairs = (own_segment[None, :], own_place[None, :], codes, flags)
    *group_kv, cot_own, second_parts, pairs = together(*group_kv, cot_own, second_parts, pairs)
    second_stacked = stack_units(second_parts)
    second_units = lax.all_gather(second_stacked, "seq", axis=0, tiled=True)
    cot_x = dp_swap(cot_own, 2)
    group_kv = jnp.concatenate(group_kv, axis=0)
    keys, values = group_kv[:, :kv_width], group_kv[:, kv_width:]

    attended, lse = attend(queries, keys, values, *pairs)
    def reduce_halves(part):
        return part[:half] + y_swap(part[half:].astype(BF16)).astype(F32)

    inputs_half = inputs[:half].astype(F32)
    out_theirs = y_swap(right_product(attended[half:], out_full).astype(BF16))
    out_mine = right_product(attended[:half], out_full)
    out_theirs, out_mine, cot_x = together(out_theirs, out_mine, cot_x)
    cot_pieces = [cot_own, cot_x, dp_swap(cot_own, 1), dp_swap(cot_x, 1)]
    cots = assemble(cot_pieces, jnp.arange(4, dtype=jnp.int32)).reshape(-1, width)
    residual = inputs_half + out_mine + out_theirs.astype(F32)
    second_inverse = inverse_rms(residual)
    second_normed = residual * second_inverse
    second_rounded = (second_normed * gain_second).astype(BF16)

    gathered, (cots,) = plane_gather(second_rounded, cots)
    tokens = assemble(gathered, jnp.arange(len(gathered), dtype=jnp.int32)).reshape(-1, width)

    kept, *far = feed(tokens, cots, first_units, 1, None, None)
    kept, *near = feed(tokens, cots, first_units, 0, kept, None)
    first_gradient = unit_gradients(tokens, cots, kept)
    second_weights = after(second_units, first_gradient)
    second_kept, back_far, out_far = feed(tokens, cots, second_weights, 1, None, far)
    second_kept, back_near, out_near = feed(
        tokens, cots, second_weights, 0, second_kept, near
    )
    first_share = lax.psum_scatter(first_gradient, "seq", scatter_dimension=0, tiled=True)
    flops = 2 * tokens.size * cut.width[1]
    cost = pl.CostEstimate(flops=flops, bytes_accessed=0, transcendentals=0)

    def second_gradient(which, operand):
        return unit_gradients(tokens, cots, after(second_kept, operand), (which,), cost)

    def sum_along_seq(gradient):
        return lax.psum_scatter(gradient, "seq", scatter_dimension=0, tiled=True)

    back = PlaneScatter(*reversed(together(dp_swap(back_far, 1), back_near)))
    corner = back.corner()
    *corners, down_gradient = together(
        dp_swap(corner[0], 2), y_swap(corner[1]), second_gradient(2, corner[0])
    )
    down_share = sum_along_seq(down_gradient)
    sides = back.sides(*corners)
    *over, gate_gradient, first_share = together(
        dp_swap(sides[0], 2), y_swap(sides[1]), second_gradient(0, sides[0]), first_share
    )
    gate_share = sum_along_seq(gate_gradient)
    second_back = back.home(*over)

    residual_inner, second_gain_term = norm_backward(
        second_back, second_normed, second_inverse, gain_second
    )
    residual_back = cot_own[:half].astype(F32) + residual_inner
    back_half = residual_back.astype(BF16)
    def exchange_units(*shares):
        stacks = [mine.reshape(n_dp, share, mine.shape[1]) for mine in shares]
        pieces = pick_pieces(stacks, dp_slots)
        return [dp_swap(piece, k) if k else piece for k, piece in enumerate(pieces)]

    out_core = dp_swap(after(out_far, back_half), 1)
    corner = PlaneScatter(out_near, out_core).summed(3 * half, 4 * half).astype(BF16)
    back_other, out_core, up_gradient, down_share, corner_x = together(
        y_swap(back_half), out_core, second_gradient(1, back_half), down_share, dp_swap(corner, 2)
    )
    down = PlaneScatter(out_near, out_core)
    attended_back, attention_back = d_o_of(
        back_half, back_other, attention_weights, qkv_end, q_width
    )

    def halves_of(left, right):
        return gradient_halves(left, right, core_place, n_seq, share)

    def x_halves(own, over_core):
        parts = own.astype(F32) + over_core.astype(F32)
        parts = parts.reshape(n_seq, n_dp // 2, share, own.shape[2])
        return take(parts, x, 1), take(parts, 1 - x, 1).astype(BF16)

    def place_of(parts, s):
        return take(parts, scalars[s % n_seq], 0)

    out_own, sent = halves_of(attention_back, attended)
    sides = down.sides_of(corner_x)
    over = dp_swap(sides[0], 2), y_swap(sides[1])
    (out_over_core,) = together(dp_swap(sent, 1))
    out_own, sent = x_halves(out_own, out_over_core)
    out_over_x = dp_swap(sent, 2)
    attended_back, out_sent = together(attended_back, sent)
    query_linear_back, kv_parts = attend_back(
        queries, keys, values, attended_back, lse, cosine, sine, *pairs
    )
    query_linear_back, kv_parts, out_over_x, *over = together(
        query_linear_back, kv_parts, out_over_x, *over
    )

    kv_moved = [z_shift(kv_parts[s * rows : (s + 1) * rows], -s) for s in range(1, n_seq)]
    query_own, query_sent = halves_of(first_rounded, query_linear_back)
    query_own, gate_share, query_over_core, *kv_moved = together(
        query_own, gate_share, dp_swap(query_sent, 1), *kv_moved
    )
    *kv_moved, up_gradient = together(*kv_moved, up_gradient)
    out_rows = out_own + out_over_x.astype(F32)
    up_share = sum_along_seq(up_gradient)
    kv_back = kv_parts[:rows].astype(F32)
    for moved in kv_moved:
        kv_back = kv_back + moved.astype(F32)
    key_linear_back = rotate(
        kv_back[:, :kv_width], cosine[:, : HEAD_DIM // 2], -sine[:, HEAD_DIM // 2 :]
    )
    kv_linear_back = jnp.concatenate([key_linear_back, kv_back[:, kv_width:]], axis=1).astype(BF16)
    linear_back = jnp.concatenate([query_linear_back, kv_linear_back], axis=1)

    query_own, sent = x_halves(query_own, query_over_core)
    query_over_x = dp_swap(sent, 2)
    kv_own, sent = halves_of(first_rounded, kv_linear_back)
    kv_over_core = dp_swap(sent, 1)
    first_theirs = y_swap(against(linear_back[half:], attention_weights, BF16))
    first_mine = against(linear_back[:half], attention_weights, F32)
    query_over_x, kv_over_core = together(query_over_x, kv_over_core)
    large = jnp.concatenate([query_own + query_over_x.astype(F32), out_rows], axis=2)

    kv_own, sent = x_halves(kv_own, kv_over_core)
    kv_over_x = dp_swap(sent, 2)
    total = z_shift(place_of(large, 1).astype(BF16), 1)
    out_half = from_inner((residual + down.home(*over)).astype(BF16))
    total, kv_over_x, first_theirs, first_mine, out_half = together(
        total, kv_over_x, first_theirs, first_mine, out_half
    )
    kv_rows = kv_own + kv_over_x.astype(F32)
    total = place_of(large, 2) + total.astype(F32)

    out_other = y_swap(out_half)
    first_back = first_mine + first_theirs.astype(F32)
    first_inverse = inverse_rms(inputs_half)
    input_inner, first_gain_term = norm_backward(
        first_back, inputs_half * first_inverse, first_inverse, gain_first
    )
    input_half = (residual_back + input_inner).astype(BF16)
    bias_terms = jnp.sum(linear_back.astype(F32), axis=0)
    sums = jnp.concatenate([first_gain_term, second_gain_term, bias_terms])

    def shift_add(values, axis):
        size = lax.axis_size(axis)
        moved = [
            lax.ppermute(values, axis, [(i, (i + s) % size) for i in range(size)])
            for s in range(1, size)
        ]
        return functools.reduce(jnp.add, moved, values)

    input_half = from_inner(input_half)
    input_other = y_swap(input_half)
    pieces = exchange_units(first_share, down_share, gate_share)
    kv_moved = [z_shift(place_of(kv_rows, s).astype(BF16), -s) for s in range(1, n_seq)]
    sums = shift_add(sums, "dp")
    for s in range(2, n_seq):
        total = z_shift(total.astype(BF16), 1)
        if s == 2:
            total, sums, out_other, up_share, *kv_moved = together(
                total, sums, out_other, up_share, *kv_moved
            )
            up_pieces = exchange_units(up_share)
            sums = shift_add(sums, "seq")
        elif s == 3:
            total, sums, input_other, *arrived = together(
                total, sums, input_other, *pieces, *up_pieces
            )
            pieces, up_pieces = arrived[:n_dp], arrived[n_dp:]
        total = place_of(large, s + 1) + total.astype(F32)
    kv_share = functools.reduce(
        lambda a, b: a + b.astype(F32), kv_moved, place_of(kv_rows, 0)
    )
    gain_terms = shift_add(sums[: 2 * width], "tensor")
    bias_terms = sums[2 * width :]
    input_gradient = join_halves(input_half, input_other, tensor_place)
    output = join_halves(out_half, out_other, tensor_place)
    large_share = total
    out_gradient = large_share[:, q_width:].T
    gate_gradient, up_gradient, down_gradient = lay_units(
        cut, pieces + up_pieces, dp_owners
    )
    down_gradient = down_gradient.T
    return (
        output,
        input_gradient,
        vector_out(gain_terms[:width]),
        large_share[:, :q_width],
        bias_terms[:q_width],
        kv_share[:, :kv_width],
        bias_terms[q_width:kv_end],
        kv_share[:, kv_width:],
        bias_terms[kv_end:],
        out_gradient,
        vector_out(gain_terms[width:]),
        gate_gradient,
        up_gradient,
        down_gradient,
    )


def solution(mesh):
    tokens = P(("dp", "seq"), None)
    by_row = P(("dp", "seq"), "tensor")
    by_column = P("tensor", ("dp", "seq"))
    heads = P("tensor")
    in_specs = (
        tokens, tokens, P("dp"), P("dp"), P(), by_row, heads, by_row, heads, by_row, heads,
        by_column, P(), by_row, by_row, by_column,
    )
    out_specs = (
        tokens, tokens, P(), by_row, heads, by_row, heads, by_row, heads, by_column, P(),
        by_row, by_row, by_column,
    )
    return jax.shard_map(
        on_device, mesh=mesh, in_specs=in_specs, out_specs=out_specs, check_vma=False
    )
```
